32 devices in a mesh: section: 2 (over core), dp: 2 (over y), ctx: 2 (over x), tp: 4 (over z).
Axes of the slice: x: 2, y: 2, z: 4, core: 2. Of those that a mesh axis runs over, the one named last changes fastest.
Arguments:
- acts: bfloat16 [4, 2, 2048, 1024], P(None, 'dp', 'ctx'), may hold values from -6 to 6
- cotangent: float32 [4, 2, 2048, 1024], P(None, 'dp', 'ctx'), may hold values from -6 to 6
- lengths: int32 [4, 2], P(None, 'dp'), may hold values from 1024 to 2048, as said below
- norm_gain: bfloat16 [2, 1024], P('section', ('dp', 'ctx')), may hold values from 0.099609375 to 1.8984375
- proj_gate_x: bfloat16 [2, 1024, 2, 2048], P('section', ('dp', 'ctx'), None, 'tp'), may hold values from -0.1875 to 0.1875
- proj_state: bfloat16 [2, 1024, 256], P('section', ('dp', 'ctx')), may hold values from -0.1875 to 0.1875
- proj_step: bfloat16 [2, 1024, 32], P('section', ('dp', 'ctx'), 'tp'), may hold values from -0.1875 to 0.1875
- conv_inner: float32 [2, 5, 2048], P('section', None, 'tp'), may hold values from -3 to 3
- conv_state: float32 [2, 5, 256], P('section'), may hold values from -3 to 3
- step_bias: float32 [2, 32], P('section', 'tp'), may hold values from -10 to -2
- decay_log: float32 [2, 32], P('section', 'tp'), may hold values from -1 to 2
- skip_weight: float32 [2, 32], P('section', 'tp'), may hold values from 0.5 to 1.5
- out_gain: float32 [2, 2048], P('section', 'tp'), may hold values from 0.1 to 1.9
- proj_out: bfloat16 [2, 2048, 1024], P('section', 'tp', ('dp', 'ctx')), may hold values from -0.125 to 0.125
Outputs:
- section_out: bfloat16 [2, 4, 2, 2048, 1024], P('section', None, 'dp', ('ctx', 'tp'))
- input_grad: float32 [2, 4, 2, 2048, 1024], P('section', None, 'dp', ('ctx', 'tp'))
- grad_norm_gain: float32 [2, 1024], P('section', ('dp', 'ctx'))
- grad_gate_x: float32 [2, 1024, 2, 2048], P('section', ('dp', 'ctx'), None, 'tp')
- grad_state: float32 [2, 1024, 256], P('section', ('dp', 'ctx'))
- grad_step: float32 [2, 1024, 32], P('section', ('dp', 'ctx'), 'tp')
- grad_conv_inner: float32 [2, 5, 2048], P('section', None, 'tp')
- grad_conv_state: float32 [2, 5, 256], P('section')
- grad_step_bias: float32 [2, 32], P('section', 'tp')
- grad_decay_log: float32 [2, 32], P('section', 'tp')
- grad_skip: float32 [2, 32], P('section', 'tp')
- grad_out_gain: float32 [2, 2048], P('section', 'tp')
- grad_out: float32 [2, 2048, 1024], P('section', 'tp', ('dp', 'ctx'))
The draws below stay inside these ranges and needn't reach their ends.
Inputs may be any that keep to these rules, and one draw needn't show every extreme that they name: `lengths`: every data rank has, in one of its 4 micro-batches drawn from the seed, a sequence that fills all 2048 positions of its row.
All inputs are finite; a program needn't handle non-finite values.
Results may differ from the reference program's by a relative error of at most 0.024.
Values may be sent and summed in bfloat16 or wider, within the bound.
No kernel may reach another device: no remote copies, remote signals or barrier semaphores. Data moves between devices by JAX's collectives and lax.ppermute only.
A program may use at most 384 MiB of HBM per device.

```python
import jax
import jax.numpy as jnp
from jax import lax

D = 1024
HEADS = 32
HEADDIM = 64
STATE = 128
INNER = 2048
CONV = 4
BLOCK = 256
MICRO = 4
ROW = 2048
MB_ROWS = 2


def draw_lengths(key, part):
    key = jax.random.fold_in(key, 11)
    key_draw, key_pick = jax.random.split(key)
    drawn_lengths = jax.random.randint(key_draw, (MICRO, MB_ROWS), ROW // 2, ROW + 1, dtype=jnp.int32)
    chosen = jax.random.randint(key_pick, (1, MB_ROWS), 0, MICRO, dtype=jnp.int32)
    row_index = jnp.arange(MICRO, dtype=jnp.int32)[:, None]
    return jnp.where(row_index == chosen, ROW, drawn_lengths).astype(jnp.int32)


def block_scale(stream_key, extent, cuts, smallest, top_value):
    loudness = 1.0
    for position, parts in cuts:
        steps = jax.random.uniform(jax.random.fold_in(jax.random.fold_in(stream_key, 6), position), (parts,), jnp.float32, smallest / len(cuts), top_value / len(cuts))
        loudness = loudness * jnp.repeat(jnp.exp(steps), extent[position] // parts).reshape((-1,) + (1,) * (len(extent) - 1 - position))
    return loudness


def scatter_about(rng, shape, spread, limit, cuts=(), kind=jnp.bfloat16):
    values = jax.random.normal(rng, shape, jnp.float32) * spread
    if len(cuts) > 0:
        values = block_scale(rng, shape, cuts, -0.22, 0.18) * values
    return jnp.clip(values, min=-limit, max=limit).astype(kind)


def setup_inputs(seed: int = 0) -> dict:
    seeds = jax.random.split(jax.random.key(seed), 15)
    return {
        "acts": scatter_about(seeds[0], (MICRO, MB_ROWS, ROW, D), 1.0, 6.0, ((1, 2), (2, 2))),
        "cotangent": scatter_about(seeds[1], (MICRO, MB_ROWS, ROW, D), 1.0, 6.0, ((1, 2), (2, 2)), jnp.float32),
        "lengths": draw_lengths(jax.random.fold_in(seeds[14], 71), 0),
        "norm_gain": jnp.clip(1.0 + 0.18 * jax.random.normal(seeds[3], (2, D), jnp.float32), 0.099609375, 1.8984375).astype(jnp.bfloat16),
        "proj_gate_x": scatter_about(seeds[4], (2, D, 2, INNER), D ** -0.5, 0.1875, ((0, 2), (1, 4), (3, 4))),
        "proj_state": scatter_about(seeds[5], (2, D, 2 * STATE), D ** -0.5, 0.1875, ((0, 2), (1, 4))),
        "proj_step": scatter_about(seeds[6], (2, D, HEADS), D ** -0.5, 0.1875, ((0, 2), (1, 4), (2, 4))),
        "conv_inner": scatter_about(seeds[7], (2, CONV + 1, INNER), CONV ** -0.5, 3.0, ((0, 2), (2, 4)), jnp.float32),
        "conv_state": scatter_about(seeds[8], (2, CONV + 1, 2 * STATE), CONV ** -0.5, 3.0, ((0, 2),), jnp.float32),
        "step_bias": jnp.clip(-10.0 + 8.0 * jax.random.uniform(seeds[9], (2, HEADS), jnp.float32) ** block_scale(seeds[9], (2, HEADS), ((0, 2), (1, 4)), -0.2, 0.2), -10.0, -2.0),
        "decay_log": jnp.clip(-1.0 + 3.0 * jax.random.uniform(seeds[10], (2, HEADS), jnp.float32) ** block_scale(seeds[10], (2, HEADS), ((0, 2), (1, 4)), -0.2, 0.2), -1.0, 2.0),
        "skip_weight": jnp.clip(0.5 + 1.0 * jax.random.uniform(seeds[11], (2, HEADS), jnp.float32) ** block_scale(seeds[11], (2, HEADS), ((0, 2), (1, 4)), -0.2, 0.2), 0.5, 1.5),
        "out_gain": jnp.clip(1.0 + 0.18 * jax.random.normal(seeds[12], (2, INNER), jnp.float32), 0.1, 1.9),
        "proj_out": scatter_about(seeds[13], (2, INNER, D), INNER ** -0.5, 0.125, ((0, 2), (1, 4), (2, 4))),
    }


@jax.custom_vjp
def low(v):
    return lax.optimization_barrier(v.astype(jnp.bfloat16)).astype(jnp.float32)

@jax.custom_vjp
def low_back(v):
    return v

def low_keep(v):
    return (low(v), None)

def low_pass(kept, grad):
    return (grad,)

def back_keep(v):
    return (v, None)

def back_low(kept, grad):
    return (low(grad),)
low.defvjp(low_keep, low_pass)
low_back.defvjp(back_keep, back_low)
highest = lax.Precision.HIGHEST
epsilon = 1e-05

def root_scale(values, gain_row):
    return values * lax.rsqrt(lax.optimization_barrier(jnp.mean(values * values, axis=-1, keepdims=True)) + epsilon) * gain_row

def block_step(running, blocks):
    inner_x, b_rows, c_rows, step_size, log_decay = blocks
    cumulative = jnp.cumsum(log_decay, axis=1)
    length_q = cumulative.shape[1]
    causal = jnp.arange(length_q)[:, None] >= jnp.arange(length_q)[None, :]
    by_head = jnp.swapaxes(cumulative, 1, 2)
    gap_logs = by_head[:, :, :, None] - by_head[:, :, None, :]
    decays = jnp.where(causal, jnp.exp(jnp.where(causal, gap_logs, 0.0)), 0.0)
    affinity = jnp.einsum('btn,bsn->bts', c_rows, b_rows, precision=highest)
    mixing = affinity[:, None] * decays * jnp.swapaxes(step_size, 1, 2)[:, :, None, :]
    inside = jnp.einsum('bhts,bshp->bthp', mixing, inner_x, precision=highest)
    carried = jnp.exp(cumulative)[..., None] * jnp.einsum('btn,bhpn->bthp', c_rows, running, precision=highest)
    block_end = cumulative[:, -1]
    weights = jnp.exp(block_end[:, None, :] - cumulative) * step_size
    fresh_state = jnp.einsum('bsh,bshp,bsn->bhpn', weights, inner_x, b_rows, precision=highest)
    running = jnp.exp(block_end)[:, :, None, None] * running + fresh_state
    return (running, inside + carried)

def mixer_layer(hidden_in, valid_rows, norm_gain, proj_gate_x, proj_state, proj_step, conv_inner, conv_state, step_bias, decay_log, skip_weight, out_gain, proj_out):
    seq_count, seq_rows = (hidden_in.shape[0], hidden_in.shape[1])
    normed = low(root_scale(hidden_in, norm_gain))
    gate_pre = low_back(jnp.einsum('btd,dk->btk', normed, proj_gate_x[:, 0], precision=highest))
    feed_x = jnp.einsum('btd,dk->btk', normed, proj_gate_x[:, 1], precision=highest)
    feed_state = jnp.einsum('btd,dk->btk', normed, proj_state, precision=highest)
    feed_in = low_back(low(jnp.concatenate([feed_x, feed_state], axis=-1)))
    raw_step = low_back(jnp.einsum('btd,dk->btk', normed, proj_step, precision=highest))
    conv_taps = jnp.concatenate([conv_inner, conv_state], axis=-1)
    padded = jnp.pad(feed_in, ((0, 0), (CONV - 1, 0), (0, 0)))
    conv_total = conv_taps[CONV] + sum((conv_taps[offset] * padded[:, offset:offset + seq_rows] for offset in range(CONV)))
    activated = jax.nn.silu(conv_total)
    inner_x = activated[..., :INNER].reshape(seq_count, seq_rows, HEADS, HEADDIM)
    b_rows = activated[..., INNER:INNER + STATE]
    c_rows = activated[..., INNER + STATE:]
    step_size = jax.nn.softplus(raw_step + step_bias)
    log_decay = -jnp.exp(decay_log) * step_size
    blocks = tuple((jnp.moveaxis(member.reshape((seq_count, seq_rows // BLOCK, BLOCK) + member.shape[2:]), 1, 0) for member in (inner_x, b_rows, c_rows, step_size, log_decay)))
    starting = jnp.zeros((seq_count, HEADS, HEADDIM, STATE), jnp.float32)
    final_state, outputs = lax.scan(jax.checkpoint(block_step), starting, blocks)
    ssm_out = jnp.moveaxis(outputs, 0, 1).reshape(seq_count, seq_rows, HEADS, HEADDIM) + skip_weight[:, None] * inner_x
    gated_out = ssm_out.reshape(seq_count, seq_rows, INNER) * jax.nn.silu(gate_pre)
    normed_out = low(root_scale(gated_out, out_gain))
    branch = low_back(jnp.einsum('btk,kd->btd', normed_out, proj_out, precision=highest))
    return hidden_in + valid_rows[..., None] * branch

def reference(acts, cotangent, lengths, norm_gain, proj_gate_x, proj_state, proj_step, conv_inner, conv_state, step_bias, decay_log, skip_weight, out_gain, proj_out):
    params = tuple((member.astype(jnp.float32) for member in (norm_gain, proj_gate_x, proj_state, proj_step, conv_inner, conv_state, step_bias, decay_log, skip_weight, out_gain, proj_out)))
    seq_total = MICRO * MB_ROWS
    inputs = acts.astype(jnp.float32).reshape(seq_total, ROW, D)
    places = jnp.arange(ROW, dtype=jnp.int32)
    valid_rows = (places[None, :] < lengths.reshape(seq_total, 1).astype(jnp.int32)).astype(jnp.float32)

    def whole_model(first_in, probe_in, *weights):
        first_out = mixer_layer(first_in, valid_rows, *[member[0] for member in weights])
        middle = low_back(low(first_out))
        last_out = mixer_layer(middle + probe_in, valid_rows, *[member[1] for member in weights])
        return (last_out, first_out)
    last_out, pullback, first_out = jax.vjp(whole_model, inputs, jnp.zeros_like(inputs), *params, has_aux=True)
    gradients = pullback(cotangent.reshape(seq_total, ROW, D))
    shape_out = (2, MICRO, MB_ROWS, ROW, D)
    section_out = jnp.stack([first_out, last_out]).astype(jnp.bfloat16).reshape(shape_out)
    input_grad = jnp.stack([gradients[0], gradients[1]]).reshape(shape_out)
    return (section_out, input_grad, gradients[2], gradients[3], gradients[4], gradients[5], gradients[6], gradients[7], gradients[8], gradients[9], gradients[10], gradients[11], gradients[12])
```

```python
import functools

import jax
import jax.numpy as jnp
from jax import lax
from jax.experimental import pallas as pl
from jax.experimental.pallas import tpu as pltpu
from jax.sharding import PartitionSpec as P

HEADDIM = 64
STATE = 128
INNER = 2048
CONV = 4
CHUNK = 128
LANES = 128

highest = lax.Precision.HIGHEST
epsilon = 1e-05
low = jnp.bfloat16
full = jnp.float32


def dot_nn(a, b, precision=None):
    return lax.dot_general(
        a, b, (((1,), (0,)), ((), ())), precision=precision, preferred_element_type=full
    )


def dot_nt(a, b, precision=None):
    return lax.dot_general(
        a, b, (((1,), (1,)), ((), ())), precision=precision, preferred_element_type=full
    )


def dot_tn(a, b, precision=None):
    return lax.dot_general(
        a, b, (((0,), (0,)), ((), ())), precision=precision, preferred_element_type=full
    )


def shifted(value, axis, steps):
    count = lax.axis_size(axis)
    first, last = (max(0, -steps), min(count, count - steps))
    return lax.ppermute(value, axis, [(source, source + steps) for source in range(first, last)])


def rotated(value, axis, steps):
    count = lax.axis_size(axis)
    return lax.ppermute(value, axis, [(i, (i + steps) % count) for i in range(count)])


def line_gather(value, axis):
    count = lax.axis_size(axis)
    place = lax.axis_index(axis)
    if count == 1:
        return value[None]
    if count == 2:
        other = rotated(value, axis, 1)
        first = place == 0
        return jnp.stack([jnp.where(first, value, other), jnp.where(first, other, value)])
    up = down = value
    before, after = [], []
    for _ in range(1, count):
        up = shifted(up, axis, 1)
        down = shifted(down, axis, -1)
        before.insert(0, up)
        after.append(down)
    line = jnp.stack(before + [value] + after)
    return lax.dynamic_slice_in_dim(line, count - 1 - place, count, 0)


def scatter_sum(value, axis):
    count = lax.axis_size(axis)
    place = lax.axis_index(axis)
    total = lax.dynamic_index_in_dim(value, place, 0, False).astype(full)
    for steps in range(1, count):
        block = lax.dynamic_index_in_dim(value, (place + steps) % count, 0, False)
        total = total + rotated(block, axis, steps).astype(full)
    return total


def all_sum(value, axis):
    total = value
    for steps in range(1, lax.axis_size(axis)):
        total = total + rotated(value, axis, steps)
    return total


def swap_cores(value):
    return lax.ppermute(value, "section", [(0, 1), (1, 0)])


def spread_rows(value, pairs_of):
    count = lax.axis_size("tp")
    place = lax.axis_index("tp")
    result = jnp.zeros_like(value)
    own = lax.dynamic_index_in_dim(value, place, 0, False)
    result = lax.dynamic_update_index_in_dim(result, own, place, 0)
    for steps in range(1, count):
        block = lax.dynamic_index_in_dim(value, (place + steps) % count, 0, False)
        pairs = [
            (core * count + i, core * count + (i + steps) % count)
            for core in pairs_of
            for i in range(count)
        ]
        arrived = lax.ppermute(block, ("section", "tp"), pairs)
        result = lax.dynamic_update_index_in_dim(result, arrived, (place - steps) % count, 0)
    return result


def gather_along_tp(packs):
    return [line_gather(pack, "tp") for pack in packs]


def gather_rows(early, late):
    width = early.shape[-1]
    half_a = line_gather(line_gather(early, "ctx"), "dp").reshape(-1, width)
    half_b = jnp.swapaxes(line_gather(line_gather(late, "dp"), "ctx"), 0, 1).reshape(-1, width)
    return half_a, half_b


def columns(pieces):
    return jnp.concatenate(list(pieces), axis=-1)


def reduce_rows(half_a, half_b):
    ndp, nctx = lax.axis_size("dp"), lax.axis_size("ctx")
    rows = half_a.shape[0] // (ndp * nctx)
    blocks_a = jnp.swapaxes(half_a.reshape(ndp, nctx, rows, -1), 0, 1)
    blocks_b = half_b.reshape(ndp, nctx, rows, -1)
    sum_a = scatter_sum(blocks_a, "ctx").astype(low)
    sum_b = scatter_sum(blocks_b, "dp").astype(low)
    return scatter_sum(sum_a, "dp").astype(low), scatter_sum(sum_b, "ctx").astype(low)


def fwd_kernel(x_ref, bc_ref, dt_ref, cum_ref, cumt_ref, skip_ref, enter_ref, y_ref, start_ref, state):
    @pl.when(pl.program_id(0) == 0)
    def _():
        state[...] = enter_ref[...].astype(full)

    heads = cumt_ref.shape[0]
    start_ref[0] = state[...].astype(low)
    b_low = bc_ref[:, :STATE].astype(low)
    c_low = bc_ref[:, STATE:].astype(low)
    row = lax.broadcasted_iota(jnp.int32, (CHUNK, CHUNK), 0)
    col = lax.broadcasted_iota(jnp.int32, (CHUNK, CHUNK), 1)
    left = col < HEADDIM
    upper = row < HEADDIM
    masked = jnp.where(row >= col, dot_nt(c_low, b_low), 0.0)
    for pair in range(heads // 2):
        h0, h1 = 2 * pair, 2 * pair + 1
        span = slice(pair * LANES, (pair + 1) * LANES)
        cum0 = jnp.broadcast_to(cum_ref[:, h0 : h0 + 1], (CHUNK, CHUNK))
        cum1 = jnp.broadcast_to(cum_ref[:, h1 : h1 + 1], (CHUNK, CHUNK))
        w0 = jnp.exp(jnp.minimum(cum0 - cumt_ref[h0 : h0 + 1, :], 0.0)) * masked
        w1 = jnp.exp(jnp.minimum(cum1 - cumt_ref[h1 : h1 + 1, :], 0.0)) * masked
        weights = jnp.concatenate([w0.astype(low), w1.astype(low)], axis=1)
        x_pair = x_ref[:, span]
        u = x_pair * jnp.where(left, dt_ref[:, h0 : h0 + 1], dt_ref[:, h1 : h1 + 1])
        u_low = u.astype(low)
        zero = jnp.zeros_like(u_low)
        u_both = jnp.concatenate([jnp.where(left, u_low, zero), jnp.where(left, zero, u_low)], axis=0)
        cum_pair = jnp.where(left, cum0, cum1)
        s_pair = state[span, :]
        carried = jnp.exp(cum_pair) * dot_nt(c_low, s_pair.astype(low))
        y_ref[:, span] = dot_nn(weights, u_both) + carried + skip_ref[:, span] * x_pair
        end0 = cum_ref[CHUNK - 1 : CHUNK, h0 : h0 + 1]
        end1 = cum_ref[CHUNK - 1 : CHUNK, h1 : h1 + 1]
        ahead = jnp.exp(jnp.where(left, end0, end1) - cum_pair)
        fresh = dot_tn((u * ahead).astype(low), b_low)
        state[span, :] = jnp.exp(jnp.where(upper, end0, end1)) * s_pair + fresh


def bwd_kernel(
    x_ref, bc_ref, dt_ref, cum_ref, cumt_ref, skip_ref, dy_ref, start_ref, later_ref,
    dx_ref, dbc_ref, ddt_ref, dlog_ref,
    adjoint, dye, uw, xdu, dyi, udu,
):
    @pl.when(pl.program_id(0) == 0)
    def _():
        adjoint[...] = later_ref[...].astype(full)

    heads = cumt_ref.shape[0]
    inner = heads * HEADDIM
    b_low = bc_ref[:, :STATE].astype(low)
    c_low = bc_ref[:, STATE:].astype(low)
    row = lax.broadcasted_iota(jnp.int32, (CHUNK, CHUNK), 0)
    col = lax.broadcasted_iota(jnp.int32, (CHUNK, CHUNK), 1)
    left = col < HEADDIM
    causal = row >= col
    onward = (row <= col).astype(low)
    masked = jnp.where(causal, dot_nt(c_low, b_low), 0.0)
    d_affinity = jnp.zeros((CHUNK, CHUNK), full)
    dlog = jnp.zeros((CHUNK, LANES), full)
    for pair in range(heads // 2):
        h0, h1 = 2 * pair, 2 * pair + 1
        span = slice(pair * LANES, (pair + 1) * LANES)
        cum0 = jnp.broadcast_to(cum_ref[:, h0 : h0 + 1], (CHUNK, CHUNK))
        cum1 = jnp.broadcast_to(cum_ref[:, h1 : h1 + 1], (CHUNK, CHUNK))
        m0 = jnp.exp(jnp.minimum(cum0 - cumt_ref[h0 : h0 + 1, :], 0.0))
        m1 = jnp.exp(jnp.minimum(cum1 - cumt_ref[h1 : h1 + 1, :], 0.0))
        w0 = m0 * masked
        w1 = m1 * masked
        dt_pair = jnp.where(left, dt_ref[:, h0 : h0 + 1], dt_ref[:, h1 : h1 + 1])
        x_pair = x_ref[:, span]
        u = x_pair * dt_pair
        u_low = u.astype(low)
        dy_pair = dy_ref[:, span]
        dy_low = dy_pair.astype(low)
        zero = jnp.zeros_like(dy_low)
        dy_both = jnp.concatenate([jnp.where(left, dy_low, zero), jnp.where(left, zero, dy_low)], axis=0)
        dw = dot_nt(dy_both, u_low)
        dw0, dw1 = dw[:CHUNK], dw[CHUNK:]
        d_affinity = d_affinity + dw0 * m0 + dw1 * m1
        z_both = jnp.concatenate([(dw0 * w0).astype(low), (dw1 * w1).astype(low)], axis=1)
        reach = dot_nn(onward, z_both)
        k0 = jnp.sum(jnp.where(row > col, reach[:, :CHUNK], 0.0), axis=1, keepdims=True)
        k1 = jnp.sum(jnp.where(row > col, reach[:, CHUNK:], 0.0), axis=1, keepdims=True)
        dlog = jnp.where(col == h0, k0, jnp.where(col == h1, k1, dlog))
        w_both = jnp.concatenate([w0.astype(low), w1.astype(low)], axis=0)
        cum_pair = jnp.where(left, cum0, cum1)
        end0 = cum_ref[CHUNK - 1 : CHUNK, h0 : h0 + 1]
        end1 = cum_ref[CHUNK - 1 : CHUNK, h1 : h1 + 1]
        ahead = jnp.exp(jnp.where(left, end0, end1) - cum_pair)
        since = jnp.exp(cum_pair)
        du_state = ahead * dot_nt(b_low, adjoint[span, :].astype(low))
        du = dot_tn(w_both, dy_both) + du_state
        dx_ref[:, span] = dt_pair * du + skip_ref[:, span] * dy_pair
        y_state = since * dot_nt(c_low, start_ref[0, span, :])
        xdu[:, span] = x_pair * du
        dyi[:, span] = dy_pair * y_state
        udu[:, span] = u * du_state
        dye[:, span] = (dy_pair * since).astype(low)
        uw[:, span] = (u * ahead).astype(low)
    inner_row = lax.broadcasted_iota(jnp.int32, (inner, LANES), 0)
    inner_col = lax.broadcasted_iota(jnp.int32, (inner, LANES), 1)
    pick = (inner_row // HEADDIM == inner_col).astype(full)
    ddt_ref[...] = dot_nn(xdu[...], pick, highest)
    by_state = dot_nn(dyi[...], pick, highest)
    by_later = dot_nn(udu[...], pick, highest)
    adjoint_now = adjoint[...]
    start_now = start_ref[0]
    both = adjoint_now * start_now.astype(full)
    over = dot_nn(dot_nt(jnp.ones((8, STATE), full), both, highest), pick, highest)
    ends = jnp.exp(cum_ref[CHUNK - 1 : CHUNK, :])
    dlog = dlog + over[0:1] * ends
    dlog = dlog + dot_nn((row <= col).astype(full), by_state, highest)
    dlog_ref[...] = dlog + dot_nn((row > col).astype(full), by_later, highest)
    d_aff = jnp.where(causal, d_affinity, 0.0).astype(low)
    dbc_ref[:, :STATE] = dot_tn(d_aff, c_low) + dot_nn(uw[...], adjoint_now.astype(low))
    dbc_ref[:, STATE:] = dot_nn(d_aff, b_low) + dot_nn(dye[...], start_now)
    fresh = dot_tn(dye[...], c_low)
    for pair in range(heads // 2):
        h0, h1 = 2 * pair, 2 * pair + 1
        span = slice(pair * LANES, (pair + 1) * LANES)
        shrink = jnp.where(row < HEADDIM, ends[:, h0 : h0 + 1], ends[:, h1 : h1 + 1])
        adjoint[span, :] = shrink * adjoint_now[span, :] + fresh[span, :]


def ssm_forward(act, dt, cum, cum_t, skip_row, entering):
    rows = act.shape[0]
    heads = cum_t.shape[0]
    inner = heads * HEADDIM
    blocks = rows // CHUNK
    return pl.pallas_call(
        fwd_kernel,
        grid=(blocks,),
        in_specs=[
            pl.BlockSpec((CHUNK, inner), lambda i: (i, 0)),
            pl.BlockSpec((CHUNK, 2 * STATE), lambda i: (i, inner // (2 * STATE))),
            pl.BlockSpec((CHUNK, LANES), lambda i: (i, 0)),
            pl.BlockSpec((CHUNK, LANES), lambda i: (i, 0)),
            pl.BlockSpec((heads, CHUNK), lambda i: (0, i)),
            pl.BlockSpec((1, inner), lambda i: (0, 0)),
            pl.BlockSpec((inner, STATE), lambda i: (0, 0)),
        ],
        out_specs=[
            pl.BlockSpec((CHUNK, inner), lambda i: (i, 0)),
            pl.BlockSpec((1, inner, STATE), lambda i: (i, 0, 0)),
        ],
        out_shape=[
            jax.ShapeDtypeStruct((rows, inner), full),
            jax.ShapeDtypeStruct((blocks, inner, STATE), low),
        ],
        scratch_shapes=[pltpu.VMEM((inner, STATE), full)],
        compiler_params=pltpu.CompilerParams(
            dimension_semantics=("arbitrary",), vmem_limit_bytes=40 * 1024 * 1024
        ),
        cost_estimate=pl.CostEstimate(
            flops=rows * inner * 2 * 4 * STATE,
            bytes_accessed=rows * inner * 10,
            transcendentals=rows * heads * CHUNK * 2,
        ),
        name="ssm_forward",
    )(act, act, dt, cum, cum_t, skip_row, entering)


def ssm_backward(act, dt, cum, cum_t, skip_row, dy, starts, later):
    rows = act.shape[0]
    heads = cum_t.shape[0]
    inner = heads * HEADDIM
    blocks = rows // CHUNK
    last = blocks - 1
    return pl.pallas_call(
        bwd_kernel,
        grid=(blocks,),
        in_specs=[
            pl.BlockSpec((CHUNK, inner), lambda i: (last - i, 0)),
            pl.BlockSpec((CHUNK, 2 * STATE), lambda i: (last - i, inner // (2 * STATE))),
            pl.BlockSpec((CHUNK, LANES), lambda i: (last - i, 0)),
            pl.BlockSpec((CHUNK, LANES), lambda i: (last - i, 0)),
            pl.BlockSpec((heads, CHUNK), lambda i: (0, last - i)),
            pl.BlockSpec((1, inner), lambda i: (0, 0)),
            pl.BlockSpec((CHUNK, inner), lambda i: (last - i, 0)),
            pl.BlockSpec((1, inner, STATE), lambda i: (last - i, 0, 0)),
            pl.BlockSpec((inner, STATE), lambda i: (0, 0)),
        ],
        out_specs=[
            pl.BlockSpec((CHUNK, inner), lambda i: (last - i, 0)),
            pl.BlockSpec((CHUNK, 2 * STATE), lambda i: (last - i, 0)),
            pl.BlockSpec((CHUNK, LANES), lambda i: (last - i, 0)),
            pl.BlockSpec((CHUNK, LANES), lambda i: (last - i, 0)),
        ],
        out_shape=[
            jax.ShapeDtypeStruct((rows, inner), full),
            jax.ShapeDtypeStruct((rows, 2 * STATE), full),
            jax.ShapeDtypeStruct((rows, LANES), full),
            jax.ShapeDtypeStruct((rows, LANES), full),
        ],
        scratch_shapes=[
            pltpu.VMEM((inner, STATE), full),
            pltpu.VMEM((CHUNK, inner), low),
            pltpu.VMEM((CHUNK, inner), low),
            pltpu.VMEM((CHUNK, inner), full),
            pltpu.VMEM((CHUNK, inner), full),
            pltpu.VMEM((CHUNK, inner), full),
        ],
        compiler_params=pltpu.CompilerParams(
            dimension_semantics=("arbitrary",), vmem_limit_bytes=40 * 1024 * 1024
        ),
        cost_estimate=pl.CostEstimate(
            flops=rows * inner * 2 * 16 * STATE,
            bytes_accessed=rows * inner * 16,
            transcendentals=rows * heads * CHUNK * 2,
        ),
        name="ssm_backward",
    )(act, act, dt, cum, cum_t, skip_row, dy, starts, later)


def heads_to_channels(values):
    return jnp.repeat(values, HEADDIM, axis=-1)


def silu_slope(value, sig):
    return sig * (1.0 + value * (1.0 - sig))


def layer_forward(hidden, valid, weights, params):
    gain, taps, step_bias, decay_log, skip, out_gain = params
    feed_weight, gate_weight, out_weight = weights
    rows, width = hidden.shape
    heads = step_bias.shape[0]
    inner = heads * HEADDIM
    channels = inner + 2 * STATE
    norm = lax.rsqrt(jnp.mean(hidden * hidden, axis=-1, keepdims=True) + epsilon)
    normed = (hidden * norm * gain).astype(low)
    feed_all = dot_nn(normed, feed_weight)
    feed = feed_all[:, :channels].astype(low)
    raw_step = steps_out(feed_all[:, channels:], heads)
    rim = shifted(feed[rows - CONV + 1 :], "ctx", 1)
    padded = jnp.concatenate([rim, feed], axis=0)
    gate = dot_nn(normed, gate_weight)
    pre = conv_total(padded, taps, rows)
    act = pre * jax.nn.sigmoid(pre)
    dt = jax.nn.softplus(raw_step + step_bias)
    log_decay = -jnp.exp(decay_log) * dt
    blocks = rows // CHUNK
    tril = jnp.tril(jnp.ones((CHUNK, CHUNK), full))
    cum = jnp.einsum("ts,csh->cth", tril, log_decay.reshape(blocks, CHUNK, heads), precision=highest)
    ends = cum[:, -1]
    running = jnp.cumsum(ends, axis=0)
    total = running[-1]
    since = (running - ends)[:, None] + cum
    decay_in = jnp.exp(since).reshape(rows, heads)
    to_end = jnp.exp(total - since).reshape(rows, heads) * dt
    cum = cum.reshape(rows, heads)
    weighted = (act[:, :inner] * heads_to_channels(to_end)).astype(low)
    local_state = dot_tn(weighted, act[:, inner : inner + STATE].astype(low))
    shrink = jnp.repeat(jnp.exp(total), HEADDIM)[:, None]
    entering = chain(local_state, shrink, 1)
    lanes = ((0, 0), (0, LANES - heads))
    skip_row = jnp.repeat(skip, HEADDIM)[None]
    scan = (jnp.pad(dt, lanes), jnp.pad(cum, lanes), cum.T, skip_row)
    ssm_out, starts = ssm_forward(act, *scan, entering)
    gated = ssm_out * (gate * jax.nn.sigmoid(gate))
    squares = jnp.sum(gated * gated, axis=-1)
    scaled = (gated * out_gain).astype(low)
    term = dot_nt(scaled, out_weight).astype(low)
    branch = term.astype(full) + swap_cores(term).astype(full)
    squares = squares + swap_cores(squares)
    out_norm = lax.rsqrt(squares / INNER + epsilon)[:, None]
    result = hidden + valid * out_norm * branch
    kept = (
        hidden, norm, normed, padded, act, gate, raw_step, dt, log_decay, decay_in, shrink,
        scan, starts, ssm_out, scaled, branch.astype(low), out_norm,
    )
    return result, kept


def steps_out(block, heads):
    count = lax.axis_size("tp")
    each = heads // count
    wide = block.shape[1] // count
    return columns(block[:, j * wide : j * wide + each] for j in range(count))


def steps_in(values, wide):
    count = lax.axis_size("tp")
    each = values.shape[1] // count
    return columns(
        jnp.pad(values[:, j * each : (j + 1) * each], ((0, 0), (0, wide - each))) for j in range(count)
    )


def conv_total(padded, taps, rows):
    wide = padded.astype(full)
    return taps[CONV] + sum(taps[k] * wide[k : k + rows] for k in range(CONV))


def chain(local_state, shrink, steps):
    entering = shifted(local_state.astype(low), "ctx", steps)
    for _ in range(lax.axis_size("ctx") - 2):
        leaving = shrink * entering.astype(full) + local_state
        entering = shifted(leaving.astype(low), "ctx", steps)
    return entering


def layer_backward(incoming, valid, weights, params, kept):
    gain, taps, step_bias, decay_log, skip, out_gain = params
    feed_weight, gate_weight, out_weight = weights
    (
        hidden, norm, normed, padded, act, gate, raw_step, dt, log_decay, decay_in, shrink,
        scan, starts, ssm_out, scaled, branch, out_norm,
    ) = kept
    rows, width = hidden.shape
    heads = step_bias.shape[0]
    inner = heads * HEADDIM
    channels = inner + 2 * STATE
    back_branch = (valid * incoming).astype(low)
    back_normed = dot_nn(back_branch, out_weight)
    back_wide = back_branch.astype(full)
    grad_out = dot_tn((back_wide * out_norm).astype(low), scaled).astype(low)
    along = jnp.sum(back_wide * branch.astype(full), axis=-1, keepdims=True)
    sig = jax.nn.sigmoid(gate)
    silu = gate * sig
    gated = ssm_out * silu
    grad_out_gain = jnp.sum(back_normed * gated * out_norm, axis=0)
    back_gated = out_norm * out_gain * back_normed - gated * (out_norm**3 * along / INNER)
    back_ssm = back_gated * silu
    back_gate = (back_gated * ssm_out * silu_slope(gate, sig)).astype(low)
    grad_gate = dot_tn(normed, back_gate).astype(low)
    weighted = (back_ssm * heads_to_channels(decay_in)).astype(low)
    local_adjoint = dot_tn(weighted, act[:, inner + STATE :].astype(low))
    later = chain(local_adjoint, shrink, -1)
    back_x, back_bc, back_dt, back_log = ssm_backward(act, *scan, back_ssm, starts, later)
    back_dt, back_log = back_dt[:, :heads], back_log[:, :heads]
    grad_skip = jnp.sum((back_ssm * act[:, :inner]).reshape(rows, heads, HEADDIM), axis=(0, 2))
    grad_decay = jnp.sum(back_log * log_decay, axis=0)
    back_raw = (back_dt - jnp.exp(decay_log) * back_log) * jax.nn.sigmoid(raw_step + step_bias)
    grad_step_bias = jnp.sum(back_raw, axis=0)
    pre = conv_total(padded, taps, rows)
    back_pre = columns([back_x, back_bc]) * silu_slope(pre, jax.nn.sigmoid(pre))
    following = shifted(back_pre[: CONV - 1], "ctx", -1)
    wide = padded.astype(full)
    grad_taps = jnp.stack(
        [jnp.sum(back_pre * wide[k : k + rows], axis=0) for k in range(CONV)]
        + [jnp.sum(back_pre, axis=0)]
    )
    extended = jnp.concatenate([back_pre, following], axis=0)
    back_feed = sum(taps[k] * extended[CONV - 1 - k : CONV - 1 - k + rows] for k in range(CONV))
    step_lanes = (feed_weight.shape[1] - channels) // lax.axis_size("tp")
    back_all = columns([back_feed.astype(low), steps_in(back_raw.astype(low), step_lanes)])
    term = (dot_nt(back_all, feed_weight) + dot_nt(back_gate, gate_weight)).astype(low)
    back_in = term.astype(full) + swap_cores(term).astype(full)
    grad_feed = dot_tn(normed, back_all).astype(low)
    grad_gain = jnp.sum(back_in * hidden * norm, axis=0)
    scaled_in = back_in * gain
    along_in = jnp.sum(scaled_in * hidden, axis=-1, keepdims=True)
    delta = norm * scaled_in - hidden * (norm**3 * along_in / width)
    small = jnp.concatenate(
        [
            grad_taps[:, :inner].reshape(-1), grad_taps[:, inner:].reshape(-1),
            grad_out_gain, grad_step_bias, grad_decay, grad_skip, grad_gain,
        ]
    )
    return delta, (grad_feed, grad_gate, grad_out), small


def reduce_grads(grads, inner):
    grad_feed, grad_gate, grad_out = grads
    count = lax.axis_size("tp")
    half = inner // 2

    def by_tp(half_a, half_b):
        rows = half_a.shape[0]
        joined = jnp.concatenate([half_a, half_b], axis=1).reshape(rows, count, -1)
        return jnp.moveaxis(joined, 1, 0)

    def plain(value):
        half_a, half_b = reduce_rows(value[:, :half], value[:, half:])
        return scatter_sum(by_tp(half_a, half_b), "tp")

    out_sum = plain(grad_out)
    gate_sum = plain(grad_gate)
    rest = grad_feed[:, inner:]
    steps = rest.shape[1] - 2 * STATE
    half_a, half_b = reduce_rows(
        columns([grad_feed[:, :half], rest[:, :STATE], rest[:, 2 * STATE : 2 * STATE + steps // 2]]),
        columns([grad_feed[:, half:inner], rest[:, STATE : 2 * STATE], rest[:, 2 * STATE + steps // 2 :]]),
    )
    split = half + STATE
    state = columns([half_a[:, half:split], half_b[:, half:split]])
    feed_parts = columns(
        [
            by_tp(half_a[:, :half], half_b[:, :half]),
            by_tp(half_a[:, split:], half_b[:, split:]),
            jnp.broadcast_to(state[None], (count,) + state.shape),
        ]
    )
    feed_sum = scatter_sum(feed_parts, "tp")
    return columns([feed_sum, gate_sum, out_sum])


def on_device(
    acts,
    cotangent,
    lengths,
    norm_gain,
    proj_gate_x,
    proj_state,
    proj_step,
    conv_inner,
    conv_state,
    step_bias,
    decay_log,
    skip_weight,
    out_gain,
    proj_out,
):
    micro_count, rows, width = (acts.shape[0], acts.shape[2], acts.shape[3])
    tp_count = lax.axis_size("tp")
    core = lax.axis_index("section")
    lane = lax.axis_index("tp")
    first = core == 0
    own_rows = proj_gate_x.shape[1]
    half = proj_gate_x.shape[3] // 2
    step_half = proj_step.shape[2] // 2
    heads = step_half * tp_count
    inner = half * tp_count
    quarter = 2 * STATE // tp_count
    wide = quarter

    state_part = lax.dynamic_slice_in_dim(proj_state[0], lane * quarter, quarter, 1)

    def pack(c):
        step = proj_step[0, :, c * step_half : (c + 1) * step_half]
        tail = jnp.pad(columns([step, norm_gain[0][:, None]]), ((0, 0), (0, wide - step_half - 1)))
        return columns(
            [
                proj_gate_x[0, :, 1, c * half : (c + 1) * half],
                state_part,
                tail,
                proj_gate_x[0, :, 0, c * half : (c + 1) * half],
                proj_out[0, c * half : (c + 1) * half].T,
            ]
        )

    def pack_small(c):
        return jnp.concatenate(
            [
                conv_inner[0, :, c * half : (c + 1) * half].reshape(-1),
                out_gain[0, c * half : (c + 1) * half],
                step_bias[0, c * step_half : (c + 1) * step_half],
                decay_log[0, c * step_half : (c + 1) * step_half],
                skip_weight[0, c * step_half : (c + 1) * step_half],
                conv_state[0].reshape(-1),
            ]
        )

    def both_layers(make):
        zero, one = make(0), make(1)
        keep = jnp.where(first, zero, one)
        came = swap_cores(jnp.where(first, one, zero))
        return jnp.where(first, keep, came), jnp.where(first, came, keep)

    small_layers = line_gather(jnp.stack(both_layers(pack_small)), "tp")

    def layer_params(layer):
        part = small_layers[:, layer]
        at = (CONV + 1) * half
        taps_inner = jnp.moveaxis(part[:, :at].reshape(tp_count, CONV + 1, half), 0, 1)
        gains = part[:, at : at + half].reshape(-1)
        at += half
        scalars = []
        for _ in range(3):
            scalars.append(part[:, at : at + step_half].reshape(-1))
            at += step_half
        taps_state = part[0, at:].reshape(CONV + 1, 2 * STATE)
        taps = columns([taps_inner.reshape(CONV + 1, inner), taps_state])
        return taps, scalars[0], scalars[1], scalars[2], gains

    cut = half + quarter + wide
    middle = tp_count // 2

    def gather_feed(part):
        def side(pieces):
            return columns(
                [
                    columns(pieces[..., :half]),
                    columns(pieces[..., half : half + quarter]),
                    columns(pieces[..., half + quarter :]),
                ]
            )

        half_a, half_b = gather_rows(side(part[:middle]), side(part[middle:]))
        x_end, s_end = middle * half, middle * (half + quarter)
        feed = columns(
            [
                half_a[:, :x_end], half_b[:, :x_end], half_a[:, x_end:s_end], half_b[:, x_end:s_end],
                half_a[:, s_end:], half_b[:, s_end:],
            ]
        )
        return feed, half_a[:, s_end + step_half].astype(full)

    def gather_pair(part):
        def side(pieces):
            return columns([columns(pieces[..., :half]), columns(pieces[..., half:])])

        half_a, half_b = gather_rows(side(part[:middle]), side(part[middle:]))
        x_end = middle * half
        return (
            columns([half_a[:, :x_end], half_b[:, :x_end]]),
            columns([half_a[:, x_end:], half_b[:, x_end:]]),
        )

    packs = both_layers(pack)
    along = []
    previous = None
    for layer in range(2):
        for part in (packs[layer][:, :cut], packs[layer][:, cut:]):
            if previous is not None:
                part, previous = lax.optimization_barrier((part, previous))
            previous = line_gather(part, "tp")
            along.append(previous)
    weights, params = [], []
    for layer in range(2):
        feed, gain = gather_feed(along[2 * layer])
        gate, out = gather_pair(along[2 * layer + 1])
        weights.append((feed, gate, out))
        params.append((gain,) + layer_params(layer))

    places = lax.axis_index("ctx") * rows + jnp.arange(rows, dtype=jnp.int32)
    length = lax.dynamic_index_in_dim(lengths[:, 0], lane, 0, False)
    valid = (places < length).astype(full)[:, None]
    hidden = lax.dynamic_index_in_dim(acts[:, 0], lane, 0, False).astype(full)
    out_grad = lax.dynamic_index_in_dim(cotangent[:, 0], lane, 0, False)

    result_first, kept_first = layer_forward(hidden, valid, weights[0], params[0])
    low_first = result_first.astype(low)
    result_last, kept_last = layer_forward(low_first.astype(full), valid, weights[1], params[1])
    own_result = jnp.where(first, low_first, result_last.astype(low))
    quarter_rows = rows // tp_count
    section_out = spread_rows(own_result.reshape(tp_count, quarter_rows, width), (0, 1))

    delta_last, grads_last, small_last = layer_backward(
        out_grad, valid, weights[1], params[1], kept_last
    )
    spread_last = spread_rows(delta_last.astype(low).reshape(tp_count, quarter_rows, width), (1,))
    sums_last = reduce_grads(grads_last, inner)
    incoming = (out_grad + delta_last).astype(low).astype(full)
    delta_first, grads_first, small_first = layer_backward(
        incoming, valid, weights[0], params[0], kept_first
    )
    grad_first = (incoming + delta_first).astype(low)
    spread_first = spread_rows(grad_first.reshape(tp_count, quarter_rows, width), (0,))
    sums_first = reduce_grads(grads_first, inner)
    own_cotangent = lax.dynamic_slice_in_dim(
        cotangent[:, 0], lane * quarter_rows, quarter_rows, 1
    )
    input_grad = jnp.where(
        first, spread_first.astype(full), own_cotangent + spread_last.astype(full)
    )

    small = jnp.stack([small_first, small_last])
    for axis in ("dp", "ctx", "tp"):
        small = all_sum(small, axis)
    small_keep = jnp.where(first, small[0], small[1])
    small_came = swap_cores(jnp.where(first, small[1], small[0]))
    keep = jnp.where(first, sums_first, sums_last)
    came = swap_cores(jnp.where(first, sums_last, sums_first))

    def halves(kept_part, came_part, axis):
        zero = jnp.where(first, kept_part, came_part)
        one = jnp.where(first, came_part, kept_part)
        return jnp.concatenate([zero, one], axis=axis)

    def own_lane(value, shape, axis):
        return lax.dynamic_index_in_dim(value.reshape(shape), lane, axis, False)

    at = half
    grad_x = halves(keep[:, :at], came[:, :at], 1)
    grad_step = halves(keep[:, at : at + step_half], came[:, at : at + step_half], 1)
    at += wide
    grad_state = keep[:, at : at + 2 * STATE] + came[:, at : at + 2 * STATE]
    at += 2 * STATE
    grad_gate = halves(keep[:, at : at + half], came[:, at : at + half], 1)
    at += half
    grad_out = halves(keep[:, at : at + half].T, came[:, at : at + half].T, 0)
    grad_gate_x = jnp.stack([grad_gate, grad_x], axis=1)

    at = (CONV + 1) * inner
    taps_shape = (CONV + 1, tp_count, half)
    grad_conv_inner = halves(
        own_lane(small_keep[:at], taps_shape, 1), own_lane(small_came[:at], taps_shape, 1), 1
    )
    end = at + (CONV + 1) * 2 * STATE
    grad_conv_state = (small_keep[at:end] + small_came[at:end]).reshape(CONV + 1, 2 * STATE)
    at = end
    vectors = []
    for size in (inner, heads, heads, heads):
        shape = (tp_count, size // tp_count)
        vectors.append(
            halves(
                own_lane(small_keep[at : at + size], shape, 0),
                own_lane(small_came[at : at + size], shape, 0),
                0,
            )
        )
        at += size
    owner = lax.axis_index("dp") * lax.axis_size("ctx") + lax.axis_index("ctx")
    grad_norm_gain = lax.dynamic_slice_in_dim(small_keep[at:], owner * own_rows, own_rows, 0)
    return (
        section_out[None, :, None],
        input_grad[None, :, None],
        grad_norm_gain[None],
        grad_gate_x[None],
        grad_state[None],
        grad_step[None],
        grad_conv_inner[None],
        grad_conv_state[None],
        vectors[1][None],
        vectors[2][None],
        vectors[3][None],
        vectors[0][None],
        grad_out[None],
    )


def solution(mesh):
    placed = (
        P(None, "dp", "ctx", None),
        P(None, "dp", "ctx", None),
        P(None, "dp"),
        P("section", ("dp", "ctx")),
        P("section", ("dp", "ctx"), None, "tp"),
        P("section", ("dp", "ctx"), None),
        P("section", ("dp", "ctx"), "tp"),
        P("section", None, "tp"),
        P("section", None, None),
        P("section", "tp"),
        P("section", "tp"),
        P("section", "tp"),
        P("section", "tp"),
        P("section", "tp", ("dp", "ctx")),
    )
    return jax.shard_map(
        on_device,
        mesh=mesh,
        in_specs=placed,
        out_specs=(
            P("section", None, "dp", ("ctx", "tp"), None),
            P("section", None, "dp", ("ctx", "tp"), None),
            P("section", ("dp", "ctx")),
            P("section", ("dp", "ctx"), None, "tp"),
            P("section", ("dp", "ctx"), None),
            P("section", ("dp", "ctx"), "tp"),
            P("section", None, "tp"),
            P("section", None, None),
            P("section", "tp"),
            P("section", "tp"),
            P("section", "tp"),
            P("section", "tp"),
            P("section", "tp", ("dp", "ctx")),
        ),
        check_vma=False,
    )
```

```python
import functools

import jax
import jax.numpy as jnp
from jax import lax
from jax.experimental import pallas as pl
from jax.experimental.pallas import tpu as pltpu
from jax.sharding import PartitionSpec as P

HEADDIM = 64
STATE = 128
INNER = 2048
CONV = 4
CHUNK = 128
LANES = 128

highest = lax.Precision.HIGHEST
epsilon = 1e-05
low = jnp.bfloat16
full = jnp.float32


def dot_nn(a, b, precision=None):
    return lax.dot_general(
        a, b, (((1,), (0,)), ((), ())), precision=precision, preferred_element_type=full
    )


def dot_nt(a, b, precision=None):
    return lax.dot_general(
        a, b, (((1,), (1,)), ((), ())), precision=precision, preferred_element_type=full
    )


def dot_tn(a, b, precision=None):
    return lax.dot_general(
        a, b, (((0,), (0,)), ((), ())), precision=precision, preferred_element_type=full
    )


def shifted(value, axis, steps):
    count = lax.axis_size(axis)
    first, last = (max(0, -steps), min(count, count - steps))
    return lax.ppermute(value, axis, [(source, source + steps) for source in range(first, last)])


def rotated(value, axis, steps):
    count = lax.axis_size(axis)
    return lax.ppermute(value, axis, [(i, (i + steps) % count) for i in range(count)])


def line_gather(value, axis, dim=0):
    count = lax.axis_size(axis)
    place = lax.axis_index(axis)
    if count == 1:
        return jnp.expand_dims(value, dim)
    if count == 2:
        other = rotated(value, axis, 1)
        first = place == 0
        return jnp.stack([jnp.where(first, value, other), jnp.where(first, other, value)], axis=dim)
    up = down = value
    before, after = [], []
    for _ in range(1, count):
        up = shifted(up, axis, 1)
        down = shifted(down, axis, -1)
        before.insert(0, up)
        after.append(down)
    line = jnp.stack(before + [value] + after, axis=dim)
    return lax.dynamic_slice_in_dim(line, count - 1 - place, count, dim)


def scatter_sum(parts, axis, dim=0):
    count = lax.axis_size(axis)
    place = lax.axis_index(axis)

    def pick(at):
        return columns(lax.dynamic_index_in_dim(part, at, dim, False) for part in parts)

    total = pick(place).astype(full)
    for steps in range(1, count):
        total = total + rotated(pick((place + steps) % count), axis, steps).astype(full)
    return total


def all_sum(value, axis):
    total = value
    for steps in range(1, lax.axis_size(axis)):
        total = total + rotated(value, axis, steps)
    return total


def swap_cores(value):
    return lax.ppermute(value, "section", [(0, 1), (1, 0)])


def spread_rows(value, pairs_of):
    count = lax.axis_size("tp")
    place = lax.axis_index("tp")
    result = jnp.zeros_like(value)
    own = lax.dynamic_index_in_dim(value, place, 0, False)
    result = lax.dynamic_update_index_in_dim(result, own, place, 0)
    for steps in range(1, count):
        block = lax.dynamic_index_in_dim(value, (place + steps) % count, 0, False)
        pairs = [
            (core * count + i, core * count + (i + steps) % count)
            for core in pairs_of
            for i in range(count)
        ]
        arrived = lax.ppermute(block, ("section", "tp"), pairs)
        result = lax.dynamic_update_index_in_dim(result, arrived, (place - steps) % count, 0)
    return result


def gather_rows(early, late):
    width = early.shape[-1]
    half_a = line_gather(line_gather(early, "ctx"), "dp").reshape(-1, width)
    half_b = line_gather(line_gather(late, "dp"), "ctx", 1).reshape(-1, width)
    return half_a, half_b


def columns(pieces):
    return jnp.concatenate(list(pieces), axis=-1)


def as_rows(vector, width):
    rows = -(-vector.shape[0] // (16 * width)) * 16
    return jnp.pad(vector, (0, rows * width - vector.shape[0])).reshape(rows, width)


def tied(value, other):
    return lax.optimization_barrier((value, other))


def fwd_kernel(x_ref, bc_ref, dt_ref, cum_ref, cumt_ref, skip_ref, enter_ref, y_ref, start_ref, state):
    @pl.when(pl.program_id(0) == 0)
    def _():
        state[...] = enter_ref[...].astype(full)

    heads = cumt_ref.shape[0]
    start_ref[0] = state[...].astype(low)
    b_low = bc_ref[:, :STATE].astype(low)
    c_low = bc_ref[:, STATE:].astype(low)
    row = lax.broadcasted_iota(jnp.int32, (CHUNK, CHUNK), 0)
    col = lax.broadcasted_iota(jnp.int32, (CHUNK, CHUNK), 1)
    left = col < HEADDIM
    upper = row < HEADDIM
    masked = jnp.where(row >= col, dot_nt(c_low, b_low), 0.0)
    for pair in range(heads // 2):
        h0, h1 = 2 * pair, 2 * pair + 1
        span = slice(pair * LANES, (pair + 1) * LANES)
        cum0 = jnp.broadcast_to(cum_ref[:, h0 : h0 + 1], (CHUNK, CHUNK))
        cum1 = jnp.broadcast_to(cum_ref[:, h1 : h1 + 1], (CHUNK, CHUNK))
        w0 = jnp.exp(jnp.minimum(cum0 - cumt_ref[h0 : h0 + 1, :], 0.0)) * masked
        w1 = jnp.exp(jnp.minimum(cum1 - cumt_ref[h1 : h1 + 1, :], 0.0)) * masked
        weights = jnp.concatenate([w0.astype(low), w1.astype(low)], axis=1)
        x_pair = x_ref[:, span]
        u = x_pair * jnp.where(left, dt_ref[:, h0 : h0 + 1], dt_ref[:, h1 : h1 + 1])
        u_low = u.astype(low)
        zero = jnp.zeros_like(u_low)
        u_both = jnp.concatenate([jnp.where(left, u_low, zero), jnp.where(left, zero, u_low)], axis=0)
        cum_pair = jnp.where(left, cum0, cum1)
        s_pair = state[span, :]
        carried = jnp.exp(cum_pair) * dot_nt(c_low, s_pair.astype(low))
        y_ref[:, span] = dot_nn(weights, u_both) + carried + skip_ref[:, span] * x_pair
        end0 = cum_ref[CHUNK - 1 : CHUNK, h0 : h0 + 1]
        end1 = cum_ref[CHUNK - 1 : CHUNK, h1 : h1 + 1]
        ahead = jnp.exp(jnp.where(left, end0, end1) - cum_pair)
        fresh = dot_tn((u * ahead).astype(low), b_low)
        state[span, :] = jnp.exp(jnp.where(upper, end0, end1)) * s_pair + fresh


def bwd_kernel(
    x_ref, bc_ref, dt_ref, cum_ref, cumt_ref, skip_ref, dy_ref, start_ref, later_ref,
    dx_ref, dbc_ref, ddt_ref, dlog_ref,
    adjoint, dye, uw, xdu, dyi, udu,
):
    @pl.when(pl.program_id(0) == 0)
    def _():
        adjoint[...] = later_ref[...].astype(full)

    heads = cumt_ref.shape[0]
    inner = heads * HEADDIM
    b_low = bc_ref[:, :STATE].astype(low)
    c_low = bc_ref[:, STATE:].astype(low)
    row = lax.broadcasted_iota(jnp.int32, (CHUNK, CHUNK), 0)
    col = lax.broadcasted_iota(jnp.int32, (CHUNK, CHUNK), 1)
    left = col < HEADDIM
    causal = row >= col
    onward = (row <= col).astype(low)
    masked = jnp.where(causal, dot_nt(c_low, b_low), 0.0)
    d_affinity = jnp.zeros((CHUNK, CHUNK), full)
    dlog = jnp.zeros((CHUNK, LANES), full)
    for pair in range(heads // 2):
        h0, h1 = 2 * pair, 2 * pair + 1
        span = slice(pair * LANES, (pair + 1) * LANES)
        cum0 = jnp.broadcast_to(cum_ref[:, h0 : h0 + 1], (CHUNK, CHUNK))
        cum1 = jnp.broadcast_to(cum_ref[:, h1 : h1 + 1], (CHUNK, CHUNK))
        m0 = jnp.exp(jnp.minimum(cum0 - cumt_ref[h0 : h0 + 1, :], 0.0))
        m1 = jnp.exp(jnp.minimum(cum1 - cumt_ref[h1 : h1 + 1, :], 0.0))
        w0 = m0 * masked
        w1 = m1 * masked
        dt_pair = jnp.where(left, dt_ref[:, h0 : h0 + 1], dt_ref[:, h1 : h1 + 1])
        x_pair = x_ref[:, span]
        u = x_pair * dt_pair
        u_low = u.astype(low)
        dy_pair = dy_ref[:, span]
        dy_low = dy_pair.astype(low)
        zero = jnp.zeros_like(dy_low)
        dy_both = jnp.concatenate([jnp.where(left, dy_low, zero), jnp.where(left, zero, dy_low)], axis=0)
        dw = dot_nt(dy_both, u_low)
        dw0, dw1 = dw[:CHUNK], dw[CHUNK:]
        d_affinity = d_affinity + dw0 * m0 + dw1 * m1
        z_both = jnp.concatenate([(dw0 * w0).astype(low), (dw1 * w1).astype(low)], axis=1)
        reach = dot_nn(onward, z_both)
        k0 = jnp.sum(jnp.where(row > col, reach[:, :CHUNK], 0.0), axis=1, keepdims=True)
        k1 = jnp.sum(jnp.where(row > col, reach[:, CHUNK:], 0.0), axis=1, keepdims=True)
        dlog = jnp.where(col == h0, k0, jnp.where(col == h1, k1, dlog))
        w_both = jnp.concatenate([w0.astype(low), w1.astype(low)], axis=0)
        cum_pair = jnp.where(left, cum0, cum1)
        end0 = cum_ref[CHUNK - 1 : CHUNK, h0 : h0 + 1]
        end1 = cum_ref[CHUNK - 1 : CHUNK, h1 : h1 + 1]
        ahead = jnp.exp(jnp.where(left, end0, end1) - cum_pair)
        since = jnp.exp(cum_pair)
        du_state = ahead * dot_nt(b_low, adjoint[span, :].astype(low))
        du = dot_tn(w_both, dy_both) + du_state
        dx_ref[:, span] = dt_pair * du + skip_ref[:, span] * dy_pair
        y_state = since * dot_nt(c_low, start_ref[0, span, :])
        xdu[:, span] = x_pair * du
        dyi[:, span] = dy_pair * y_state
        udu[:, span] = u * du_state
        dye[:, span] = (dy_pair * since).astype(low)
        uw[:, span] = (u * ahead).astype(low)
    inner_row = lax.broadcasted_iota(jnp.int32, (inner, LANES), 0)
    inner_col = lax.broadcasted_iota(jnp.int32, (inner, LANES), 1)
    pick = (inner_row // HEADDIM == inner_col).astype(full)
    ddt_ref[...] = dot_nn(xdu[...], pick, highest)
    by_state = dot_nn(dyi[...], pick, highest)
    by_later = dot_nn(udu[...], pick, highest)
    adjoint_now = adjoint[...]
    start_now = start_ref[0]
    both = adjoint_now * start_now.astype(full)
    over = dot_nn(dot_nt(jnp.ones((8, STATE), full), both, highest), pick, highest)
    ends = jnp.exp(cum_ref[CHUNK - 1 : CHUNK, :])
    dlog = dlog + over[0:1] * ends
    dlog = dlog + dot_nn((row <= col).astype(full), by_state, highest)
    dlog_ref[...] = dlog + dot_nn((row > col).astype(full), by_later, highest)
    d_aff = jnp.where(causal, d_affinity, 0.0).astype(low)
    dbc_ref[:, :STATE] = dot_tn(d_aff, c_low) + dot_nn(uw[...], adjoint_now.astype(low))
    dbc_ref[:, STATE:] = dot_nn(d_aff, b_low) + dot_nn(dye[...], start_now)
    fresh = dot_tn(dye[...], c_low)
    for pair in range(heads // 2):
        h0, h1 = 2 * pair, 2 * pair + 1
        span = slice(pair * LANES, (pair + 1) * LANES)
        shrink = jnp.where(row < HEADDIM, ends[:, h0 : h0 + 1], ends[:, h1 : h1 + 1])
        adjoint[span, :] = shrink * adjoint_now[span, :] + fresh[span, :]


def ssm_forward(act, dt, cum, cum_t, skip_row, entering):
    rows = act.shape[0]
    heads = cum_t.shape[0]
    inner = heads * HEADDIM
    blocks = rows // CHUNK
    return pl.pallas_call(
        fwd_kernel,
        grid=(blocks,),
        in_specs=[
            pl.BlockSpec((CHUNK, inner), lambda i: (i, 0)),
            pl.BlockSpec((CHUNK, 2 * STATE), lambda i: (i, inner // (2 * STATE))),
            pl.BlockSpec((CHUNK, LANES), lambda i: (i, 0)),
            pl.BlockSpec((CHUNK, LANES), lambda i: (i, 0)),
            pl.BlockSpec((heads, CHUNK), lambda i: (0, i)),
            pl.BlockSpec((1, inner), lambda i: (0, 0)),
            pl.BlockSpec((inner, STATE), lambda i: (0, 0)),
        ],
        out_specs=[
            pl.BlockSpec((CHUNK, inner), lambda i: (i, 0)),
            pl.BlockSpec((1, inner, STATE), lambda i: (i, 0, 0)),
        ],
        out_shape=[
            jax.ShapeDtypeStruct((rows, inner), full),
            jax.ShapeDtypeStruct((blocks, inner, STATE), low),
        ],
        scratch_shapes=[pltpu.VMEM((inner, STATE), full)],
        compiler_params=pltpu.CompilerParams(
            dimension_semantics=("arbitrary",), vmem_limit_bytes=40 * 1024 * 1024
        ),
        cost_estimate=pl.CostEstimate(
            flops=rows * inner * 2 * 4 * STATE,
            bytes_accessed=rows * inner * 10,
            transcendentals=rows * heads * CHUNK * 2,
        ),
        name="ssm_forward",
    )(act, act, dt, cum, cum_t, skip_row, entering)


def ssm_backward(act, dt, cum, cum_t, skip_row, dy, starts, later):
    rows = act.shape[0]
    heads = cum_t.shape[0]
    inner = heads * HEADDIM
    blocks = rows // CHUNK
    last = blocks - 1
    return pl.pallas_call(
        bwd_kernel,
        grid=(blocks,),
        in_specs=[
            pl.BlockSpec((CHUNK, inner), lambda i: (last - i, 0)),
            pl.BlockSpec((CHUNK, 2 * STATE), lambda i: (last - i, inner // (2 * STATE))),
            pl.BlockSpec((CHUNK, LANES), lambda i: (last - i, 0)),
            pl.BlockSpec((CHUNK, LANES), lambda i: (last - i, 0)),
            pl.BlockSpec((heads, CHUNK), lambda i: (0, last - i)),
            pl.BlockSpec((1, inner), lambda i: (0, 0)),
            pl.BlockSpec((CHUNK, inner), lambda i: (last - i, 0)),
            pl.BlockSpec((1, inner, STATE), lambda i: (last - i, 0, 0)),
            pl.BlockSpec((inner, STATE), lambda i: (0, 0)),
        ],
        out_specs=[
            pl.BlockSpec((CHUNK, inner), lambda i: (last - i, 0)),
            pl.BlockSpec((CHUNK, 2 * STATE), lambda i: (last - i, 0)),
            pl.BlockSpec((CHUNK, LANES), lambda i: (last - i, 0)),
            pl.BlockSpec((CHUNK, LANES), lambda i: (last - i, 0)),
        ],
        out_shape=[
            jax.ShapeDtypeStruct((rows, inner), full),
            jax.ShapeDtypeStruct((rows, 2 * STATE), full),
            jax.ShapeDtypeStruct((rows, LANES), full),
            jax.ShapeDtypeStruct((rows, LANES), full),
        ],
        scratch_shapes=[
            pltpu.VMEM((inner, STATE), full),
            pltpu.VMEM((CHUNK, inner), low),
            pltpu.VMEM((CHUNK, inner), low),
            pltpu.VMEM((CHUNK, inner), full),
            pltpu.VMEM((CHUNK, inner), full),
            pltpu.VMEM((CHUNK, inner), full),
        ],
        compiler_params=pltpu.CompilerParams(
            dimension_semantics=("arbitrary",), vmem_limit_bytes=40 * 1024 * 1024
        ),
        cost_estimate=pl.CostEstimate(
            flops=rows * inner * 2 * 16 * STATE,
            bytes_accessed=rows * inner * 16,
            transcendentals=rows * heads * CHUNK * 2,
        ),
        name="ssm_backward",
    )(act, act, dt, cum, cum_t, skip_row, dy, starts, later)


def heads_to_channels(values):
    heads = values.shape[1]
    head = lax.broadcasted_iota(jnp.int32, (heads, heads * HEADDIM), 0)
    channel = lax.broadcasted_iota(jnp.int32, (heads, heads * HEADDIM), 1)
    return dot_nn(values, (channel // HEADDIM == head).astype(full), highest)


def silu_slope(value, sig):
    return sig * (1.0 + value * (1.0 - sig))


def layer_forward(hidden, valid, weights, params):
    gain, taps, step_bias, decay_log, skip, out_gain = params
    feed_weight, gate_weight, out_weight = weights
    rows, width = hidden.shape
    heads = step_bias.shape[0]
    inner = heads * HEADDIM
    channels = inner + 2 * STATE
    norm = lax.rsqrt(jnp.mean(hidden * hidden, axis=-1, keepdims=True) + epsilon)
    normed = (hidden * norm * gain).astype(low)
    feed_all = dot_nn(normed, feed_weight)
    feed = feed_all[:, :channels].astype(low)
    raw_step = feed_all[:, channels : channels + heads]
    rim = shifted(feed[rows - CONV + 1 :], "ctx", 1)
    padded = jnp.concatenate([rim, feed], axis=0)
    gate = dot_nn(normed, gate_weight)
    pre = conv_total(padded, taps, rows)
    act = pre * jax.nn.sigmoid(pre)
    dt = jax.nn.softplus(raw_step + step_bias)
    log_decay = -jnp.exp(decay_log) * dt
    blocks = rows // CHUNK
    tril = jnp.tril(jnp.ones((CHUNK, CHUNK), full))
    cum = jnp.einsum("ts,csh->cth", tril, log_decay.reshape(blocks, CHUNK, heads), precision=highest)
    ends = cum[:, -1]
    running = jnp.cumsum(ends, axis=0)
    total = running[-1]
    since = (running - ends)[:, None] + cum
    decay_in = jnp.exp(since).reshape(rows, heads)
    to_end = jnp.exp(total - since).reshape(rows, heads) * dt
    cum = cum.reshape(rows, heads)
    weighted = (act[:, :inner] * heads_to_channels(to_end)).astype(low)
    local_state = dot_tn(weighted, act[:, inner : inner + STATE].astype(low))
    shrink = jnp.repeat(jnp.exp(total), HEADDIM)[:, None]
    entering = chain(local_state, shrink, 1)
    lanes = ((0, 0), (0, LANES - heads))
    skip_row = jnp.repeat(skip, HEADDIM)[None]
    scan = (jnp.pad(dt, lanes), jnp.pad(cum, lanes), cum.T, skip_row)
    ssm_out, starts = ssm_forward(act, *scan, entering)
    gated = ssm_out * (gate * jax.nn.sigmoid(gate))
    squares = jnp.sum(gated * gated, axis=-1)
    scaled = (gated * out_gain).astype(low)
    term = dot_nt(scaled, out_weight).astype(low)
    branch = term.astype(full) + swap_cores(term).astype(full)
    squares = squares + swap_cores(squares)
    out_norm = lax.rsqrt(squares / INNER + epsilon)[:, None]
    result = hidden + valid * out_norm * branch
    kept = (
        hidden, norm, normed, padded, act, gate, raw_step, dt, log_decay, decay_in, shrink,
        scan, starts, ssm_out, scaled, branch.astype(low), out_norm,
    )
    return result, kept


def conv_total(padded, taps, rows):
    wide = padded.astype(full)
    return taps[CONV] + sum(taps[k] * wide[k : k + rows] for k in range(CONV))


def chain(local_state, shrink, steps):
    entering = shifted(local_state.astype(low), "ctx", steps)
    for _ in range(lax.axis_size("ctx") - 2):
        leaving = shrink * entering.astype(full) + local_state
        entering = shifted(leaving.astype(low), "ctx", steps)
    return entering


def layer_backward(incoming, valid, weights, params, kept, pending=None):
    gain, taps, step_bias, decay_log, skip, out_gain = params
    feed_weight, gate_weight, out_weight = weights
    (
        hidden, norm, normed, padded, act, gate, raw_step, dt, log_decay, decay_in, shrink,
        scan, starts, ssm_out, scaled, branch, out_norm,
    ) = kept
    rows, width = hidden.shape
    heads = step_bias.shape[0]
    inner = heads * HEADDIM
    channels = inner + 2 * STATE
    back_branch = (valid * incoming).astype(low)
    back_normed = dot_nn(back_branch, out_weight)
    back_wide = back_branch.astype(full)
    grad_out = dot_tn((back_wide * out_norm).astype(low), scaled).astype(low)
    along = jnp.sum(back_wide * branch.astype(full), axis=-1, keepdims=True)
    sig = jax.nn.sigmoid(gate)
    silu = gate * sig
    gated = ssm_out * silu
    grad_out_gain = jnp.sum(back_normed * gated * out_norm, axis=0)
    back_gated = out_norm * out_gain * back_normed - gated * (out_norm**3 * along / INNER)
    back_ssm = back_gated * silu
    back_gate = (back_gated * ssm_out * silu_slope(gate, sig)).astype(low)
    grad_gate = dot_tn(normed, back_gate).astype(low)
    weighted = (back_ssm * heads_to_channels(decay_in)).astype(low)
    local_adjoint = dot_tn(weighted, act[:, inner + STATE :].astype(low))
    later = chain(local_adjoint, shrink, -1)
    early = None
    if pending is not None:
        early = Reduction([grad_gate], [grad_out])
        back_ssm, pending.sums = tied(back_ssm, pending.sums)
        pending.second()
        early.first()
    back_x, back_bc, back_dt, back_log = ssm_backward(act, *scan, back_ssm, starts, later)
    if pending is not None:
        back_x, (pending.sums, early.sums) = tied(back_x, (pending.sums, early.sums))
        pending.sums = scatter_sum(pending.blocks(pending.sums), "tp")
        early.second()
    back_dt, back_log = back_dt[:, :heads], back_log[:, :heads]
    grad_skip = jnp.sum((back_ssm * act[:, :inner]).reshape(rows, heads, HEADDIM), axis=(0, 2))
    grad_decay = jnp.sum(back_log * log_decay, axis=0)
    back_raw = (back_dt - jnp.exp(decay_log) * back_log) * jax.nn.sigmoid(raw_step + step_bias)
    grad_step_bias = jnp.sum(back_raw, axis=0)
    pre = conv_total(padded, taps, rows)
    back_pre = columns([back_x, back_bc]) * silu_slope(pre, jax.nn.sigmoid(pre))
    following = shifted(back_pre[: CONV - 1], "ctx", -1)
    wide = padded.astype(full)
    grad_taps = jnp.stack(
        [jnp.sum(back_pre * wide[k : k + rows], axis=0) for k in range(CONV)]
        + [jnp.sum(back_pre, axis=0)]
    )
    extended = jnp.concatenate([back_pre, following], axis=0)
    back_feed = sum(taps[k] * extended[CONV - 1 - k : CONV - 1 - k + rows] for k in range(CONV))
    spare = feed_weight.shape[1] - channels - heads
    back_all = columns([back_feed.astype(low), jnp.pad(back_raw.astype(low), ((0, 0), (0, spare)))])
    term = (dot_nt(back_all, feed_weight) + dot_nt(back_gate, gate_weight)).astype(low)
    if pending is not None:
        term, (pending.sums, early.sums) = tied(term, (pending.sums, early.sums))
        early.sums = scatter_sum([by_tp(early.sums[0]), by_tp(early.sums[1])], "tp")
    back_in = term.astype(full) + swap_cores(term).astype(full)
    grad_feed = dot_tn(normed, back_all).astype(low)
    grad_gain = jnp.sum(back_in * hidden * norm, axis=0)
    scaled_in = back_in * gain
    along_in = jnp.sum(scaled_in * hidden, axis=-1, keepdims=True)
    delta = norm * scaled_in - hidden * (norm**3 * along_in / width)
    small = jnp.concatenate(
        [
            grad_taps[:, :inner].reshape(-1), grad_taps[:, inner:].reshape(-1),
            grad_out_gain, grad_step_bias, grad_decay, grad_skip, grad_gain,
        ]
    )
    return delta, (grad_feed, grad_gate, grad_out), small, early


def by_tp(value):
    return jnp.moveaxis(value.reshape(value.shape[0], lax.axis_size("tp"), -1), 1, 0)


class Reduction:
    def __init__(self, half_a, half_b):
        ndp, nctx = lax.axis_size("dp"), lax.axis_size("ctx")
        rows = half_a[0].shape[0] // (ndp * nctx)
        self.halves = [
            [part.reshape(ndp, nctx, rows, part.shape[1]) for part in half] for half in (half_a, half_b)
        ]

    def first(self):
        self.sums = (
            scatter_sum(self.halves[0], "ctx", 1).astype(low),
            scatter_sum(self.halves[1], "dp", 0).astype(low),
        )

    def second(self):
        self.sums = (
            scatter_sum([self.sums[0]], "dp").astype(low),
            scatter_sum([self.sums[1]], "ctx").astype(low),
        )


def feed_blocks(feed, inner):
    rest = feed[:, inner:]
    return [by_tp(feed[:, :inner]), jnp.broadcast_to(rest, (lax.axis_size("tp"),) + rest.shape)]


def on_device(
    acts,
    cotangent,
    lengths,
    norm_gain,
    proj_gate_x,
    proj_state,
    proj_step,
    conv_inner,
    conv_state,
    step_bias,
    decay_log,
    skip_weight,
    out_gain,
    proj_out,
):
    micro_count, rows, width = (acts.shape[0], acts.shape[2], acts.shape[3])
    tp_count = lax.axis_size("tp")
    core = lax.axis_index("section")
    lane = lax.axis_index("tp")
    first = core == 0
    own_rows = proj_gate_x.shape[1]
    half = proj_gate_x.shape[3] // 2
    step_half = proj_step.shape[2] // 2
    heads = step_half * tp_count
    inner = half * tp_count
    quarter = 2 * STATE // tp_count
    wide = quarter

    state_part = lax.dynamic_slice_in_dim(proj_state[0], lane * quarter, quarter, 1)

    def pack(c):
        step = proj_step[0, :, c * step_half : (c + 1) * step_half]
        tail = jnp.pad(columns([step, norm_gain[0][:, None]]), ((0, 0), (0, wide - step_half - 1)))
        return columns(
            [
                proj_gate_x[0, :, 1, c * half : (c + 1) * half],
                state_part,
                tail,
                proj_gate_x[0, :, 0, c * half : (c + 1) * half],
                proj_out[0, c * half : (c + 1) * half].T,
            ]
        )

    def pack_small(c):
        vector = jnp.concatenate(
            [
                conv_inner[0, :, c * half : (c + 1) * half].reshape(-1),
                out_gain[0, c * half : (c + 1) * half],
                step_bias[0, c * step_half : (c + 1) * step_half],
                decay_log[0, c * step_half : (c + 1) * step_half],
                skip_weight[0, c * step_half : (c + 1) * step_half],
                conv_state[0].reshape(-1),
            ]
        )
        parts = []
        for _ in range(3):
            part = lax.reduce_precision(vector, 8, 7)
            parts.append(part.astype(low))
            vector = vector - part
        return as_rows(jnp.concatenate(parts), cut)

    def both_layers(make):
        zero, one = make(0), make(1)
        keep = jnp.where(first, zero, one)
        came = swap_cores(jnp.where(first, one, zero))
        return jnp.where(first, keep, came), jnp.where(first, came, keep)

    def layer_params(rows_of_small):
        size = (CONV + 1) * half + half + 3 * step_half + (CONV + 1) * 2 * STATE
        three = rows_of_small.reshape(tp_count, -1)[:, : 3 * size].reshape(tp_count, 3, size)
        part = jnp.sum(three.astype(full), axis=1)
        at = (CONV + 1) * half
        taps_inner = jnp.moveaxis(part[:, :at].reshape(tp_count, CONV + 1, half), 0, 1)
        gains = part[:, at : at + half].reshape(-1)
        at += half
        scalars = []
        for _ in range(3):
            scalars.append(part[:, at : at + step_half].reshape(-1))
            at += step_half
        taps_state = part[0, at:].reshape(CONV + 1, 2 * STATE)
        taps = columns([taps_inner.reshape(CONV + 1, inner), taps_state])
        return taps, scalars[0], scalars[1], scalars[2], gains

    cut = half + quarter + wide
    middle = tp_count // 2

    def gather_item(part, sections):
        def side(pieces):
            parts, at = [], 0
            for size in sections:
                parts.append(columns(pieces[..., at : at + size]))
                at += size
            return columns(parts)

        half_a, half_b = gather_rows(side(part[:middle]), side(part[middle:]))
        result, at = [], 0
        for size in sections:
            result.append((half_a[:, at : at + middle * size], half_b[:, at : at + middle * size]))
            at += middle * size
        return result

    def feed_weights(parts):
        tails = [side.reshape(-1, middle, wide)[:, :, :step_half].reshape(-1, heads // 2) for side in parts[2]]
        gain = parts[2][0][:, step_half].astype(full)
        steps = jnp.pad(columns(tails), ((0, 0), (0, LANES - heads)))
        return columns(parts[0] + parts[1] + (steps,)), gain

    smalls = both_layers(pack_small)
    packs = both_layers(pack)
    feed_sections, pair_sections = (half, quarter, wide), (half, half)
    along_feed = line_gather(jnp.concatenate([packs[0][:, :cut], smalls[0]], axis=0), "tp")
    pair_pack, along_feed = tied(packs[0][:, cut:], along_feed)
    along_pair = line_gather(pair_pack, "tp")
    feed_parts = gather_item(along_feed[:, :own_rows], feed_sections)
    last_pack, feed_parts = tied(packs[1], feed_parts)
    small_pad = jnp.pad(smalls[1], ((0, 0), (0, last_pack.shape[1] - cut)))
    along_last = line_gather(jnp.concatenate([last_pack, small_pad], axis=0), "tp")
    pair_parts = gather_item(along_pair, pair_sections)
    along_last, pair_parts = tied(along_last, pair_parts)
    last_parts = gather_item(along_last[:, :own_rows, :cut], feed_sections)
    along_last, last_parts = tied(along_last, last_parts)
    last_parts += gather_item(along_last[:, :own_rows, cut:], pair_sections)
    feed_first, gain_first = feed_weights(feed_parts)
    feed_last, gain_last = feed_weights(last_parts[:3])
    weights = [
        (feed_first, columns(pair_parts[0]), columns(pair_parts[1])),
        (feed_last, columns(last_parts[3]), columns(last_parts[4])),
    ]
    params = [
        (gain_first,) + layer_params(along_feed[:, own_rows:]),
        (gain_last,) + layer_params(along_last[:, own_rows:, :cut]),
    ]

    places = lax.axis_index("ctx") * rows + jnp.arange(rows, dtype=jnp.int32)
    length = lax.dynamic_index_in_dim(lengths[:, 0], lane, 0, False)
    valid = (places < length).astype(full)[:, None]
    hidden = lax.dynamic_index_in_dim(acts[:, 0], lane, 0, False).astype(full)
    out_grad = lax.dynamic_index_in_dim(cotangent[:, 0], lane, 0, False)

    result_first, kept_first = layer_forward(hidden, valid, weights[0], params[0])
    low_first = result_first.astype(low)
    result_last, kept_last = layer_forward(low_first.astype(full), valid, weights[1], params[1])
    own_result = jnp.where(first, low_first, result_last.astype(low))
    quarter_rows = rows // tp_count
    section_out = spread_rows(own_result.reshape(tp_count, quarter_rows, width), (0, 1))

    delta_last, grads_last, small_last, _ = layer_backward(
        out_grad, valid, weights[1], params[1], kept_last
    )
    feed_last, gate_last, out_last = grads_last
    share = inner // 4
    last = Reduction([feed_last, out_last[:, :share]], [gate_last, out_last[:, share:]])

    def last_blocks(sums):
        at = feed_last.shape[1]
        out_part = columns([sums[0][:, at:], sums[1][:, inner:]])
        return [by_tp(sums[1][:, :inner]), by_tp(out_part)] + feed_blocks(sums[0][:, :at], inner)

    last.blocks = last_blocks
    last.first()
    spread_last = spread_rows(delta_last.astype(low).reshape(tp_count, quarter_rows, width), (1,))
    incoming = (out_grad + delta_last).astype(low).astype(full)
    delta_first, grads_first, small_first, early = layer_backward(
        incoming, valid, weights[0], params[0], kept_first, last
    )
    feed_first = grads_first[0]
    part = inner // 2 + LANES
    feed = Reduction([feed_first[:, :part]], [feed_first[:, part:]])
    feed.first()
    small = jnp.stack([small_first, small_last])
    grad_first = (incoming + delta_first).astype(low)
    spread_first = spread_rows(grad_first.reshape(tp_count, quarter_rows, width), (0,))
    small = all_sum(all_sum(small, "ctx"), "dp")
    feed.second()
    payload = columns(feed_blocks(columns(feed.sums), inner))
    extra = as_rows(small.astype(low).reshape(-1), payload.shape[2])
    payload = jnp.concatenate([payload, jnp.broadcast_to(extra, (tp_count,) + extra.shape)], axis=1)
    feed_sums = scatter_sum([payload], "tp")
    own_cotangent = lax.dynamic_slice_in_dim(
        cotangent[:, 0], lane * quarter_rows, quarter_rows, 1
    )
    input_grad = jnp.where(
        first, spread_first.astype(full), own_cotangent + spread_last.astype(full)
    )

    size = small_first.shape[0]
    small_sums = feed_sums[own_rows:].reshape(-1)[: 2 * size].reshape(2, size)
    sums_first = columns([early.sums, feed_sums[:own_rows]])
    sums_last = last.sums
    total_width = sums_first.shape[1]
    joined = [
        jnp.concatenate([sums, as_rows(vector, total_width)])
        for sums, vector in zip((sums_first, sums_last), small_sums)
    ]
    keep = jnp.where(first, joined[0], joined[1])
    came = swap_cores(jnp.where(first, joined[1], joined[0]))
    small_keep = keep[own_rows:].reshape(-1)[:size]
    small_came = came[own_rows:].reshape(-1)[:size]
    keep, came = keep[:own_rows], came[:own_rows]

    def halves(kept_part, came_part, axis):
        zero = jnp.where(first, kept_part, came_part)
        one = jnp.where(first, came_part, kept_part)
        return jnp.concatenate([zero, one], axis=axis)

    def own_lane(value, shape, axis):
        return lax.dynamic_index_in_dim(value.reshape(shape), lane, axis, False)

    grad_gate = halves(keep[:, :half], came[:, :half], 1)
    at = half
    grad_out = halves(keep[:, at : at + half].T, came[:, at : at + half].T, 0)
    at += half
    grad_x = halves(keep[:, at : at + half], came[:, at : at + half], 1)
    at += half
    grad_state = keep[:, at : at + 2 * STATE] + came[:, at : at + 2 * STATE]
    at += 2 * STATE + lane * step_half
    grad_step = halves(
        lax.dynamic_slice_in_dim(keep, at, step_half, 1), lax.dynamic_slice_in_dim(came, at, step_half, 1), 1
    )
    grad_gate_x = jnp.stack([grad_gate, grad_x], axis=1)

    at = (CONV + 1) * inner
    taps_shape = (CONV + 1, tp_count, half)
    grad_conv_inner = halves(
        own_lane(small_keep[:at], taps_shape, 1), own_lane(small_came[:at], taps_shape, 1), 1
    )
    end = at + (CONV + 1) * 2 * STATE
    grad_conv_state = (small_keep[at:end] + small_came[at:end]).reshape(CONV + 1, 2 * STATE)
    at = end
    vectors = []
    for size in (inner, heads, heads, heads):
        shape = (tp_count, size // tp_count)
        vectors.append(
            halves(
                own_lane(small_keep[at : at + size], shape, 0),
                own_lane(small_came[at : at + size], shape, 0),
                0,
            )
        )
        at += size
    owner = lax.axis_index("dp") * lax.axis_size("ctx") + lax.axis_index("ctx")
    grad_norm_gain = lax.dynamic_slice_in_dim(small_keep[at:], owner * own_rows, own_rows, 0)
    return (
        section_out[None, :, None],
        input_grad[None, :, None],
        grad_norm_gain[None],
        grad_gate_x[None],
        grad_state[None],
        grad_step[None],
        grad_conv_inner[None],
        grad_conv_state[None],
        vectors[1][None],
        vectors[2][None],
        vectors[3][None],
        vectors[0][None],
        grad_out[None],
    )


def solution(mesh):
    placed = (
        P(None, "dp", "ctx", None),
        P(None, "dp", "ctx", None),
        P(None, "dp"),
        P("section", ("dp", "ctx")),
        P("section", ("dp", "ctx"), None, "tp"),
        P("section", ("dp", "ctx"), None),
        P("section", ("dp", "ctx"), "tp"),
        P("section", None, "tp"),
        P("section", None, None),
        P("section", "tp"),
        P("section", "tp"),
        P("section", "tp"),
        P("section", "tp"),
        P("section", "tp", ("dp", "ctx")),
    )
    return jax.shard_map(
        on_device,
        mesh=mesh,
        in_specs=placed,
        out_specs=(
            P("section", None, "dp", ("ctx", "tp"), None),
            P("section", None, "dp", ("ctx", "tp"), None),
            P("section", ("dp", "ctx")),
            P("section", ("dp", "ctx"), None, "tp"),
            P("section", ("dp", "ctx"), None),
            P("section", ("dp", "ctx"), "tp"),
            P("section", None, "tp"),
            P("section", None, None),
            P("section", "tp"),
            P("section", "tp"),
            P("section", "tp"),
            P("section", "tp"),
            P("section", "tp", ("dp", "ctx")),
        ),
        check_vma=False,
    )
```

```python
import functools

import jax
import jax.numpy as jnp
from jax import lax
from jax.experimental import pallas as pl
from jax.experimental.pallas import tpu as pltpu
from jax.sharding import PartitionSpec as P

HEADDIM = 64
STATE = 128
INNER = 2048
CONV = 4
CHUNK = 128
LANES = 128
RIM = 16

highest = lax.Precision.HIGHEST
epsilon = 1e-05
low = jnp.bfloat16
full = jnp.float32


def dot_nn(a, b, precision=None):
    return lax.dot_general(
        a, b, (((1,), (0,)), ((), ())), precision=precision, preferred_element_type=full
    )


def dot_nt(a, b, precision=None):
    return lax.dot_general(
        a, b, (((1,), (1,)), ((), ())), precision=precision, preferred_element_type=full
    )


def dot_tn(a, b, precision=None):
    return lax.dot_general(
        a, b, (((0,), (0,)), ((), ())), precision=precision, preferred_element_type=full
    )


def shifted(value, axis, steps):
    count = lax.axis_size(axis)
    first, last = (max(0, -steps), min(count, count - steps))
    return lax.ppermute(value, axis, [(source, source + steps) for source in range(first, last)])


def rotated(value, axis, steps):
    count = lax.axis_size(axis)
    return lax.ppermute(value, axis, [(i, (i + steps) % count) for i in range(count)])


def line_gather(value, axis, dim=0):
    count = lax.axis_size(axis)
    place = lax.axis_index(axis)
    if count == 1:
        return jnp.expand_dims(value, dim)
    if count == 2:
        other = rotated(value, axis, 1)
        first = place == 0
        return jnp.stack([jnp.where(first, value, other), jnp.where(first, other, value)], axis=dim)
    up = down = value
    before, after = [], []
    for _ in range(1, count):
        up = shifted(up, axis, 1)
        down = shifted(down, axis, -1)
        before.insert(0, up)
        after.append(down)
    line = jnp.stack(before + [value] + after, axis=dim)
    return lax.dynamic_slice_in_dim(line, count - 1 - place, count, dim)


def scatter_sum(parts, axis, dim=0):
    count = lax.axis_size(axis)
    place = lax.axis_index(axis)

    def pick(at):
        return columns(lax.dynamic_index_in_dim(part, at, dim, False) for part in parts)

    total = pick(place).astype(full)
    for steps in range(1, count):
        total = total + rotated(pick((place + steps) % count), axis, steps).astype(full)
    return total


def all_sum(value, axis):
    total = value
    for steps in range(1, lax.axis_size(axis)):
        total = total + rotated(value, axis, steps)
    return total


def swap_cores(value):
    return lax.ppermute(value, "section", [(0, 1), (1, 0)])


def spread_rows(value, pairs_of):
    count = lax.axis_size("tp")
    place = lax.axis_index("tp")
    result = jnp.zeros_like(value)
    own = lax.dynamic_index_in_dim(value, place, 0, False)
    result = lax.dynamic_update_index_in_dim(result, own, place, 0)
    for steps in range(1, count):
        block = lax.dynamic_index_in_dim(value, (place + steps) % count, 0, False)
        pairs = [
            (core * count + i, core * count + (i + steps) % count)
            for core in pairs_of
            for i in range(count)
        ]
        arrived = lax.ppermute(block, ("section", "tp"), pairs)
        result = lax.dynamic_update_index_in_dim(result, arrived, (place - steps) % count, 0)
    return result


def gather_rows(early, late):
    width = early.shape[-1]
    half_a = line_gather(line_gather(early, "ctx"), "dp").reshape(-1, width)
    half_b = line_gather(line_gather(late, "dp"), "ctx", 1).reshape(-1, width)
    return half_a, half_b


def columns(pieces):
    return jnp.concatenate(list(pieces), axis=-1)


def as_rows(vector, width):
    rows = -(-vector.shape[0] // (16 * width)) * 16
    return jnp.pad(vector, (0, rows * width - vector.shape[0])).reshape(rows, width)


def tied(value, other):
    return lax.optimization_barrier((value, other))


def conv_taps_sum(taps_ref, rows_of):
    total = taps_ref[CONV : CONV + 1, :]
    for k in range(CONV):
        total = total + taps_ref[k : k + 1, :] * rows_of(k)
    return total


def prep_kernel(
    feed_ref, rim_ref, taps_ref, raw_ref, bias_ref, rate_ref,
    act_ref, dt_ref, cum_ref, cumt_ref, since_ref, local_ref,
    window, run,
):
    inner = local_ref.shape[0]

    @pl.when(pl.program_id(0) == 0)
    def _():
        window[:RIM, :] = rim_ref[...].astype(full)
        run[...] = jnp.zeros_like(run)
        local_ref[...] = jnp.zeros_like(local_ref)

    window[RIM:, :] = feed_ref[...].astype(full)
    pre = conv_taps_sum(taps_ref, lambda k: window[RIM - CONV + 1 + k : RIM - CONV + 1 + k + CHUNK, :])
    act = pre * jax.nn.sigmoid(pre)
    act_ref[...] = act
    window[:RIM, :] = window[CHUNK:, :]
    raw = raw_ref[...] + bias_ref[...]
    dt = jnp.maximum(raw, 0.0) + jnp.log1p(jnp.exp(-jnp.abs(raw)))
    row = lax.broadcasted_iota(jnp.int32, (CHUNK, CHUNK), 0)
    col = lax.broadcasted_iota(jnp.int32, (CHUNK, CHUNK), 1)
    cum = dot_nn((row >= col).astype(full), rate_ref[...] * dt, highest)
    dt_ref[...] = dt
    cum_ref[...] = cum
    cumt_ref[...] = cum.T[: cumt_ref.shape[0]]
    since_ref[...] = jnp.exp(run[0:1, :] + cum)
    end = cum[CHUNK - 1 : CHUNK, :]
    run[...] = run[...] + end
    weight = jnp.exp(end - cum) * dt
    shrink = jnp.exp(end)
    left = col < HEADDIM
    upper = row < HEADDIM
    b_low = act[:, inner : inner + STATE].astype(low)
    for pair in range(inner // LANES):
        h0, h1 = 2 * pair, 2 * pair + 1
        span = slice(pair * LANES, (pair + 1) * LANES)
        each = jnp.where(left, weight[:, h0 : h0 + 1], weight[:, h1 : h1 + 1])
        fresh = dot_tn((act[:, span] * each).astype(low), b_low)
        keep = jnp.where(upper, shrink[:, h0 : h0 + 1], shrink[:, h1 : h1 + 1])
        local_ref[span, :] = keep * local_ref[span, :] + fresh


def mixer_prep(feed, rim, taps, raw, bias, rate, heads):
    rows, channels = feed.shape
    inner = heads * HEADDIM
    lanes = pl.BlockSpec((CHUNK, LANES), lambda i: (i, 0))
    lane_row = pl.BlockSpec((1, LANES), lambda i: (0, 0))
    by_lane = jax.ShapeDtypeStruct((rows, LANES), full)
    return pl.pallas_call(
        prep_kernel,
        grid=(rows // CHUNK,),
        in_specs=[
            pl.BlockSpec((CHUNK, channels), lambda i: (i, 0)),
            pl.BlockSpec((RIM, channels), lambda i: (0, 0)),
            pl.BlockSpec((8, channels), lambda i: (0, 0)),
            lanes,
            lane_row,
            lane_row,
        ],
        out_specs=[
            pl.BlockSpec((CHUNK, channels), lambda i: (i, 0)),
            lanes,
            lanes,
            pl.BlockSpec((heads, CHUNK), lambda i: (0, i)),
            lanes,
            pl.BlockSpec((inner, STATE), lambda i: (0, 0)),
        ],
        out_shape=[
            jax.ShapeDtypeStruct((rows, channels), full),
            by_lane,
            by_lane,
            jax.ShapeDtypeStruct((heads, rows), full),
            by_lane,
            jax.ShapeDtypeStruct((inner, STATE), full),
        ],
        scratch_shapes=[pltpu.VMEM((CHUNK + RIM, channels), full), pltpu.VMEM((8, LANES), full)],
        compiler_params=pltpu.CompilerParams(
            dimension_semantics=("arbitrary",), vmem_limit_bytes=40 * 1024 * 1024
        ),
        cost_estimate=pl.CostEstimate(
            flops=rows * inner * 2 * STATE, bytes_accessed=rows * channels * 6, transcendentals=rows * channels
        ),
        name="mixer_prep",
    )(feed, rim, taps, raw, bias, rate)


def fwd_kernel(x_ref, bc_ref, dt_ref, cum_ref, cumt_ref, skip_ref, enter_ref, y_ref, start_ref, state):
    @pl.when(pl.program_id(0) == 0)
    def _():
        state[...] = enter_ref[...].astype(full)

    heads = cumt_ref.shape[0]
    start_ref[0] = state[...].astype(low)
    b_low = bc_ref[:, :STATE].astype(low)
    c_low = bc_ref[:, STATE:].astype(low)
    row = lax.broadcasted_iota(jnp.int32, (CHUNK, CHUNK), 0)
    col = lax.broadcasted_iota(jnp.int32, (CHUNK, CHUNK), 1)
    left = col < HEADDIM
    upper = row < HEADDIM
    masked = jnp.where(row >= col, dot_nt(c_low, b_low), 0.0)
    for pair in range(heads // 2):
        h0, h1 = 2 * pair, 2 * pair + 1
        span = slice(pair * LANES, (pair + 1) * LANES)
        cum0 = jnp.broadcast_to(cum_ref[:, h0 : h0 + 1], (CHUNK, CHUNK))
        cum1 = jnp.broadcast_to(cum_ref[:, h1 : h1 + 1], (CHUNK, CHUNK))
        w0 = jnp.exp(jnp.minimum(cum0 - cumt_ref[h0 : h0 + 1, :], 0.0)) * masked
        w1 = jnp.exp(jnp.minimum(cum1 - cumt_ref[h1 : h1 + 1, :], 0.0)) * masked
        weights = jnp.concatenate([w0.astype(low), w1.astype(low)], axis=1)
        x_pair = x_ref[:, span]
        u = x_pair * jnp.where(left, dt_ref[:, h0 : h0 + 1], dt_ref[:, h1 : h1 + 1])
        u_low = u.astype(low)
        zero = jnp.zeros_like(u_low)
        u_both = jnp.concatenate([jnp.where(left, u_low, zero), jnp.where(left, zero, u_low)], axis=0)
        cum_pair = jnp.where(left, cum0, cum1)
        s_pair = state[span, :]
        carried = jnp.exp(cum_pair) * dot_nt(c_low, s_pair.astype(low))
        y_ref[:, span] = dot_nn(weights, u_both) + carried + skip_ref[:, span] * x_pair
        end0 = cum_ref[CHUNK - 1 : CHUNK, h0 : h0 + 1]
        end1 = cum_ref[CHUNK - 1 : CHUNK, h1 : h1 + 1]
        ahead = jnp.exp(jnp.where(left, end0, end1) - cum_pair)
        fresh = dot_tn((u * ahead).astype(low), b_low)
        state[span, :] = jnp.exp(jnp.where(upper, end0, end1)) * s_pair + fresh


def bwd_kernel(
    x_ref, bc_ref, dt_ref, cum_ref, cumt_ref, skip_ref, dy_ref, start_ref, later_ref,
    feed_ref, before_ref, rim_ref, taps_ref, raw_ref, bias_ref, rate_ref,
    back_ref, first_ref, sums_ref, head_sums_ref,
    adjoint, dye, uw, xdu, dyi, udu, window, back,
):
    channels = feed_ref.shape[1]

    @pl.when(pl.program_id(0) == 0)
    def _():
        adjoint[...] = later_ref[...].astype(full)
        back[CHUNK:, :] = jnp.zeros((8, channels), full)
        sums_ref[...] = jnp.zeros_like(sums_ref)
        head_sums_ref[...] = jnp.zeros_like(head_sums_ref)

    at_start = pl.program_id(0) == pl.num_programs(0) - 1
    window[:RIM, :] = jnp.where(at_start, rim_ref[...].astype(full), before_ref[...].astype(full))
    window[RIM:, :] = feed_ref[...].astype(full)

    heads = cumt_ref.shape[0]
    inner = heads * HEADDIM
    b_low = bc_ref[:, :STATE].astype(low)
    c_low = bc_ref[:, STATE:].astype(low)
    row = lax.broadcasted_iota(jnp.int32, (CHUNK, CHUNK), 0)
    col = lax.broadcasted_iota(jnp.int32, (CHUNK, CHUNK), 1)
    left = col < HEADDIM
    causal = row >= col
    onward = (row <= col).astype(low)
    masked = jnp.where(causal, dot_nt(c_low, b_low), 0.0)
    d_affinity = jnp.zeros((CHUNK, CHUNK), full)
    dlog = jnp.zeros((CHUNK, LANES), full)
    for pair in range(heads // 2):
        h0, h1 = 2 * pair, 2 * pair + 1
        span = slice(pair * LANES, (pair + 1) * LANES)
        cum0 = jnp.broadcast_to(cum_ref[:, h0 : h0 + 1], (CHUNK, CHUNK))
        cum1 = jnp.broadcast_to(cum_ref[:, h1 : h1 + 1], (CHUNK, CHUNK))
        m0 = jnp.exp(jnp.minimum(cum0 - cumt_ref[h0 : h0 + 1, :], 0.0))
        m1 = jnp.exp(jnp.minimum(cum1 - cumt_ref[h1 : h1 + 1, :], 0.0))
        w0 = m0 * masked
        w1 = m1 * masked
        dt_pair = jnp.where(left, dt_ref[:, h0 : h0 + 1], dt_ref[:, h1 : h1 + 1])
        x_pair = x_ref[:, span]
        u = x_pair * dt_pair
        u_low = u.astype(low)
        dy_pair = dy_ref[:, span]
        dy_low = dy_pair.astype(low)
        zero = jnp.zeros_like(dy_low)
        dy_both = jnp.concatenate([jnp.where(left, dy_low, zero), jnp.where(left, zero, dy_low)], axis=0)
        dw = dot_nt(dy_both, u_low)
        dw0, dw1 = dw[:CHUNK], dw[CHUNK:]
        d_affinity = d_affinity + dw0 * m0 + dw1 * m1
        z_both = jnp.concatenate([(dw0 * w0).astype(low), (dw1 * w1).astype(low)], axis=1)
        reach = dot_nn(onward, z_both)
        k0 = jnp.sum(jnp.where(row > col, reach[:, :CHUNK], 0.0), axis=1, keepdims=True)
        k1 = jnp.sum(jnp.where(row > col, reach[:, CHUNK:], 0.0), axis=1, keepdims=True)
        dlog = jnp.where(col == h0, k0, jnp.where(col == h1, k1, dlog))
        w_both = jnp.concatenate([w0.astype(low), w1.astype(low)], axis=0)
        cum_pair = jnp.where(left, cum0, cum1)
        end0 = cum_ref[CHUNK - 1 : CHUNK, h0 : h0 + 1]
        end1 = cum_ref[CHUNK - 1 : CHUNK, h1 : h1 + 1]
        ahead = jnp.exp(jnp.where(left, end0, end1) - cum_pair)
        since = jnp.exp(cum_pair)
        du_state = ahead * dot_nt(b_low, adjoint[span, :].astype(low))
        du = dot_tn(w_both, dy_both) + du_state
        back[:CHUNK, span] = dt_pair * du + skip_ref[:, span] * dy_pair
        sums_ref[CONV + 1 : CONV + 2, span] += jnp.sum(x_pair * dy_pair, axis=0, keepdims=True)
        y_state = since * dot_nt(c_low, start_ref[0, span, :])
        xdu[:, span] = x_pair * du
        dyi[:, span] = dy_pair * y_state
        udu[:, span] = u * du_state
        dye[:, span] = (dy_pair * since).astype(low)
        uw[:, span] = (u * ahead).astype(low)
    inner_row = lax.broadcasted_iota(jnp.int32, (inner, LANES), 0)
    inner_col = lax.broadcasted_iota(jnp.int32, (inner, LANES), 1)
    pick = (inner_row // HEADDIM == inner_col).astype(full)
    ddt = dot_nn(xdu[...], pick, highest)
    by_state = dot_nn(dyi[...], pick, highest)
    by_later = dot_nn(udu[...], pick, highest)
    adjoint_now = adjoint[...]
    start_now = start_ref[0]
    both = adjoint_now * start_now.astype(full)
    over = dot_nn(dot_nt(jnp.ones((8, STATE), full), both, highest), pick, highest)
    ends = jnp.exp(cum_ref[CHUNK - 1 : CHUNK, :])
    dlog = dlog + over[0:1] * ends
    dlog = dlog + dot_nn((row <= col).astype(full), by_state, highest)
    dlog = dlog + dot_nn((row > col).astype(full), by_later, highest)
    rate = rate_ref[...]
    step = (ddt + rate * dlog) * jax.nn.sigmoid(raw_ref[...] + bias_ref[...])
    back_ref[:, channels:] = step.astype(low)
    head_sums_ref[0:1, :] += jnp.sum(step, axis=0, keepdims=True)
    head_sums_ref[1:2, :] += jnp.sum(dlog * rate * dt_ref[...], axis=0, keepdims=True)
    d_aff = jnp.where(causal, d_affinity, 0.0).astype(low)
    back[:CHUNK, inner : inner + STATE] = dot_tn(d_aff, c_low) + dot_nn(uw[...], adjoint_now.astype(low))
    back[:CHUNK, inner + STATE :] = dot_nn(d_aff, b_low) + dot_nn(dye[...], start_now)
    fresh = dot_tn(dye[...], c_low)
    for pair in range(heads // 2):
        h0, h1 = 2 * pair, 2 * pair + 1
        span = slice(pair * LANES, (pair + 1) * LANES)
        shrink = jnp.where(row < HEADDIM, ends[:, h0 : h0 + 1], ends[:, h1 : h1 + 1])
        adjoint[span, :] = shrink * adjoint_now[span, :] + fresh[span, :]
    for group in range(channels // LANES):
        span = slice(group * LANES, (group + 1) * LANES)
        taken = [
            window[RIM - CONV + 1 + k : RIM - CONV + 1 + k + CHUNK, span] for k in range(CONV)
        ]
        pre = taps_ref[CONV : CONV + 1, span]
        for k in range(CONV):
            pre = pre + taps_ref[k : k + 1, span] * taken[k]
        sig = jax.nn.sigmoid(pre)
        back_pre = back[:CHUNK, span] * (sig * (1.0 + pre * (1.0 - sig)))
        back[:CHUNK, span] = back_pre
        for k in range(CONV):
            sums_ref[k : k + 1, span] += jnp.sum(back_pre * taken[k], axis=0, keepdims=True)
        sums_ref[CONV : CONV + 1, span] += jnp.sum(back_pre, axis=0, keepdims=True)
        total = taps_ref[CONV - 1 : CONV, span] * back_pre
        for k in range(CONV - 1):
            total = total + taps_ref[k : k + 1, span] * back[CONV - 1 - k : CONV - 1 - k + CHUNK, span]
        back_ref[:, span] = total.astype(low)
    back[CHUNK:, :] = back[:8, :]

    @pl.when(at_start)
    def _():
        first_ref[...] = back[:8, :]


def ssm_forward(act, dt, cum, cum_t, skip_row, entering):
    rows = act.shape[0]
    heads = cum_t.shape[0]
    inner = heads * HEADDIM
    blocks = rows // CHUNK
    return pl.pallas_call(
        fwd_kernel,
        grid=(blocks,),
        in_specs=[
            pl.BlockSpec((CHUNK, inner), lambda i: (i, 0)),
            pl.BlockSpec((CHUNK, 2 * STATE), lambda i: (i, inner // (2 * STATE))),
            pl.BlockSpec((CHUNK, LANES), lambda i: (i, 0)),
            pl.BlockSpec((CHUNK, LANES), lambda i: (i, 0)),
            pl.BlockSpec((heads, CHUNK), lambda i: (0, i)),
            pl.BlockSpec((1, inner), lambda i: (0, 0)),
            pl.BlockSpec((inner, STATE), lambda i: (0, 0)),
        ],
        out_specs=[
            pl.BlockSpec((CHUNK, inner), lambda i: (i, 0)),
            pl.BlockSpec((1, inner, STATE), lambda i: (i, 0, 0)),
        ],
        out_shape=[
            jax.ShapeDtypeStruct((rows, inner), full),
            jax.ShapeDtypeStruct((blocks, inner, STATE), low),
        ],
        scratch_shapes=[pltpu.VMEM((inner, STATE), full)],
        compiler_params=pltpu.CompilerParams(
            dimension_semantics=("arbitrary",), vmem_limit_bytes=40 * 1024 * 1024
        ),
        cost_estimate=pl.CostEstimate(
            flops=rows * inner * 2 * 4 * STATE,
            bytes_accessed=rows * inner * 10,
            transcendentals=rows * heads * CHUNK * 2,
        ),
        name="ssm_forward",
    )(act, act, dt, cum, cum_t, skip_row, entering)


def ssm_backward(act, dt, cum, cum_t, skip_row, dy, starts, later, feed, rim, taps, raw, bias, rate):
    rows, channels = feed.shape
    lane_row = pl.BlockSpec((1, LANES), lambda i: (0, 0))
    per_block = CHUNK // RIM
    heads = cum_t.shape[0]
    inner = heads * HEADDIM
    blocks = rows // CHUNK
    last = blocks - 1
    return pl.pallas_call(
        bwd_kernel,
        grid=(blocks,),
        in_specs=[
            pl.BlockSpec((CHUNK, inner), lambda i: (last - i, 0)),
            pl.BlockSpec((CHUNK, 2 * STATE), lambda i: (last - i, inner // (2 * STATE))),
            pl.BlockSpec((CHUNK, LANES), lambda i: (last - i, 0)),
            pl.BlockSpec((CHUNK, LANES), lambda i: (last - i, 0)),
            pl.BlockSpec((heads, CHUNK), lambda i: (0, last - i)),
            pl.BlockSpec((1, inner), lambda i: (0, 0)),
            pl.BlockSpec((CHUNK, inner), lambda i: (last - i, 0)),
            pl.BlockSpec((1, inner, STATE), lambda i: (last - i, 0, 0)),
            pl.BlockSpec((inner, STATE), lambda i: (0, 0)),
            pl.BlockSpec((CHUNK, channels), lambda i: (last - i, 0)),
            pl.BlockSpec((RIM, channels), lambda i: (jnp.maximum((last - i) * per_block - 1, 0), 0)),
            pl.BlockSpec((RIM, channels), lambda i: (0, 0)),
            pl.BlockSpec((8, channels), lambda i: (0, 0)),
            pl.BlockSpec((CHUNK, LANES), lambda i: (last - i, 0)),
            lane_row,
            lane_row,
        ],
        out_specs=[
            pl.BlockSpec((CHUNK, channels + LANES), lambda i: (last - i, 0)),
            pl.BlockSpec((8, channels), lambda i: (0, 0)),
            pl.BlockSpec((8, channels), lambda i: (0, 0)),
            pl.BlockSpec((8, LANES), lambda i: (0, 0)),
        ],
        out_shape=[
            jax.ShapeDtypeStruct((rows, channels + LANES), low),
            jax.ShapeDtypeStruct((8, channels), full),
            jax.ShapeDtypeStruct((8, channels), full),
            jax.ShapeDtypeStruct((8, LANES), full),
        ],
        scratch_shapes=[
            pltpu.VMEM((inner, STATE), full),
            pltpu.VMEM((CHUNK, inner), low),
            pltpu.VMEM((CHUNK, inner), low),
            pltpu.VMEM((CHUNK, inner), full),
            pltpu.VMEM((CHUNK, inner), full),
            pltpu.VMEM((CHUNK, inner), full),
            pltpu.VMEM((CHUNK + RIM, channels), full),
            pltpu.VMEM((CHUNK + 8, channels), full),
        ],
        compiler_params=pltpu.CompilerParams(
            dimension_semantics=("arbitrary",), vmem_limit_bytes=40 * 1024 * 1024
        ),
        cost_estimate=pl.CostEstimate(
            flops=rows * inner * 2 * 16 * STATE,
            bytes_accessed=rows * inner * 16,
            transcendentals=rows * heads * CHUNK * 2,
        ),
        name="ssm_backward",
    )(act, act, dt, cum, cum_t, skip_row, dy, starts, later, feed, feed, rim, taps, raw, bias, rate)


def heads_to_channels(values):
    heads = values.shape[1]
    head = lax.broadcasted_iota(jnp.int32, (heads, heads * HEADDIM), 0)
    channel = lax.broadcasted_iota(jnp.int32, (heads, heads * HEADDIM), 1)
    return dot_nn(values, (channel // HEADDIM == head).astype(full), highest)


def silu_slope(value, sig):
    return sig * (1.0 + value * (1.0 - sig))


def layer_forward(hidden, valid, weights, params):
    gain, taps, step_bias, decay_log, skip, out_gain = params
    feed_weight, gate_weight, out_weight = weights
    rows, width = hidden.shape
    heads = step_bias.shape[0]
    inner = heads * HEADDIM
    channels = inner + 2 * STATE
    norm = lax.rsqrt(jnp.mean(hidden * hidden, axis=-1, keepdims=True) + epsilon)
    normed = (hidden * norm * gain).astype(low)
    feed_all = dot_nn(normed, feed_weight)
    feed = feed_all[:, :channels].astype(low)
    raw = feed_all[:, channels:]
    rim = shifted(feed[rows - RIM :], "ctx", 1)
    gate = dot_nn(normed, gate_weight)
    lanes = ((0, 0), (0, LANES - heads))
    bias = jnp.pad(step_bias[None], lanes)
    rate = jnp.pad(-jnp.exp(decay_log)[None], lanes)
    taps = jnp.pad(taps, ((0, 8 - CONV - 1), (0, 0)))
    act, dt, cum, cum_t, since, local_state = mixer_prep(feed, rim, taps, raw, bias, rate, heads)
    shrink = jnp.repeat(since[rows - 1, :heads], HEADDIM)[:, None]
    entering = chain(local_state, shrink, 1)
    skip_row = jnp.repeat(skip, HEADDIM)[None]
    scan = (act, dt, cum, cum_t, skip_row)
    conv = (feed, rim, taps, raw, bias, rate)
    ssm_out, starts = ssm_forward(*scan, entering)
    gated = ssm_out * (gate * jax.nn.sigmoid(gate))
    squares = jnp.sum(gated * gated, axis=-1)
    scaled = (gated * out_gain).astype(low)
    term = dot_nt(scaled, out_weight).astype(low)
    branch = term.astype(full) + swap_cores(term).astype(full)
    squares = squares + swap_cores(squares)
    out_norm = lax.rsqrt(squares / INNER + epsilon)[:, None]
    result = hidden + valid * out_norm * branch
    kept = (
        hidden, norm, normed, act, gate, since, shrink,
        scan, conv, starts, ssm_out, scaled, branch.astype(low), out_norm,
    )
    return result, kept


def chain(local_state, shrink, steps):
    entering = shifted(local_state.astype(low), "ctx", steps)
    for _ in range(lax.axis_size("ctx") - 2):
        leaving = shrink * entering.astype(full) + local_state
        entering = shifted(leaving.astype(low), "ctx", steps)
    return entering


def layer_backward(incoming, valid, weights, params, kept, pending=None):
    gain, taps, step_bias, decay_log, skip, out_gain = params
    feed_weight, gate_weight, out_weight = weights
    (
        hidden, norm, normed, act, gate, since, shrink,
        scan, conv, starts, ssm_out, scaled, branch, out_norm,
    ) = kept
    rows, width = hidden.shape
    heads = step_bias.shape[0]
    inner = heads * HEADDIM
    channels = inner + 2 * STATE
    back_branch = (valid * incoming).astype(low)
    back_normed = dot_nn(back_branch, out_weight)
    back_wide = back_branch.astype(full)
    grad_out = dot_tn((back_wide * out_norm).astype(low), scaled).astype(low)
    along = jnp.sum(back_wide * branch.astype(full), axis=-1, keepdims=True)
    sig = jax.nn.sigmoid(gate)
    silu = gate * sig
    gated = ssm_out * silu
    grad_out_gain = jnp.sum(back_normed * gated * out_norm, axis=0)
    back_gated = out_norm * out_gain * back_normed - gated * (out_norm**3 * along / INNER)
    back_ssm = back_gated * silu
    back_gate = (back_gated * ssm_out * silu_slope(gate, sig)).astype(low)
    grad_gate = dot_tn(normed, back_gate).astype(low)
    weighted = (back_ssm * heads_to_channels(since[:, :heads])).astype(low)
    local_adjoint = dot_tn(weighted, act[:, inner + STATE :].astype(low))
    later = chain(local_adjoint, shrink, -1)
    early = None
    if pending is not None:
        early = Reduction([grad_gate], [grad_out])
        back_ssm, pending.sums = tied(back_ssm, pending.sums)
        pending.second()
        early.first()
    back_all, first_rows, sums, head_sums = ssm_backward(*scan, back_ssm, starts, later, *conv)
    following = shifted(first_rows, "ctx", -1)
    taps = conv[2]
    edge = sum(
        jnp.pad(taps[k] * following[: CONV - 1 - k], ((RIM - CONV + 1 + k, 0), (0, LANES))) for k in range(CONV - 1)
    )
    back_all = lax.dynamic_update_slice_in_dim(
        back_all, (back_all[rows - RIM :].astype(full) + edge).astype(low), rows - RIM, 0
    )
    if pending is not None:
        back_all, (pending.sums, early.sums) = tied(back_all, (pending.sums, early.sums))
        pending.sums = scatter_sum(pending.blocks(pending.sums), "tp")
        early.second()
    grad_skip = jnp.sum(sums[CONV + 1, :inner].reshape(heads, HEADDIM), axis=1)
    grad_step_bias, grad_decay = head_sums[0, :heads], head_sums[1, :heads]
    grad_taps = sums[: CONV + 1]
    term = (dot_nt(back_all, feed_weight) + dot_nt(back_gate, gate_weight)).astype(low)
    if pending is not None:
        term, (pending.sums, early.sums) = tied(term, (pending.sums, early.sums))
        early.sums = scatter_sum([by_tp(early.sums[0]), by_tp(early.sums[1])], "tp")
    back_in = term.astype(full) + swap_cores(term).astype(full)
    grad_feed = dot_tn(normed, back_all).astype(low)
    grad_gain = jnp.sum(back_in * hidden * norm, axis=0)
    scaled_in = back_in * gain
    along_in = jnp.sum(scaled_in * hidden, axis=-1, keepdims=True)
    delta = norm * scaled_in - hidden * (norm**3 * along_in / width)
    small = jnp.concatenate(
        [
            grad_taps[:, :inner].reshape(-1), grad_taps[:, inner:].reshape(-1),
            grad_out_gain, grad_step_bias, grad_decay, grad_skip, grad_gain,
        ]
    )
    return delta, (grad_feed, grad_gate, grad_out), small, early


def by_tp(value):
    return jnp.moveaxis(value.reshape(value.shape[0], lax.axis_size("tp"), -1), 1, 0)


class Reduction:
    def __init__(self, half_a, half_b):
        ndp, nctx = lax.axis_size("dp"), lax.axis_size("ctx")
        rows = half_a[0].shape[0] // (ndp * nctx)
        self.halves = [
            [part.reshape(ndp, nctx, rows, part.shape[1]) for part in half] for half in (half_a, half_b)
        ]

    def first(self):
        self.sums = (
            scatter_sum(self.halves[0], "ctx", 1).astype(low),
            scatter_sum(self.halves[1], "dp", 0).astype(low),
        )

    def second(self):
        self.sums = (
            scatter_sum([self.sums[0]], "dp").astype(low),
            scatter_sum([self.sums[1]], "ctx").astype(low),
        )


def feed_blocks(feed, inner):
    rest = feed[:, inner:]
    return [by_tp(feed[:, :inner]), jnp.broadcast_to(rest, (lax.axis_size("tp"),) + rest.shape)]


def on_device(
    acts,
    cotangent,
    lengths,
    norm_gain,
    proj_gate_x,
    proj_state,
    proj_step,
    conv_inner,
    conv_state,
    step_bias,
    decay_log,
    skip_weight,
    out_gain,
    proj_out,
):
    micro_count, rows, width = (acts.shape[0], acts.shape[2], acts.shape[3])
    tp_count = lax.axis_size("tp")
    core = lax.axis_index("section")
    lane = lax.axis_index("tp")
    first = core == 0
    own_rows = proj_gate_x.shape[1]
    half = proj_gate_x.shape[3] // 2
    step_half = proj_step.shape[2] // 2
    heads = step_half * tp_count
    inner = half * tp_count
    quarter = 2 * STATE // tp_count
    wide = quarter

    state_part = lax.dynamic_slice_in_dim(proj_state[0], lane * quarter, quarter, 1)

    def pack(c):
        step = proj_step[0, :, c * step_half : (c + 1) * step_half]
        tail = jnp.pad(columns([step, norm_gain[0][:, None]]), ((0, 0), (0, wide - step_half - 1)))
        return columns(
            [
                proj_gate_x[0, :, 1, c * half : (c + 1) * half],
                state_part,
                tail,
                proj_gate_x[0, :, 0, c * half : (c + 1) * half],
                proj_out[0, c * half : (c + 1) * half].T,
            ]
        )

    def pack_small(c):
        vector = jnp.concatenate(
            [
                conv_inner[0, :, c * half : (c + 1) * half].reshape(-1),
                out_gain[0, c * half : (c + 1) * half],
                step_bias[0, c * step_half : (c + 1) * step_half],
                decay_log[0, c * step_half : (c + 1) * step_half],
                skip_weight[0, c * step_half : (c + 1) * step_half],
                conv_state[0].reshape(-1),
            ]
        )
        parts = []
        for _ in range(3):
            part = lax.reduce_precision(vector, 8, 7)
            parts.append(part.astype(low))
            vector = vector - part
        return as_rows(jnp.concatenate(parts), cut)

    def both_layers(make):
        zero, one = make(0), make(1)
        keep = jnp.where(first, zero, one)
        came = swap_cores(jnp.where(first, one, zero))
        return jnp.where(first, keep, came), jnp.where(first, came, keep)

    def layer_params(rows_of_small):
        size = (CONV + 1) * half + half + 3 * step_half + (CONV + 1) * 2 * STATE
        three = rows_of_small.reshape(tp_count, -1)[:, : 3 * size].reshape(tp_count, 3, size)
        part = jnp.sum(three.astype(full), axis=1)
        at = (CONV + 1) * half
        taps_inner = jnp.moveaxis(part[:, :at].reshape(tp_count, CONV + 1, half), 0, 1)
        gains = part[:, at : at + half].reshape(-1)
        at += half
        scalars = []
        for _ in range(3):
            scalars.append(part[:, at : at + step_half].reshape(-1))
            at += step_half
        taps_state = part[0, at:].reshape(CONV + 1, 2 * STATE)
        taps = columns([taps_inner.reshape(CONV + 1, inner), taps_state])
        return taps, scalars[0], scalars[1], scalars[2], gains

    cut = half + quarter + wide
    middle = tp_count // 2

    def gather_item(part, sections):
        def side(pieces):
            parts, at = [], 0
            for size in sections:
                parts.append(columns(pieces[..., at : at + size]))
                at += size
            return columns(parts)

        half_a, half_b = gather_rows(side(part[:middle]), side(part[middle:]))
        result, at = [], 0
        for size in sections:
            result.append((half_a[:, at : at + middle * size], half_b[:, at : at + middle * size]))
            at += middle * size
        return result

    def feed_weights(parts):
        tails = [side.reshape(-1, middle, wide)[:, :, :step_half].reshape(-1, heads // 2) for side in parts[2]]
        gain = parts[2][0][:, step_half].astype(full)
        steps = jnp.pad(columns(tails), ((0, 0), (0, LANES - heads)))
        return columns(parts[0] + parts[1] + (steps,)), gain

    smalls = both_layers(pack_small)
    packs = both_layers(pack)
    feed_sections, pair_sections = (half, quarter, wide), (half, half)
    along_feed = line_gather(jnp.concatenate([packs[0][:, :cut], smalls[0]], axis=0), "tp")
    pair_pack, along_feed = tied(packs[0][:, cut:], along_feed)
    along_pair = line_gather(pair_pack, "tp")
    feed_parts = gather_item(along_feed[:, :own_rows], feed_sections)
    last_pack, feed_parts = tied(packs[1], feed_parts)
    small_pad = jnp.pad(smalls[1], ((0, 0), (0, last_pack.shape[1] - cut)))
    along_last = line_gather(jnp.concatenate([last_pack, small_pad], axis=0), "tp")
    pair_parts = gather_item(along_pair, pair_sections)
    along_last, pair_parts = tied(along_last, pair_parts)
    last_parts = gather_item(along_last[:, :own_rows, :cut], feed_sections)
    along_last, last_parts = tied(along_last, last_parts)
    last_parts += gather_item(along_last[:, :own_rows, cut:], pair_sections)
    feed_first, gain_first = feed_weights(feed_parts)
    feed_last, gain_last = feed_weights(last_parts[:3])
    weights = [
        (feed_first, columns(pair_parts[0]), columns(pair_parts[1])),
        (feed_last, columns(last_parts[3]), columns(last_parts[4])),
    ]
    params = [
        (gain_first,) + layer_params(along_feed[:, own_rows:]),
        (gain_last,) + layer_params(along_last[:, own_rows:, :cut]),
    ]

    places = lax.axis_index("ctx") * rows + jnp.arange(rows, dtype=jnp.int32)
    length = lax.dynamic_index_in_dim(lengths[:, 0], lane, 0, False)
    valid = (places < length).astype(full)[:, None]
    hidden = lax.dynamic_index_in_dim(acts[:, 0], lane, 0, False).astype(full)
    out_grad = lax.dynamic_index_in_dim(cotangent[:, 0], lane, 0, False)

    result_first, kept_first = layer_forward(hidden, valid, weights[0], params[0])
    low_first = result_first.astype(low)
    result_last, kept_last = layer_forward(low_first.astype(full), valid, weights[1], params[1])
    own_result = jnp.where(first, low_first, result_last.astype(low))
    quarter_rows = rows // tp_count
    section_out = spread_rows(own_result.reshape(tp_count, quarter_rows, width), (0, 1))

    delta_last, grads_last, small_last, _ = layer_backward(
        out_grad, valid, weights[1], params[1], kept_last
    )
    feed_last, gate_last, out_last = grads_last
    share = inner // 4
    last = Reduction([feed_last, out_last[:, :share]], [gate_last, out_last[:, share:]])

    def last_blocks(sums):
        at = feed_last.shape[1]
        out_part = columns([sums[0][:, at:], sums[1][:, inner:]])
        return [by_tp(sums[1][:, :inner]), by_tp(out_part)] + feed_blocks(sums[0][:, :at], inner)

    last.blocks = last_blocks
    last.first()
    spread_last = spread_rows(delta_last.astype(low).reshape(tp_count, quarter_rows, width), (1,))
    incoming = (out_grad + delta_last).astype(low).astype(full)
    delta_first, grads_first, small_first, early = layer_backward(
        incoming, valid, weights[0], params[0], kept_first, last
    )
    feed_first = grads_first[0]
    grad_first = (incoming + delta_first).astype(low)
    feed_first, grad_first = tied(feed_first, grad_first)
    part = inner // 2 + LANES
    feed = Reduction([feed_first[:, :part]], [feed_first[:, part:]])
    feed.first()
    small = jnp.stack([small_first, small_last])
    spread_first = spread_rows(grad_first.reshape(tp_count, quarter_rows, width), (0,))
    small = all_sum(all_sum(small, "ctx"), "dp")
    feed.second()
    payload = columns(feed_blocks(columns(feed.sums), inner))
    extra = as_rows(small.astype(low).reshape(-1), payload.shape[2])
    payload = jnp.concatenate([payload, jnp.broadcast_to(extra, (tp_count,) + extra.shape)], axis=1)
    feed_sums = scatter_sum([payload], "tp")
    own_cotangent = lax.dynamic_slice_in_dim(
        cotangent[:, 0], lane * quarter_rows, quarter_rows, 1
    )
    input_grad = jnp.where(
        first, spread_first.astype(full), own_cotangent + spread_last.astype(full)
    )

    pair_width = 2 * half
    pair_keep = jnp.where(first, early.sums, last.sums[:, :pair_width])
    pair_came = swap_cores(jnp.where(first, last.sums[:, :pair_width], early.sums))
    size = small_first.shape[0]
    small_sums = feed_sums[own_rows:].reshape(-1)[: 2 * size].reshape(2, size)
    sums_last = last.sums[:, pair_width:]
    total_width = sums_last.shape[1]
    joined = [
        jnp.concatenate([sums, as_rows(vector, total_width)])
        for sums, vector in zip((feed_sums[:own_rows], sums_last), small_sums)
    ]
    keep = jnp.where(first, joined[0], joined[1])
    came = swap_cores(jnp.where(first, joined[1], joined[0]))
    small_keep = keep[own_rows:].reshape(-1)[:size]
    small_came = came[own_rows:].reshape(-1)[:size]
    keep, came = keep[:own_rows], came[:own_rows]

    def halves(kept_part, came_part, axis):
        zero = jnp.where(first, kept_part, came_part)
        one = jnp.where(first, came_part, kept_part)
        return jnp.concatenate([zero, one], axis=axis)

    def own_lane(value, shape, axis):
        return lax.dynamic_index_in_dim(value.reshape(shape), lane, axis, False)

    grad_gate = halves(pair_keep[:, :half], pair_came[:, :half], 1)
    grad_out = halves(pair_keep[:, half:].T, pair_came[:, half:].T, 0)
    at = 0
    grad_x = halves(keep[:, at : at + half], came[:, at : at + half], 1)
    at += half
    grad_state = keep[:, at : at + 2 * STATE] + came[:, at : at + 2 * STATE]
    at += 2 * STATE + lane * step_half
    grad_step = halves(
        lax.dynamic_slice_in_dim(keep, at, step_half, 1), lax.dynamic_slice_in_dim(came, at, step_half, 1), 1
    )
    grad_gate_x = jnp.stack([grad_gate, grad_x], axis=1)

    at = (CONV + 1) * inner
    taps_shape = (CONV + 1, tp_count, half)
    grad_conv_inner = halves(
        own_lane(small_keep[:at], taps_shape, 1), own_lane(small_came[:at], taps_shape, 1), 1
    )
    end = at + (CONV + 1) * 2 * STATE
    grad_conv_state = (small_keep[at:end] + small_came[at:end]).reshape(CONV + 1, 2 * STATE)
    at = end
    vectors = []
    for size in (inner, heads, heads, heads):
        shape = (tp_count, size // tp_count)
        vectors.append(
            halves(
                own_lane(small_keep[at : at + size], shape, 0),
                own_lane(small_came[at : at + size], shape, 0),
                0,
            )
        )
        at += size
    owner = lax.axis_index("dp") * lax.axis_size("ctx") + lax.axis_index("ctx")
    grad_norm_gain = lax.dynamic_slice_in_dim(small_keep[at:], owner * own_rows, own_rows, 0)
    return (
        section_out[None, :, None],
        input_grad[None, :, None],
        grad_norm_gain[None],
        grad_gate_x[None],
        grad_state[None],
        grad_step[None],
        grad_conv_inner[None],
        grad_conv_state[None],
        vectors[1][None],
        vectors[2][None],
        vectors[3][None],
        vectors[0][None],
        grad_out[None],
    )


def solution(mesh):
    placed = (
        P(None, "dp", "ctx", None),
        P(None, "dp", "ctx", None),
        P(None, "dp"),
        P("section", ("dp", "ctx")),
        P("section", ("dp", "ctx"), None, "tp"),
        P("section", ("dp", "ctx"), None),
        P("section", ("dp", "ctx"), "tp"),
        P("section", None, "tp"),
        P("section", None, None),
        P("section", "tp"),
        P("section", "tp"),
        P("section", "tp"),
        P("section", "tp"),
        P("section", "tp", ("dp", "ctx")),
    )
    return jax.shard_map(
        on_device,
        mesh=mesh,
        in_specs=placed,
        out_specs=(
            P("section", None, "dp", ("ctx", "tp"), None),
            P("section", None, "dp", ("ctx", "tp"), None),
            P("section", ("dp", "ctx")),
            P("section", ("dp", "ctx"), None, "tp"),
            P("section", ("dp", "ctx"), None),
            P("section", ("dp", "ctx"), "tp"),
            P("section", None, "tp"),
            P("section", None, None),
            P("section", "tp"),
            P("section", "tp"),
            P("section", "tp"),
            P("section", "tp"),
            P("section", "tp", ("dp", "ctx")),
        ),
        check_vma=False,
    )
```

```python
import functools

import jax
import jax.numpy as jnp
from jax import lax
from jax.experimental import pallas as pl
from jax.experimental.pallas import tpu as pltpu
from jax.sharding import PartitionSpec as P

HEADDIM = 64
STATE = 128
INNER = 2048
CONV = 4
CHUNK = 128
LANES = 128
RIM = 16

highest = lax.Precision.HIGHEST
epsilon = 1e-05
low = jnp.bfloat16
full = jnp.float32


def dot_nn(a, b, precision=None):
    return lax.dot_general(
        a, b, (((1,), (0,)), ((), ())), precision=precision, preferred_element_type=full
    )


def dot_nt(a, b, precision=None):
    return lax.dot_general(
        a, b, (((1,), (1,)), ((), ())), precision=precision, preferred_element_type=full
    )


def dot_tn(a, b, precision=None):
    return lax.dot_general(
        a, b, (((0,), (0,)), ((), ())), precision=precision, preferred_element_type=full
    )


def shifted(value, axis, steps):
    count = lax.axis_size(axis)
    first, last = (max(0, -steps), min(count, count - steps))
    return lax.ppermute(value, axis, [(source, source + steps) for source in range(first, last)])


def rotated(value, axis, steps):
    count = lax.axis_size(axis)
    return lax.ppermute(value, axis, [(i, (i + steps) % count) for i in range(count)])


def line_gather(value, axis, dim=0):
    count = lax.axis_size(axis)
    place = lax.axis_index(axis)
    if count == 1:
        return jnp.expand_dims(value, dim)
    if count == 2:
        other = rotated(value, axis, 1)
        first = place == 0
        return jnp.stack([jnp.where(first, value, other), jnp.where(first, other, value)], axis=dim)
    up = down = value
    before, after = [], []
    for _ in range(1, count):
        up = shifted(up, axis, 1)
        down = shifted(down, axis, -1)
        before.insert(0, up)
        after.append(down)
    line = jnp.stack(before + [value] + after, axis=dim)
    return lax.dynamic_slice_in_dim(line, count - 1 - place, count, dim)


def scatter_sum(parts, axis, dim=0):
    count = lax.axis_size(axis)
    place = lax.axis_index(axis)

    def pick(at):
        return columns(lax.dynamic_index_in_dim(part, at, dim, False) for part in parts)

    total = pick(place).astype(full)
    for steps in range(1, count):
        total = total + rotated(pick((place + steps) % count), axis, steps).astype(full)
    return total


def all_sum(value, axis):
    total = value
    for steps in range(1, lax.axis_size(axis)):
        total = total + rotated(value, axis, steps)
    return total


def swap_cores(value):
    return lax.ppermute(value, "section", [(0, 1), (1, 0)])


def spread_rows(value, pairs_of):
    count = lax.axis_size("tp")
    place = lax.axis_index("tp")
    result = jnp.zeros_like(value)
    own = lax.dynamic_index_in_dim(value, place, 0, False)
    result = lax.dynamic_update_index_in_dim(result, own, place, 0)
    for steps in range(1, count):
        block = lax.dynamic_index_in_dim(value, (place + steps) % count, 0, False)
        pairs = [
            (core * count + i, core * count + (i + steps) % count)
            for core in pairs_of
            for i in range(count)
        ]
        arrived = lax.ppermute(block, ("section", "tp"), pairs)
        result = lax.dynamic_update_index_in_dim(result, arrived, (place - steps) % count, 0)
    return result


def gather_rows(early, late):
    width = early.shape[-1]
    half_a = line_gather(line_gather(early, "ctx"), "dp").reshape(-1, width)
    half_b = line_gather(line_gather(late, "dp"), "ctx", 1).reshape(-1, width)
    return half_a, half_b


def columns(pieces):
    return jnp.concatenate(list(pieces), axis=-1)


def as_rows(vector, width):
    rows = -(-vector.shape[0] // (16 * width)) * 16
    return jnp.pad(vector, (0, rows * width - vector.shape[0])).reshape(rows, width)


def tied(value, other):
    return lax.optimization_barrier((value, other))


def conv_taps_sum(taps_ref, rows_of):
    total = taps_ref[CONV : CONV + 1, :]
    for k in range(CONV):
        total = total + taps_ref[k : k + 1, :] * rows_of(k)
    return total


def prep_kernel(
    feed_ref, rim_ref, taps_ref, raw_ref, bias_ref, rate_ref,
    act_ref, dt_ref, cum_ref, cumt_ref, since_ref, local_ref,
    window, run,
):
    inner = local_ref.shape[0]

    @pl.when(pl.program_id(0) == 0)
    def _():
        window[:RIM, :] = rim_ref[...].astype(full)
        run[...] = jnp.zeros_like(run)
        local_ref[...] = jnp.zeros_like(local_ref)

    window[RIM:, :] = feed_ref[...].astype(full)
    pre = conv_taps_sum(taps_ref, lambda k: window[RIM - CONV + 1 + k : RIM - CONV + 1 + k + CHUNK, :])
    act = pre * jax.nn.sigmoid(pre)
    act_ref[...] = act
    window[:RIM, :] = window[CHUNK:, :]
    raw = raw_ref[...] + bias_ref[...]
    dt = jnp.maximum(raw, 0.0) + jnp.log1p(jnp.exp(-jnp.abs(raw)))
    row = lax.broadcasted_iota(jnp.int32, (CHUNK, CHUNK), 0)
    col = lax.broadcasted_iota(jnp.int32, (CHUNK, CHUNK), 1)
    cum = dot_nn((row >= col).astype(full), rate_ref[...] * dt, highest)
    dt_ref[...] = dt
    cum_ref[...] = cum
    cumt_ref[...] = cum.T[: cumt_ref.shape[0]]
    since_ref[...] = jnp.exp(run[0:1, :] + cum)
    end = cum[CHUNK - 1 : CHUNK, :]
    run[...] = run[...] + end
    weight = jnp.exp(end - cum) * dt
    shrink = jnp.exp(end)
    left = col < HEADDIM
    upper = row < HEADDIM
    b_low = act[:, inner : inner + STATE].astype(low)
    for pair in range(inner // LANES):
        h0, h1 = 2 * pair, 2 * pair + 1
        span = slice(pair * LANES, (pair + 1) * LANES)
        each = jnp.where(left, weight[:, h0 : h0 + 1], weight[:, h1 : h1 + 1])
        fresh = dot_tn((act[:, span] * each).astype(low), b_low)
        keep = jnp.where(upper, shrink[:, h0 : h0 + 1], shrink[:, h1 : h1 + 1])
        local_ref[span, :] = keep * local_ref[span, :] + fresh


def mixer_prep(feed, rim, taps, raw, bias, rate, heads):
    rows, channels = feed.shape
    inner = heads * HEADDIM
    lanes = pl.BlockSpec((CHUNK, LANES), lambda i: (i, 0))
    lane_row = pl.BlockSpec((1, LANES), lambda i: (0, 0))
    by_lane = jax.ShapeDtypeStruct((rows, LANES), full)
    return pl.pallas_call(
        prep_kernel,
        grid=(rows // CHUNK,),
        in_specs=[
            pl.BlockSpec((CHUNK, channels), lambda i: (i, 0)),
            pl.BlockSpec((RIM, channels), lambda i: (0, 0)),
            pl.BlockSpec((8, channels), lambda i: (0, 0)),
            lanes,
            lane_row,
            lane_row,
        ],
        out_specs=[
            pl.BlockSpec((CHUNK, channels), lambda i: (i, 0)),
            lanes,
            lanes,
            pl.BlockSpec((heads, CHUNK), lambda i: (0, i)),
            lanes,
            pl.BlockSpec((inner, STATE), lambda i: (0, 0)),
        ],
        out_shape=[
            jax.ShapeDtypeStruct((rows, channels), full),
            by_lane,
            by_lane,
            jax.ShapeDtypeStruct((heads, rows), full),
            by_lane,
            jax.ShapeDtypeStruct((inner, STATE), full),
        ],
        scratch_shapes=[pltpu.VMEM((CHUNK + RIM, channels), full), pltpu.VMEM((8, LANES), full)],
        compiler_params=pltpu.CompilerParams(
            dimension_semantics=("arbitrary",), vmem_limit_bytes=40 * 1024 * 1024
        ),
        cost_estimate=pl.CostEstimate(
            flops=rows * inner * 2 * STATE, bytes_accessed=rows * channels * 6, transcendentals=rows * channels
        ),
        name="mixer_prep",
    )(feed, rim, taps, raw, bias, rate)


def fwd_kernel(x_ref, bc_ref, dt_ref, cum_ref, cumt_ref, skip_ref, enter_ref, y_ref, start_ref, state):
    @pl.when(pl.program_id(0) == 0)
    def _():
        state[...] = enter_ref[...].astype(full)

    heads = cumt_ref.shape[0]
    start_ref[0] = state[...].astype(low)
    b_low = bc_ref[:, :STATE].astype(low)
    c_low = bc_ref[:, STATE:].astype(low)
    row = lax.broadcasted_iota(jnp.int32, (CHUNK, CHUNK), 0)
    col = lax.broadcasted_iota(jnp.int32, (CHUNK, CHUNK), 1)
    left = col < HEADDIM
    upper = row < HEADDIM
    masked = jnp.where(row >= col, dot_nt(c_low, b_low), 0.0)
    for pair in range(heads // 2):
        h0, h1 = 2 * pair, 2 * pair + 1
        span = slice(pair * LANES, (pair + 1) * LANES)
        cum0 = jnp.broadcast_to(cum_ref[:, h0 : h0 + 1], (CHUNK, CHUNK))
        cum1 = jnp.broadcast_to(cum_ref[:, h1 : h1 + 1], (CHUNK, CHUNK))
        w0 = jnp.exp(jnp.minimum(cum0 - cumt_ref[h0 : h0 + 1, :], 0.0)) * masked
        w1 = jnp.exp(jnp.minimum(cum1 - cumt_ref[h1 : h1 + 1, :], 0.0)) * masked
        weights = jnp.concatenate([w0.astype(low), w1.astype(low)], axis=1)
        x_pair = x_ref[:, span]
        u = x_pair * jnp.where(left, dt_ref[:, h0 : h0 + 1], dt_ref[:, h1 : h1 + 1])
        u_low = u.astype(low)
        zero = jnp.zeros_like(u_low)
        u_both = jnp.concatenate([jnp.where(left, u_low, zero), jnp.where(left, zero, u_low)], axis=0)
        cum_pair = jnp.where(left, cum0, cum1)
        s_pair = state[span, :]
        carried = jnp.exp(cum_pair) * dot_nt(c_low, s_pair.astype(low))
        y_ref[:, span] = dot_nn(weights, u_both) + carried + skip_ref[:, span] * x_pair
        end0 = cum_ref[CHUNK - 1 : CHUNK, h0 : h0 + 1]
        end1 = cum_ref[CHUNK - 1 : CHUNK, h1 : h1 + 1]
        ahead = jnp.exp(jnp.where(left, end0, end1) - cum_pair)
        fresh = dot_tn((u * ahead).astype(low), b_low)
        state[span, :] = jnp.exp(jnp.where(upper, end0, end1)) * s_pair + fresh


def bwd_kernel(
    x_ref, bc_ref, dt_ref, cum_ref, cumt_ref, skip_ref, dy_ref, start_ref, later_ref,
    feed_ref, before_ref, rim_ref, taps_ref, raw_ref, bias_ref, rate_ref, pick_ref,
    back_ref, first_ref, sums_ref, head_sums_ref,
    adjoint, dye, uw, xdu, dyi, udu, window, back,
):
    channels = feed_ref.shape[1]

    @pl.when(pl.program_id(0) == 0)
    def _():
        adjoint[...] = later_ref[...].astype(full)
        back[CHUNK:, :] = jnp.zeros((8, channels), full)
        sums_ref[...] = jnp.zeros_like(sums_ref)
        head_sums_ref[...] = jnp.zeros_like(head_sums_ref)

    at_start = pl.program_id(0) == pl.num_programs(0) - 1
    window[:RIM, :] = jnp.where(at_start, rim_ref[...].astype(full), before_ref[...].astype(full))
    window[RIM:, :] = feed_ref[...].astype(full)

    heads = cumt_ref.shape[0]
    inner = heads * HEADDIM
    b_low = bc_ref[:, :STATE].astype(low)
    c_low = bc_ref[:, STATE:].astype(low)
    row = lax.broadcasted_iota(jnp.int32, (CHUNK, CHUNK), 0)
    col = lax.broadcasted_iota(jnp.int32, (CHUNK, CHUNK), 1)
    left = col < HEADDIM
    causal = row >= col
    onward = (row <= col).astype(low)
    masked = jnp.where(causal, dot_nt(c_low, b_low), 0.0)
    d_affinity = jnp.zeros((CHUNK, CHUNK), full)
    dlog = jnp.zeros((CHUNK, LANES), full)
    for pair in range(heads // 2):
        h0, h1 = 2 * pair, 2 * pair + 1
        span = slice(pair * LANES, (pair + 1) * LANES)
        cum0 = jnp.broadcast_to(cum_ref[:, h0 : h0 + 1], (CHUNK, CHUNK))
        cum1 = jnp.broadcast_to(cum_ref[:, h1 : h1 + 1], (CHUNK, CHUNK))
        m0 = jnp.exp(jnp.minimum(cum0 - cumt_ref[h0 : h0 + 1, :], 0.0))
        m1 = jnp.exp(jnp.minimum(cum1 - cumt_ref[h1 : h1 + 1, :], 0.0))
        w0 = m0 * masked
        w1 = m1 * masked
        dt_pair = jnp.where(left, dt_ref[:, h0 : h0 + 1], dt_ref[:, h1 : h1 + 1])
        x_pair = x_ref[:, span]
        u = x_pair * dt_pair
        u_low = u.astype(low)
        dy_pair = dy_ref[:, span]
        dy_low = dy_pair.astype(low)
        zero = jnp.zeros_like(dy_low)
        dy_both = jnp.concatenate([jnp.where(left, dy_low, zero), jnp.where(left, zero, dy_low)], axis=0)
        dw = dot_nt(dy_both, u_low)
        dw0, dw1 = dw[:CHUNK], dw[CHUNK:]
        d_affinity = d_affinity + dw0 * m0 + dw1 * m1
        z_both = jnp.concatenate([(dw0 * w0).astype(low), (dw1 * w1).astype(low)], axis=1)
        reach = dot_nn(onward, z_both)
        k0 = jnp.sum(jnp.where(row > col, reach[:, :CHUNK], 0.0), axis=1, keepdims=True)
        k1 = jnp.sum(jnp.where(row > col, reach[:, CHUNK:], 0.0), axis=1, keepdims=True)
        dlog = jnp.where(col == h0, k0, jnp.where(col == h1, k1, dlog))
        w_both = jnp.concatenate([w0.astype(low), w1.astype(low)], axis=0)
        cum_pair = jnp.where(left, cum0, cum1)
        end0 = cum_ref[CHUNK - 1 : CHUNK, h0 : h0 + 1]
        end1 = cum_ref[CHUNK - 1 : CHUNK, h1 : h1 + 1]
        ahead = jnp.exp(jnp.where(left, end0, end1) - cum_pair)
        since = jnp.exp(cum_pair)
        du_state = ahead * dot_nt(b_low, adjoint[span, :].astype(low))
        du = dot_tn(w_both, dy_both) + du_state
        back[:CHUNK, span] = dt_pair * du + skip_ref[:, span] * dy_pair
        sums_ref[CONV + 1 : CONV + 2, span] += jnp.sum(x_pair * dy_pair, axis=0, keepdims=True)
        y_state = since * dot_nt(c_low, start_ref[0, span, :])
        xdu[:, span] = (x_pair * du).astype(low)
        dyi[:, span] = (dy_pair * y_state).astype(low)
        udu[:, span] = (u * du_state).astype(low)
        dye[:, span] = (dy_pair * since).astype(low)
        uw[:, span] = (u * ahead).astype(low)
    pick = pick_ref[...]
    ddt = dot_nn(xdu[...], pick)
    by_state = dot_nn(dyi[...], pick)
    by_later = dot_nn(udu[...], pick)
    adjoint_now = adjoint[...]
    start_now = start_ref[0]
    both = adjoint_now * start_now.astype(full)
    by_head = jnp.sum(both.reshape(heads, HEADDIM, STATE), axis=1)
    by_head = jnp.concatenate([by_head, jnp.zeros((LANES - heads, STATE), full)], axis=0)
    over = dot_nt(jnp.ones((8, STATE), full), by_head, highest)
    ends = jnp.exp(cum_ref[CHUNK - 1 : CHUNK, :])
    dlog = dlog + over[0:1] * ends
    dlog = dlog + dot_nn((row <= col).astype(full), by_state, highest)
    dlog = dlog + dot_nn((row > col).astype(full), by_later, highest)
    rate = rate_ref[...]
    step = (ddt + rate * dlog) * jax.nn.sigmoid(raw_ref[...] + bias_ref[...])
    back_ref[:, channels:] = step.astype(low)
    head_sums_ref[0:1, :] += jnp.sum(step, axis=0, keepdims=True)
    head_sums_ref[1:2, :] += jnp.sum(dlog * rate * dt_ref[...], axis=0, keepdims=True)
    d_aff = jnp.where(causal, d_affinity, 0.0).astype(low)
    back[:CHUNK, inner : inner + STATE] = dot_tn(d_aff, c_low) + dot_nn(uw[...], adjoint_now.astype(low))
    back[:CHUNK, inner + STATE :] = dot_nn(d_aff, b_low) + dot_nn(dye[...], start_now)
    fresh = dot_tn(dye[...], c_low)
    for pair in range(heads // 2):
        h0, h1 = 2 * pair, 2 * pair + 1
        span = slice(pair * LANES, (pair + 1) * LANES)
        shrink = jnp.where(row < HEADDIM, ends[:, h0 : h0 + 1], ends[:, h1 : h1 + 1])
        adjoint[span, :] = shrink * adjoint_now[span, :] + fresh[span, :]
    for group in range(channels // LANES):
        span = slice(group * LANES, (group + 1) * LANES)
        taken = [
            window[RIM - CONV + 1 + k : RIM - CONV + 1 + k + CHUNK, span] for k in range(CONV)
        ]
        pre = taps_ref[CONV : CONV + 1, span]
        for k in range(CONV):
            pre = pre + taps_ref[k : k + 1, span] * taken[k]
        sig = jax.nn.sigmoid(pre)
        back_pre = back[:CHUNK, span] * (sig * (1.0 + pre * (1.0 - sig)))
        back[:CHUNK, span] = back_pre
        for k in range(CONV):
            sums_ref[k : k + 1, span] += jnp.sum(back_pre * taken[k], axis=0, keepdims=True)
        sums_ref[CONV : CONV + 1, span] += jnp.sum(back_pre, axis=0, keepdims=True)
        total = taps_ref[CONV - 1 : CONV, span] * back_pre
        for k in range(CONV - 1):
            total = total + taps_ref[k : k + 1, span] * back[CONV - 1 - k : CONV - 1 - k + CHUNK, span]
        back_ref[:, span] = total.astype(low)
    back[CHUNK:, :] = back[:8, :]

    @pl.when(at_start)
    def _():
        first_ref[...] = back[:8, :]


def ssm_forward(act, dt, cum, cum_t, skip_row, entering):
    rows = act.shape[0]
    heads = cum_t.shape[0]
    inner = heads * HEADDIM
    blocks = rows // CHUNK
    return pl.pallas_call(
        fwd_kernel,
        grid=(blocks,),
        in_specs=[
            pl.BlockSpec((CHUNK, inner), lambda i: (i, 0)),
            pl.BlockSpec((CHUNK, 2 * STATE), lambda i: (i, inner // (2 * STATE))),
            pl.BlockSpec((CHUNK, LANES), lambda i: (i, 0)),
            pl.BlockSpec((CHUNK, LANES), lambda i: (i, 0)),
            pl.BlockSpec((heads, CHUNK), lambda i: (0, i)),
            pl.BlockSpec((1, inner), lambda i: (0, 0)),
            pl.BlockSpec((inner, STATE), lambda i: (0, 0)),
        ],
        out_specs=[
            pl.BlockSpec((CHUNK, inner), lambda i: (i, 0)),
            pl.BlockSpec((1, inner, STATE), lambda i: (i, 0, 0)),
        ],
        out_shape=[
            jax.ShapeDtypeStruct((rows, inner), full),
            jax.ShapeDtypeStruct((blocks, inner, STATE), low),
        ],
        scratch_shapes=[pltpu.VMEM((inner, STATE), full)],
        compiler_params=pltpu.CompilerParams(
            dimension_semantics=("arbitrary",), vmem_limit_bytes=40 * 1024 * 1024
        ),
        cost_estimate=pl.CostEstimate(
            flops=rows * inner * 2 * 4 * STATE,
            bytes_accessed=rows * inner * 10,
            transcendentals=rows * heads * CHUNK * 2,
        ),
        name="ssm_forward",
    )(act, act, dt, cum, cum_t, skip_row, entering)


def ssm_backward(act, dt, cum, cum_t, skip_row, dy, starts, later, feed, rim, taps, raw, bias, rate):
    rows, channels = feed.shape
    lane_row = pl.BlockSpec((1, LANES), lambda i: (0, 0))
    per_block = CHUNK // RIM
    channel = lax.broadcasted_iota(jnp.int32, (cum_t.shape[0] * HEADDIM, LANES), 0)
    pick = (channel // HEADDIM == lax.broadcasted_iota(jnp.int32, channel.shape, 1)).astype(low)
    heads = cum_t.shape[0]
    inner = heads * HEADDIM
    blocks = rows // CHUNK
    last = blocks - 1
    return pl.pallas_call(
        bwd_kernel,
        grid=(blocks,),
        in_specs=[
            pl.BlockSpec((CHUNK, inner), lambda i: (last - i, 0)),
            pl.BlockSpec((CHUNK, 2 * STATE), lambda i: (last - i, inner // (2 * STATE))),
            pl.BlockSpec((CHUNK, LANES), lambda i: (last - i, 0)),
            pl.BlockSpec((CHUNK, LANES), lambda i: (last - i, 0)),
            pl.BlockSpec((heads, CHUNK), lambda i: (0, last - i)),
            pl.BlockSpec((1, inner), lambda i: (0, 0)),
            pl.BlockSpec((CHUNK, inner), lambda i: (last - i, 0)),
            pl.BlockSpec((1, inner, STATE), lambda i: (last - i, 0, 0)),
            pl.BlockSpec((inner, STATE), lambda i: (0, 0)),
            pl.BlockSpec((CHUNK, channels), lambda i: (last - i, 0)),
            pl.BlockSpec((RIM, channels), lambda i: (jnp.maximum((last - i) * per_block - 1, 0), 0)),
            pl.BlockSpec((RIM, channels), lambda i: (0, 0)),
            pl.BlockSpec((8, channels), lambda i: (0, 0)),
            pl.BlockSpec((CHUNK, LANES), lambda i: (last - i, 0)),
            lane_row,
            lane_row,
            pl.BlockSpec((inner, LANES), lambda i: (0, 0)),
        ],
        out_specs=[
            pl.BlockSpec((CHUNK, channels + LANES), lambda i: (last - i, 0)),
            pl.BlockSpec((8, channels), lambda i: (0, 0)),
            pl.BlockSpec((8, channels), lambda i: (0, 0)),
            pl.BlockSpec((8, LANES), lambda i: (0, 0)),
        ],
        out_shape=[
            jax.ShapeDtypeStruct((rows, channels + LANES), low),
            jax.ShapeDtypeStruct((8, channels), full),
            jax.ShapeDtypeStruct((8, channels), full),
            jax.ShapeDtypeStruct((8, LANES), full),
        ],
        scratch_shapes=[
            pltpu.VMEM((inner, STATE), full),
            pltpu.VMEM((CHUNK, inner), low),
            pltpu.VMEM((CHUNK, inner), low),
            pltpu.VMEM((CHUNK, inner), low),
            pltpu.VMEM((CHUNK, inner), low),
            pltpu.VMEM((CHUNK, inner), low),
            pltpu.VMEM((CHUNK + RIM, channels), full),
            pltpu.VMEM((CHUNK + 8, channels), full),
        ],
        compiler_params=pltpu.CompilerParams(
            dimension_semantics=("arbitrary",), vmem_limit_bytes=40 * 1024 * 1024
        ),
        cost_estimate=pl.CostEstimate(
            flops=rows * inner * 2 * 16 * STATE,
            bytes_accessed=rows * inner * 16,
            transcendentals=rows * heads * CHUNK * 2,
        ),
        name="ssm_backward",
    )(act, act, dt, cum, cum_t, skip_row, dy, starts, later, feed, feed, rim, taps, raw, bias, rate, pick)


def heads_to_channels(values):
    heads = values.shape[1]
    head = lax.broadcasted_iota(jnp.int32, (heads, heads * HEADDIM), 0)
    channel = lax.broadcasted_iota(jnp.int32, (heads, heads * HEADDIM), 1)
    return dot_nn(values, (channel // HEADDIM == head).astype(full), highest)


def silu_slope(value, sig):
    return sig * (1.0 + value * (1.0 - sig))


def layer_forward(hidden, valid, weights, params):
    gain, taps, step_bias, decay_log, skip, out_gain = params
    feed_weight, gate_weight, out_weight = weights
    rows, width = hidden.shape
    heads = step_bias.shape[0]
    inner = heads * HEADDIM
    channels = inner + 2 * STATE
    norm = lax.rsqrt(jnp.mean(hidden * hidden, axis=-1, keepdims=True) + epsilon)
    normed = (hidden * norm * gain).astype(low)
    feed_all = dot_nn(normed, feed_weight)
    feed = feed_all[:, :channels].astype(low)
    raw = feed_all[:, channels:]
    rim = shifted(feed[rows - RIM :], "ctx", 1)
    gate = dot_nn(normed, gate_weight)
    lanes = ((0, 0), (0, LANES - heads))
    bias = jnp.pad(step_bias[None], lanes)
    rate = jnp.pad(-jnp.exp(decay_log)[None], lanes)
    taps = jnp.pad(taps, ((0, 8 - CONV - 1), (0, 0)))
    act, dt, cum, cum_t, since, local_state = mixer_prep(feed, rim, taps, raw, bias, rate, heads)
    shrink = jnp.repeat(since[rows - 1, :heads], HEADDIM)[:, None]
    entering = chain(local_state, shrink, 1)
    skip_row = jnp.repeat(skip, HEADDIM)[None]
    scan = (act, dt, cum, cum_t, skip_row)
    conv = (feed, rim, taps, raw, bias, rate)
    ssm_out, starts = ssm_forward(*scan, entering)
    gated = ssm_out * (gate * jax.nn.sigmoid(gate))
    squares = jnp.sum(gated * gated, axis=-1)
    scaled = (gated * out_gain).astype(low)
    term = dot_nt(scaled, out_weight).astype(low)
    branch = term.astype(full) + swap_cores(term).astype(full)
    squares = squares + swap_cores(squares)
    out_norm = lax.rsqrt(squares / INNER + epsilon)[:, None]
    result = hidden + valid * out_norm * branch
    kept = (
        hidden, norm, normed, act, gate, since, shrink,
        scan, conv, starts, ssm_out, scaled, branch.astype(low), out_norm,
    )
    return result, kept


def chain(local_state, shrink, steps):
    entering = shifted(local_state.astype(low), "ctx", steps)
    for _ in range(lax.axis_size("ctx") - 2):
        leaving = shrink * entering.astype(full) + local_state
        entering = shifted(leaving.astype(low), "ctx", steps)
    return entering


def layer_backward(incoming, valid, weights, params, kept, pending=None):
    gain, taps, step_bias, decay_log, skip, out_gain = params
    feed_weight, gate_weight, out_weight = weights
    (
        hidden, norm, normed, act, gate, since, shrink,
        scan, conv, starts, ssm_out, scaled, branch, out_norm,
    ) = kept
    rows, width = hidden.shape
    heads = step_bias.shape[0]
    inner = heads * HEADDIM
    channels = inner + 2 * STATE
    back_branch = (valid * incoming).astype(low)
    back_normed = dot_nn(back_branch, out_weight)
    if pending is not None:
        pair, feed = pending
        back_normed, (pair.sums, feed.sums) = tied(back_normed, (pair.sums, feed.sums))
        pair.sums = scatter_sum([by_tp(pair.sums[0]), by_tp(pair.sums[1])], "tp")
        feed.second()
    back_wide = back_branch.astype(full)
    grad_out = dot_tn((back_wide * out_norm).astype(low), scaled).astype(low)
    along = jnp.sum(back_wide * branch.astype(full), axis=-1, keepdims=True)
    sig = jax.nn.sigmoid(gate)
    silu = gate * sig
    gated = ssm_out * silu
    grad_out_gain = jnp.sum(back_normed * gated * out_norm, axis=0)
    back_gated = out_norm * out_gain * back_normed - gated * (out_norm**3 * along / INNER)
    back_ssm = back_gated * silu
    back_gate = (back_gated * ssm_out * silu_slope(gate, sig)).astype(low)
    grad_gate = dot_tn(normed, back_gate).astype(low)
    weighted = (back_ssm * heads_to_channels(since[:, :heads])).astype(low)
    local_adjoint = dot_tn(weighted, act[:, inner + STATE :].astype(low))
    later = chain(local_adjoint, shrink, -1)
    early = Reduction([grad_gate], [grad_out])
    if pending is not None:
        back_ssm, feed.sums = tied(back_ssm, feed.sums)
        feed.sums = scatter_sum(feed_blocks(columns(feed.sums), inner), "tp")
    early.first()
    back_all, first_rows, sums, head_sums = ssm_backward(*scan, back_ssm, starts, later, *conv)
    following = shifted(first_rows, "ctx", -1)
    taps = conv[2]
    edge = sum(
        jnp.pad(taps[k] * following[: CONV - 1 - k], ((RIM - CONV + 1 + k, 0), (0, LANES))) for k in range(CONV - 1)
    )
    back_all = lax.dynamic_update_slice_in_dim(
        back_all, (back_all[rows - RIM :].astype(full) + edge).astype(low), rows - RIM, 0
    )
    back_all, early.sums = tied(back_all, early.sums)
    if pending is not None:
        back_all, (pair.sums, feed.sums) = tied(back_all, (pair.sums, feed.sums))
    early.second()
    grad_skip = jnp.sum(sums[CONV + 1, :inner].reshape(heads, HEADDIM), axis=1)
    grad_step_bias, grad_decay = head_sums[0, :heads], head_sums[1, :heads]
    grad_taps = sums[: CONV + 1]
    term = (dot_nt(back_all, feed_weight) + dot_nt(back_gate, gate_weight)).astype(low)
    back_in = term.astype(full) + swap_cores(term).astype(full)
    grad_feed = dot_tn(normed, back_all).astype(low)
    grad_gain = jnp.sum(back_in * hidden * norm, axis=0)
    scaled_in = back_in * gain
    along_in = jnp.sum(scaled_in * hidden, axis=-1, keepdims=True)
    delta = norm * scaled_in - hidden * (norm**3 * along_in / width)
    small = jnp.concatenate(
        [
            grad_taps[:, :inner].reshape(-1), grad_taps[:, inner:].reshape(-1),
            grad_out_gain, grad_step_bias, grad_decay, grad_skip, grad_gain,
        ]
    )
    return delta, grad_feed, small, early


def by_tp(value):
    return jnp.moveaxis(value.reshape(value.shape[0], lax.axis_size("tp"), -1), 1, 0)


class Reduction:
    def __init__(self, half_a, half_b):
        ndp, nctx = lax.axis_size("dp"), lax.axis_size("ctx")
        rows = half_a[0].shape[0] // (ndp * nctx)
        self.halves = [
            [part.reshape(ndp, nctx, rows, part.shape[1]) for part in half] for half in (half_a, half_b)
        ]

    def first(self):
        self.sums = (
            scatter_sum(self.halves[0], "ctx", 1).astype(low),
            scatter_sum(self.halves[1], "dp", 0).astype(low),
        )

    def second(self):
        self.sums = (
            scatter_sum([self.sums[0]], "dp").astype(low),
            scatter_sum([self.sums[1]], "ctx").astype(low),
        )


def feed_blocks(feed, inner):
    rest = feed[:, inner:]
    return [by_tp(feed[:, :inner]), jnp.broadcast_to(rest, (lax.axis_size("tp"),) + rest.shape)]


def on_device(
    acts,
    cotangent,
    lengths,
    norm_gain,
    proj_gate_x,
    proj_state,
    proj_step,
    conv_inner,
    conv_state,
    step_bias,
    decay_log,
    skip_weight,
    out_gain,
    proj_out,
):
    micro_count, rows, width = (acts.shape[0], acts.shape[2], acts.shape[3])
    tp_count = lax.axis_size("tp")
    core = lax.axis_index("section")
    lane = lax.axis_index("tp")
    first = core == 0
    own_rows = proj_gate_x.shape[1]
    half = proj_gate_x.shape[3] // 2
    step_half = proj_step.shape[2] // 2
    heads = step_half * tp_count
    inner = half * tp_count
    quarter = 2 * STATE // tp_count
    wide = quarter

    state_part = lax.dynamic_slice_in_dim(proj_state[0], lane * quarter, quarter, 1)

    def pack(c):
        step = proj_step[0, :, c * step_half : (c + 1) * step_half]
        tail = jnp.pad(columns([step, norm_gain[0][:, None]]), ((0, 0), (0, wide - step_half - 1)))
        return columns(
            [
                proj_gate_x[0, :, 1, c * half : (c + 1) * half],
                state_part,
                tail,
                proj_gate_x[0, :, 0, c * half : (c + 1) * half],
                proj_out[0, c * half : (c + 1) * half].T,
            ]
        )

    def pack_small(c):
        vector = jnp.concatenate(
            [
                conv_inner[0, :, c * half : (c + 1) * half].reshape(-1),
                out_gain[0, c * half : (c + 1) * half],
                step_bias[0, c * step_half : (c + 1) * step_half],
                decay_log[0, c * step_half : (c + 1) * step_half],
                skip_weight[0, c * step_half : (c + 1) * step_half],
                conv_state[0].reshape(-1),
            ]
        )
        parts = []
        for _ in range(3):
            part = lax.reduce_precision(vector, 8, 7)
            parts.append(part.astype(low))
            vector = vector - part
        return as_rows(jnp.concatenate(parts), cut)

    def both_layers(make):
        zero, one = make(0), make(1)
        keep = jnp.where(first, zero, one)
        came = swap_cores(jnp.where(first, one, zero))
        return jnp.where(first, keep, came), jnp.where(first, came, keep)

    def layer_params(rows_of_small):
        size = (CONV + 1) * half + half + 3 * step_half + (CONV + 1) * 2 * STATE
        three = rows_of_small.reshape(tp_count, -1)[:, : 3 * size].reshape(tp_count, 3, size)
        part = jnp.sum(three.astype(full), axis=1)
        at = (CONV + 1) * half
        taps_inner = jnp.moveaxis(part[:, :at].reshape(tp_count, CONV + 1, half), 0, 1)
        gains = part[:, at : at + half].reshape(-1)
        at += half
        scalars = []
        for _ in range(3):
            scalars.append(part[:, at : at + step_half].reshape(-1))
            at += step_half
        taps_state = part[0, at:].reshape(CONV + 1, 2 * STATE)
        taps = columns([taps_inner.reshape(CONV + 1, inner), taps_state])
        return taps, scalars[0], scalars[1], scalars[2], gains

    cut = half + quarter + wide
    middle = tp_count // 2

    def gather_item(part, sections):
        def side(pieces):
            parts, at = [], 0
            for size in sections:
                parts.append(columns(pieces[..., at : at + size]))
                at += size
            return columns(parts)

        half_a, half_b = gather_rows(side(part[:middle]), side(part[middle:]))
        result, at = [], 0
        for size in sections:
            result.append((half_a[:, at : at + middle * size], half_b[:, at : at + middle * size]))
            at += middle * size
        return result

    def feed_weights(parts):
        tails = [side.reshape(-1, middle, wide)[:, :, :step_half].reshape(-1, heads // 2) for side in parts[2]]
        gain = parts[2][0][:, step_half].astype(full)
        steps = jnp.pad(columns(tails), ((0, 0), (0, LANES - heads)))
        return columns(parts[0] + parts[1] + (steps,)), gain

    smalls = both_layers(pack_small)
    packs = both_layers(pack)
    feed_sections, pair_sections = (half, quarter, wide), (half, half)
    along_feed = line_gather(jnp.concatenate([packs[0][:, :cut], smalls[0]], axis=0), "tp")
    pair_pack, along_feed = tied(packs[0][:, cut:], along_feed)
    along_pair = line_gather(pair_pack, "tp")
    feed_parts = gather_item(along_feed[:, :own_rows], feed_sections)
    last_pack, along_pair = tied(packs[1], along_pair)
    small_pad = jnp.pad(smalls[1], ((0, 0), (0, last_pack.shape[1] - cut)))
    along_last = line_gather(jnp.concatenate([last_pack, small_pad], axis=0), "tp")
    pair_parts = gather_item(along_pair, pair_sections)
    along_last, pair_parts = tied(along_last, pair_parts)
    last_parts = gather_item(along_last[:, :own_rows, :cut], feed_sections)
    along_last, last_parts = tied(along_last, last_parts)
    last_parts += gather_item(along_last[:, :own_rows, cut:], pair_sections)
    feed_first, gain_first = feed_weights(feed_parts)
    feed_last, gain_last = feed_weights(last_parts[:3])
    weights = [
        (feed_first, columns(pair_parts[0]), columns(pair_parts[1])),
        (feed_last, columns(last_parts[3]), columns(last_parts[4])),
    ]
    params = [
        (gain_first,) + layer_params(along_feed[:, own_rows:]),
        (gain_last,) + layer_params(along_last[:, own_rows:, :cut]),
    ]

    places = lax.axis_index("ctx") * rows + jnp.arange(rows, dtype=jnp.int32)
    length = lax.dynamic_index_in_dim(lengths[:, 0], lane, 0, False)
    valid = (places < length).astype(full)[:, None]
    hidden = lax.dynamic_index_in_dim(acts[:, 0], lane, 0, False).astype(full)
    out_grad = lax.dynamic_index_in_dim(cotangent[:, 0], lane, 0, False)

    result_first, kept_first = layer_forward(hidden, valid, weights[0], params[0])
    low_first = result_first.astype(low)
    result_last, kept_last = layer_forward(low_first.astype(full), valid, weights[1], params[1])
    own_result = jnp.where(first, low_first, result_last.astype(low))
    quarter_rows = rows // tp_count
    section_out = spread_rows(own_result.reshape(tp_count, quarter_rows, width), (0, 1))

    part = inner // 2 + LANES
    delta_last, feed_last, small_last, pair_last = layer_backward(
        out_grad, valid, weights[1], params[1], kept_last
    )
    last = Reduction([feed_last[:, :part]], [feed_last[:, part:]])
    last.first()
    spread_last = spread_rows(delta_last.astype(low).reshape(tp_count, quarter_rows, width), (1,))
    incoming = (out_grad + delta_last).astype(low).astype(full)
    delta_first, feed_first, small_first, pair_first = layer_backward(
        incoming, valid, weights[0], params[0], kept_first, (pair_last, last)
    )
    grad_first = (incoming + delta_first).astype(low)
    feed_first, (grad_first, pair_first.sums) = tied(feed_first, (grad_first, pair_first.sums))
    feed = Reduction([feed_first[:, :part]], [feed_first[:, part:]])
    feed.first()
    pair_first_sum = scatter_sum([by_tp(pair_first.sums[0]), by_tp(pair_first.sums[1])], "tp")
    small = jnp.stack([small_first, small_last])
    spread_first = spread_rows(grad_first.reshape(tp_count, quarter_rows, width), (0,))
    small = all_sum(all_sum(small, "ctx"), "dp")
    feed.second()
    payload = columns(feed_blocks(columns(feed.sums), inner))
    extra = as_rows(small.astype(low).reshape(-1), payload.shape[2])
    payload = jnp.concatenate([payload, jnp.broadcast_to(extra, (tp_count,) + extra.shape)], axis=1)
    feed_sums = scatter_sum([payload], "tp")
    own_cotangent = lax.dynamic_slice_in_dim(
        cotangent[:, 0], lane * quarter_rows, quarter_rows, 1
    )
    input_grad = jnp.where(
        first, spread_first.astype(full), own_cotangent + spread_last.astype(full)
    )

    pair_keep = jnp.where(first, pair_first_sum, pair_last.sums)
    pair_came = swap_cores(jnp.where(first, pair_last.sums, pair_first_sum))
    size = small_first.shape[0]
    small_sums = feed_sums[own_rows:].reshape(-1)[: 2 * size].reshape(2, size)
    sums_last = last.sums
    total_width = sums_last.shape[1]
    joined = [
        jnp.concatenate([sums, as_rows(vector, total_width)])
        for sums, vector in zip((feed_sums[:own_rows], sums_last), small_sums)
    ]
    keep = jnp.where(first, joined[0], joined[1])
    came = swap_cores(jnp.where(first, joined[1], joined[0]))
    small_keep = keep[own_rows:].reshape(-1)[:size]
    small_came = came[own_rows:].reshape(-1)[:size]
    keep, came = keep[:own_rows], came[:own_rows]

    def halves(kept_part, came_part, axis):
        zero = jnp.where(first, kept_part, came_part)
        one = jnp.where(first, came_part, kept_part)
        return jnp.concatenate([zero, one], axis=axis)

    def own_lane(value, shape, axis):
        return lax.dynamic_index_in_dim(value.reshape(shape), lane, axis, False)

    grad_gate = halves(pair_keep[:, :half], pair_came[:, :half], 1)
    grad_out = halves(pair_keep[:, half:].T, pair_came[:, half:].T, 0)
    at = 0
    grad_x = halves(keep[:, at : at + half], came[:, at : at + half], 1)
    at += half
    grad_state = keep[:, at : at + 2 * STATE] + came[:, at : at + 2 * STATE]
    at += 2 * STATE + lane * step_half
    grad_step = halves(
        lax.dynamic_slice_in_dim(keep, at, step_half, 1), lax.dynamic_slice_in_dim(came, at, step_half, 1), 1
    )
    grad_gate_x = jnp.stack([grad_gate, grad_x], axis=1)

    at = (CONV + 1) * inner
    taps_shape = (CONV + 1, tp_count, half)
    grad_conv_inner = halves(
        own_lane(small_keep[:at], taps_shape, 1), own_lane(small_came[:at], taps_shape, 1), 1
    )
    end = at + (CONV + 1) * 2 * STATE
    grad_conv_state = (small_keep[at:end] + small_came[at:end]).reshape(CONV + 1, 2 * STATE)
    at = end
    vectors = []
    for size in (inner, heads, heads, heads):
        shape = (tp_count, size // tp_count)
        vectors.append(
            halves(
                own_lane(small_keep[at : at + size], shape, 0),
                own_lane(small_came[at : at + size], shape, 0),
                0,
            )
        )
        at += size
    owner = lax.axis_index("dp") * lax.axis_size("ctx") + lax.axis_index("ctx")
    grad_norm_gain = lax.dynamic_slice_in_dim(small_keep[at:], owner * own_rows, own_rows, 0)
    return (
        section_out[None, :, None],
        input_grad[None, :, None],
        grad_norm_gain[None],
        grad_gate_x[None],
        grad_state[None],
        grad_step[None],
        grad_conv_inner[None],
        grad_conv_state[None],
        vectors[1][None],
        vectors[2][None],
        vectors[3][None],
        vectors[0][None],
        grad_out[None],
    )


def solution(mesh):
    placed = (
        P(None, "dp", "ctx", None),
        P(None, "dp", "ctx", None),
        P(None, "dp"),
        P("section", ("dp", "ctx")),
        P("section", ("dp", "ctx"), None, "tp"),
        P("section", ("dp", "ctx"), None),
        P("section", ("dp", "ctx"), "tp"),
        P("section", None, "tp"),
        P("section", None, None),
        P("section", "tp"),
        P("section", "tp"),
        P("section", "tp"),
        P("section", "tp"),
        P("section", "tp", ("dp", "ctx")),
    )
    return jax.shard_map(
        on_device,
        mesh=mesh,
        in_specs=placed,
        out_specs=(
            P("section", None, "dp", ("ctx", "tp"), None),
            P("section", None, "dp", ("ctx", "tp"), None),
            P("section", ("dp", "ctx")),
            P("section", ("dp", "ctx"), None, "tp"),
            P("section", ("dp", "ctx"), None),
            P("section", ("dp", "ctx"), "tp"),
            P("section", None, "tp"),
            P("section", None, None),
            P("section", "tp"),
            P("section", "tp"),
            P("section", "tp"),
            P("section", "tp"),
            P("section", "tp", ("dp", "ctx")),
        ),
        check_vma=False,
    )
```

```python
import functools

import jax
import jax.numpy as jnp
from jax import lax
from jax.experimental import pallas as pl
from jax.experimental.pallas import tpu as pltpu
from jax.sharding import PartitionSpec as P

HEADDIM = 64
STATE = 128
INNER = 2048
CONV = 4
CHUNK = 128
LANES = 128
RIM = 16

highest = lax.Precision.HIGHEST
epsilon = 1e-05
low = jnp.bfloat16
full = jnp.float32


def dot_nn(a, b, precision=None):
    return lax.dot_general(
        a, b, (((1,), (0,)), ((), ())), precision=precision, preferred_element_type=full
    )


def dot_nt(a, b, precision=None):
    return lax.dot_general(
        a, b, (((1,), (1,)), ((), ())), precision=precision, preferred_element_type=full
    )


def dot_tn(a, b, precision=None):
    return lax.dot_general(
        a, b, (((0,), (0,)), ((), ())), precision=precision, preferred_element_type=full
    )


def shifted(value, axis, steps):
    count = lax.axis_size(axis)
    first, last = (max(0, -steps), min(count, count - steps))
    return lax.ppermute(value, axis, [(source, source + steps) for source in range(first, last)])


def rotated(value, axis, steps):
    count = lax.axis_size(axis)
    return lax.ppermute(value, axis, [(i, (i + steps) % count) for i in range(count)])


def line_gather(value, axis, dim=0):
    count = lax.axis_size(axis)
    place = lax.axis_index(axis)
    if count == 1:
        return jnp.expand_dims(value, dim)
    if count == 2:
        other = rotated(value, axis, 1)
        first = place == 0
        return jnp.stack([jnp.where(first, value, other), jnp.where(first, other, value)], axis=dim)
    up = down = value
    before, after = [], []
    for _ in range(1, count):
        up = shifted(up, axis, 1)
        down = shifted(down, axis, -1)
        before.insert(0, up)
        after.append(down)
    line = jnp.stack(before + [value] + after, axis=dim)
    return lax.dynamic_slice_in_dim(line, count - 1 - place, count, dim)


def ring_gather(value, axis):
    count = lax.axis_size(axis)
    place = lax.axis_index(axis)
    came = [value] + [rotated(value, axis, steps) for steps in range(1, count)]
    line = jnp.stack(came[::-1] + came[:0:-1])
    return lax.dynamic_slice_in_dim(line, count - 1 - place, count, 0)


def scatter_sum(pick, axis):
    count = lax.axis_size(axis)
    place = lax.axis_index(axis)
    total = pick(place).astype(full)
    for steps in range(1, count):
        total = total + rotated(pick((place + steps) % count), axis, steps).astype(full)
    return total


def all_sum(value, axis):
    total = value
    for steps in range(1, lax.axis_size(axis)):
        total = total + rotated(value, axis, steps)
    return total


def swap_cores(value):
    return lax.ppermute(value, "section", [(0, 1), (1, 0)])


def spread_rows(value, pairs_of):
    count = lax.axis_size("tp")
    place = lax.axis_index("tp")
    result = jnp.zeros_like(value)
    own = lax.dynamic_index_in_dim(value, place, 0, False)
    result = lax.dynamic_update_index_in_dim(result, own, place, 0)
    for steps in range(1, count):
        block = lax.dynamic_index_in_dim(value, (place + steps) % count, 0, False)
        pairs = [
            (core * count + i, core * count + (i + steps) % count)
            for core in pairs_of
            for i in range(count)
        ]
        arrived = lax.ppermute(block, ("section", "tp"), pairs)
        result = lax.dynamic_update_index_in_dim(result, arrived, (place - steps) % count, 0)
    return result


def gather_rows(early, late):
    width = early.shape[-1]
    half_a = line_gather(line_gather(early, "ctx"), "dp").reshape(-1, width)
    half_b = line_gather(line_gather(late, "dp"), "ctx", 1).reshape(-1, width)
    return half_a, half_b


def columns(pieces):
    return jnp.concatenate(list(pieces), axis=-1)


def as_rows(vector, width):
    rows = -(-vector.shape[0] // (16 * width)) * 16
    return jnp.pad(vector, (0, rows * width - vector.shape[0])).reshape(rows, width)


def tied(value, other):
    return lax.optimization_barrier((value, other))


def conv_taps_sum(taps_ref, rows_of):
    total = taps_ref[CONV : CONV + 1, :]
    for k in range(CONV):
        total = total + taps_ref[k : k + 1, :] * rows_of(k)
    return total


def prep_kernel(
    feed_ref, rim_ref, taps_ref, raw_ref, bias_ref, rate_ref,
    act_ref, dt_ref, cum_ref, cumt_ref, since_ref, local_ref,
    window, run,
):
    inner = local_ref.shape[0]

    @pl.when(pl.program_id(0) == 0)
    def _():
        window[:RIM, :] = rim_ref[...].astype(full)
        run[...] = jnp.zeros_like(run)
        local_ref[...] = jnp.zeros_like(local_ref)

    window[RIM:, :] = feed_ref[...].astype(full)
    pre = conv_taps_sum(taps_ref, lambda k: window[RIM - CONV + 1 + k : RIM - CONV + 1 + k + CHUNK, :])
    act = pre * jax.nn.sigmoid(pre)
    act_ref[...] = act
    window[:RIM, :] = window[CHUNK:, :]
    raw = raw_ref[...] + bias_ref[...]
    dt = jnp.maximum(raw, 0.0) + jnp.log1p(jnp.exp(-jnp.abs(raw)))
    row = lax.broadcasted_iota(jnp.int32, (CHUNK, CHUNK), 0)
    col = lax.broadcasted_iota(jnp.int32, (CHUNK, CHUNK), 1)
    cum = dot_nn((row >= col).astype(full), rate_ref[...] * dt, highest)
    dt_ref[...] = dt
    cum_ref[...] = cum
    cumt_ref[...] = cum.T[: cumt_ref.shape[0]]
    since_ref[...] = jnp.exp(run[0:1, :] + cum)
    end = cum[CHUNK - 1 : CHUNK, :]
    run[...] = run[...] + end
    weight = jnp.exp(end - cum) * dt
    shrink = jnp.exp(end)
    left = col < HEADDIM
    upper = row < HEADDIM
    b_low = act[:, inner : inner + STATE].astype(low)
    for pair in range(inner // LANES):
        h0, h1 = 2 * pair, 2 * pair + 1
        span = slice(pair * LANES, (pair + 1) * LANES)
        each = jnp.where(left, weight[:, h0 : h0 + 1], weight[:, h1 : h1 + 1])
        fresh = dot_tn((act[:, span] * each).astype(low), b_low)
        keep = jnp.where(upper, shrink[:, h0 : h0 + 1], shrink[:, h1 : h1 + 1])
        local_ref[span, :] = keep * local_ref[span, :] + fresh


def mixer_prep(feed, rim, taps, raw, bias, rate, heads):
    rows, channels = feed.shape
    inner = heads * HEADDIM
    lanes = pl.BlockSpec((CHUNK, LANES), lambda i: (i, 0))
    lane_row = pl.BlockSpec((1, LANES), lambda i: (0, 0))
    by_lane = jax.ShapeDtypeStruct((rows, LANES), full)
    return pl.pallas_call(
        prep_kernel,
        grid=(rows // CHUNK,),
        in_specs=[
            pl.BlockSpec((CHUNK, channels), lambda i: (i, 0)),
            pl.BlockSpec((RIM, channels), lambda i: (0, 0)),
            pl.BlockSpec((8, channels), lambda i: (0, 0)),
            lanes,
            lane_row,
            lane_row,
        ],
        out_specs=[
            pl.BlockSpec((CHUNK, channels), lambda i: (i, 0)),
            lanes,
            lanes,
            pl.BlockSpec((heads, CHUNK), lambda i: (0, i)),
            lanes,
            pl.BlockSpec((inner, STATE), lambda i: (0, 0)),
        ],
        out_shape=[
            jax.ShapeDtypeStruct((rows, channels), full),
            by_lane,
            by_lane,
            jax.ShapeDtypeStruct((heads, rows), full),
            by_lane,
            jax.ShapeDtypeStruct((inner, STATE), full),
        ],
        scratch_shapes=[pltpu.VMEM((CHUNK + RIM, channels), full), pltpu.VMEM((8, LANES), full)],
        compiler_params=pltpu.CompilerParams(
            dimension_semantics=("arbitrary",), vmem_limit_bytes=40 * 1024 * 1024
        ),
        cost_estimate=pl.CostEstimate(
            flops=rows * inner * 2 * STATE, bytes_accessed=rows * channels * 6, transcendentals=rows * channels
        ),
        name="mixer_prep",
    )(feed, rim, taps, raw, bias, rate)


def fwd_kernel(x_ref, bc_ref, dt_ref, cum_ref, cumt_ref, skip_ref, enter_ref, y_ref, start_ref, state):
    @pl.when(pl.program_id(0) == 0)
    def _():
        state[...] = enter_ref[...].astype(full)

    heads = cumt_ref.shape[0]
    start_ref[0] = state[...].astype(low)
    b_low = bc_ref[:, :STATE].astype(low)
    c_low = bc_ref[:, STATE:].astype(low)
    row = lax.broadcasted_iota(jnp.int32, (CHUNK, CHUNK), 0)
    col = lax.broadcasted_iota(jnp.int32, (CHUNK, CHUNK), 1)
    left = col < HEADDIM
    upper = row < HEADDIM
    masked = jnp.where(row >= col, dot_nt(c_low, b_low), 0.0)
    for pair in range(heads // 2):
        h0, h1 = 2 * pair, 2 * pair + 1
        span = slice(pair * LANES, (pair + 1) * LANES)
        cum0 = jnp.broadcast_to(cum_ref[:, h0 : h0 + 1], (CHUNK, CHUNK))
        cum1 = jnp.broadcast_to(cum_ref[:, h1 : h1 + 1], (CHUNK, CHUNK))
        w0 = jnp.exp(jnp.minimum(cum0 - cumt_ref[h0 : h0 + 1, :], 0.0)) * masked
        w1 = jnp.exp(jnp.minimum(cum1 - cumt_ref[h1 : h1 + 1, :], 0.0)) * masked
        weights = jnp.concatenate([w0.astype(low), w1.astype(low)], axis=1)
        x_pair = x_ref[:, span]
        u = x_pair * jnp.where(left, dt_ref[:, h0 : h0 + 1], dt_ref[:, h1 : h1 + 1])
        u_low = u.astype(low)
        zero = jnp.zeros_like(u_low)
        u_both = jnp.concatenate([jnp.where(left, u_low, zero), jnp.where(left, zero, u_low)], axis=0)
        cum_pair = jnp.where(left, cum0, cum1)
        s_pair = state[span, :]
        carried = jnp.exp(cum_pair) * dot_nt(c_low, s_pair.astype(low))
        y_ref[:, span] = dot_nn(weights, u_both) + carried + skip_ref[:, span] * x_pair
        end0 = cum_ref[CHUNK - 1 : CHUNK, h0 : h0 + 1]
        end1 = cum_ref[CHUNK - 1 : CHUNK, h1 : h1 + 1]
        ahead = jnp.exp(jnp.where(left, end0, end1) - cum_pair)
        fresh = dot_tn((u * ahead).astype(low), b_low)
        state[span, :] = jnp.exp(jnp.where(upper, end0, end1)) * s_pair + fresh


def bwd_kernel(
    x_ref, bc_ref, dt_ref, cum_ref, cumt_ref, skip_ref, dy_ref, start_ref, later_ref,
    feed_ref, before_ref, rim_ref, taps_ref, raw_ref, bias_ref, rate_ref, pick_ref,
    back_ref, first_ref, sums_ref, head_sums_ref,
    adjoint, dye, uw, xdu, dyi, udu, window, back,
):
    channels = feed_ref.shape[1]

    @pl.when(pl.program_id(0) == 0)
    def _():
        adjoint[...] = later_ref[...].astype(full)
        back[CHUNK:, :] = jnp.zeros((8, channels), full)
        sums_ref[...] = jnp.zeros_like(sums_ref)
        head_sums_ref[...] = jnp.zeros_like(head_sums_ref)

    at_start = pl.program_id(0) == pl.num_programs(0) - 1
    window[:RIM, :] = jnp.where(at_start, rim_ref[...].astype(full), before_ref[...].astype(full))
    window[RIM:, :] = feed_ref[...].astype(full)

    heads = cumt_ref.shape[0]
    inner = heads * HEADDIM
    b_low = bc_ref[:, :STATE].astype(low)
    c_low = bc_ref[:, STATE:].astype(low)
    row = lax.broadcasted_iota(jnp.int32, (CHUNK, CHUNK), 0)
    col = lax.broadcasted_iota(jnp.int32, (CHUNK, CHUNK), 1)
    left = col < HEADDIM
    causal = row >= col
    onward = (row <= col).astype(low)
    masked = jnp.where(causal, dot_nt(c_low, b_low), 0.0)
    d_affinity = jnp.zeros((CHUNK, CHUNK), full)
    dlog = jnp.zeros((CHUNK, LANES), full)
    for pair in range(heads // 2):
        h0, h1 = 2 * pair, 2 * pair + 1
        span = slice(pair * LANES, (pair + 1) * LANES)
        cum0 = jnp.broadcast_to(cum_ref[:, h0 : h0 + 1], (CHUNK, CHUNK))
        cum1 = jnp.broadcast_to(cum_ref[:, h1 : h1 + 1], (CHUNK, CHUNK))
        m0 = jnp.exp(jnp.minimum(cum0 - cumt_ref[h0 : h0 + 1, :], 0.0))
        m1 = jnp.exp(jnp.minimum(cum1 - cumt_ref[h1 : h1 + 1, :], 0.0))
        w0 = m0 * masked
        w1 = m1 * masked
        dt_pair = jnp.where(left, dt_ref[:, h0 : h0 + 1], dt_ref[:, h1 : h1 + 1])
        x_pair = x_ref[:, span]
        u = x_pair * dt_pair
        u_low = u.astype(low)
        dy_pair = dy_ref[:, span]
        dy_low = dy_pair.astype(low)
        zero = jnp.zeros_like(dy_low)
        dy_both = jnp.concatenate([jnp.where(left, dy_low, zero), jnp.where(left, zero, dy_low)], axis=0)
        dw = dot_nt(dy_both, u_low)
        dw0, dw1 = dw[:CHUNK], dw[CHUNK:]
        d_affinity = d_affinity + dw0 * m0 + dw1 * m1
        z_both = jnp.concatenate([(dw0 * w0).astype(low), (dw1 * w1).astype(low)], axis=1)
        reach = dot_nn(onward, z_both)
        k0 = jnp.sum(jnp.where(row > col, reach[:, :CHUNK], 0.0), axis=1, keepdims=True)
        k1 = jnp.sum(jnp.where(row > col, reach[:, CHUNK:], 0.0), axis=1, keepdims=True)
        dlog = jnp.where(col == h0, k0, jnp.where(col == h1, k1, dlog))
        w_both = jnp.concatenate([w0.astype(low), w1.astype(low)], axis=0)
        cum_pair = jnp.where(left, cum0, cum1)
        end0 = cum_ref[CHUNK - 1 : CHUNK, h0 : h0 + 1]
        end1 = cum_ref[CHUNK - 1 : CHUNK, h1 : h1 + 1]
        ahead = jnp.exp(jnp.where(left, end0, end1) - cum_pair)
        since = jnp.exp(cum_pair)
        du_state = ahead * dot_nt(b_low, adjoint[span, :].astype(low))
        du = dot_tn(w_both, dy_both) + du_state
        back[:CHUNK, span] = dt_pair * du + skip_ref[:, span] * dy_pair
        sums_ref[CONV + 1 : CONV + 2, span] += jnp.sum(x_pair * dy_pair, axis=0, keepdims=True)
        y_state = since * dot_nt(c_low, start_ref[0, span, :])
        xdu[:, span] = (x_pair * du).astype(low)
        dyi[:, span] = (dy_pair * y_state).astype(low)
        udu[:, span] = (u * du_state).astype(low)
        dye[:, span] = (dy_pair * since).astype(low)
        uw[:, span] = (u * ahead).astype(low)
    pick = pick_ref[...]
    ddt = dot_nn(xdu[...], pick)
    by_state = dot_nn(dyi[...], pick)
    by_later = dot_nn(udu[...], pick)
    adjoint_now = adjoint[...]
    start_now = start_ref[0]
    both = adjoint_now * start_now.astype(full)
    by_head = jnp.sum(both.reshape(heads, HEADDIM, STATE), axis=1)
    by_head = jnp.concatenate([by_head, jnp.zeros((LANES - heads, STATE), full)], axis=0)
    over = dot_nt(jnp.ones((8, STATE), full), by_head, highest)
    ends = jnp.exp(cum_ref[CHUNK - 1 : CHUNK, :])
    dlog = dlog + over[0:1] * ends
    dlog = dlog + dot_nn((row <= col).astype(full), by_state, highest)
    dlog = dlog + dot_nn((row > col).astype(full), by_later, highest)
    rate = rate_ref[...]
    step = (ddt + rate * dlog) * jax.nn.sigmoid(raw_ref[...] + bias_ref[...])
    back_ref[:, channels:] = step.astype(low)
    head_sums_ref[0:1, :] += jnp.sum(step, axis=0, keepdims=True)
    head_sums_ref[1:2, :] += jnp.sum(dlog * rate * dt_ref[...], axis=0, keepdims=True)
    d_aff = jnp.where(causal, d_affinity, 0.0).astype(low)
    back[:CHUNK, inner : inner + STATE] = dot_tn(d_aff, c_low) + dot_nn(uw[...], adjoint_now.astype(low))
    back[:CHUNK, inner + STATE :] = dot_nn(d_aff, b_low) + dot_nn(dye[...], start_now)
    fresh = dot_tn(dye[...], c_low)
    for pair in range(heads // 2):
        h0, h1 = 2 * pair, 2 * pair + 1
        span = slice(pair * LANES, (pair + 1) * LANES)
        shrink = jnp.where(row < HEADDIM, ends[:, h0 : h0 + 1], ends[:, h1 : h1 + 1])
        adjoint[span, :] = shrink * adjoint_now[span, :] + fresh[span, :]
    for group in range(channels // LANES):
        span = slice(group * LANES, (group + 1) * LANES)
        taken = [
            window[RIM - CONV + 1 + k : RIM - CONV + 1 + k + CHUNK, span] for k in range(CONV)
        ]
        pre = taps_ref[CONV : CONV + 1, span]
        for k in range(CONV):
            pre = pre + taps_ref[k : k + 1, span] * taken[k]
        sig = jax.nn.sigmoid(pre)
        back_pre = back[:CHUNK, span] * (sig * (1.0 + pre * (1.0 - sig)))
        back[:CHUNK, span] = back_pre
        for k in range(CONV):
            sums_ref[k : k + 1, span] += jnp.sum(back_pre * taken[k], axis=0, keepdims=True)
        sums_ref[CONV : CONV + 1, span] += jnp.sum(back_pre, axis=0, keepdims=True)
        total = taps_ref[CONV - 1 : CONV, span] * back_pre
        for k in range(CONV - 1):
            total = total + taps_ref[k : k + 1, span] * back[CONV - 1 - k : CONV - 1 - k + CHUNK, span]
        back_ref[:, span] = total.astype(low)
    back[CHUNK:, :] = back[:8, :]

    @pl.when(at_start)
    def _():
        first_ref[...] = back[:8, :]


def ssm_forward(act, dt, cum, cum_t, skip_row, entering):
    rows = act.shape[0]
    heads = cum_t.shape[0]
    inner = heads * HEADDIM
    blocks = rows // CHUNK
    return pl.pallas_call(
        fwd_kernel,
        grid=(blocks,),
        in_specs=[
            pl.BlockSpec((CHUNK, inner), lambda i: (i, 0)),
            pl.BlockSpec((CHUNK, 2 * STATE), lambda i: (i, inner // (2 * STATE))),
            pl.BlockSpec((CHUNK, LANES), lambda i: (i, 0)),
            pl.BlockSpec((CHUNK, LANES), lambda i: (i, 0)),
            pl.BlockSpec((heads, CHUNK), lambda i: (0, i)),
            pl.BlockSpec((1, inner), lambda i: (0, 0)),
            pl.BlockSpec((inner, STATE), lambda i: (0, 0)),
        ],
        out_specs=[
            pl.BlockSpec((CHUNK, inner), lambda i: (i, 0)),
            pl.BlockSpec((1, inner, STATE), lambda i: (i, 0, 0)),
        ],
        out_shape=[
            jax.ShapeDtypeStruct((rows, inner), full),
            jax.ShapeDtypeStruct((blocks, inner, STATE), low),
        ],
        scratch_shapes=[pltpu.VMEM((inner, STATE), full)],
        compiler_params=pltpu.CompilerParams(
            dimension_semantics=("arbitrary",), vmem_limit_bytes=40 * 1024 * 1024
        ),
        cost_estimate=pl.CostEstimate(
            flops=rows * inner * 2 * 4 * STATE,
            bytes_accessed=rows * inner * 10,
            transcendentals=rows * heads * CHUNK * 2,
        ),
        name="ssm_forward",
    )(act, act, dt, cum, cum_t, skip_row, entering)


def ssm_backward(act, dt, cum, cum_t, skip_row, dy, starts, later, feed, rim, taps, raw, bias, rate):
    rows, channels = feed.shape
    lane_row = pl.BlockSpec((1, LANES), lambda i: (0, 0))
    per_block = CHUNK // RIM
    channel = lax.broadcasted_iota(jnp.int32, (cum_t.shape[0] * HEADDIM, LANES), 0)
    pick = (channel // HEADDIM == lax.broadcasted_iota(jnp.int32, channel.shape, 1)).astype(low)
    heads = cum_t.shape[0]
    inner = heads * HEADDIM
    blocks = rows // CHUNK
    last = blocks - 1
    return pl.pallas_call(
        bwd_kernel,
        grid=(blocks,),
        in_specs=[
            pl.BlockSpec((CHUNK, inner), lambda i: (last - i, 0)),
            pl.BlockSpec((CHUNK, 2 * STATE), lambda i: (last - i, inner // (2 * STATE))),
            pl.BlockSpec((CHUNK, LANES), lambda i: (last - i, 0)),
            pl.BlockSpec((CHUNK, LANES), lambda i: (last - i, 0)),
            pl.BlockSpec((heads, CHUNK), lambda i: (0, last - i)),
            pl.BlockSpec((1, inner), lambda i: (0, 0)),
            pl.BlockSpec((CHUNK, inner), lambda i: (last - i, 0)),
            pl.BlockSpec((1, inner, STATE), lambda i: (last - i, 0, 0)),
            pl.BlockSpec((inner, STATE), lambda i: (0, 0)),
            pl.BlockSpec((CHUNK, channels), lambda i: (last - i, 0)),
            pl.BlockSpec((RIM, channels), lambda i: (jnp.maximum((last - i) * per_block - 1, 0), 0)),
            pl.BlockSpec((RIM, channels), lambda i: (0, 0)),
            pl.BlockSpec((8, channels), lambda i: (0, 0)),
            pl.BlockSpec((CHUNK, LANES), lambda i: (last - i, 0)),
            lane_row,
            lane_row,
            pl.BlockSpec((inner, LANES), lambda i: (0, 0)),
        ],
        out_specs=[
            pl.BlockSpec((CHUNK, channels + LANES), lambda i: (last - i, 0)),
            pl.BlockSpec((8, channels), lambda i: (0, 0)),
            pl.BlockSpec((8, channels), lambda i: (0, 0)),
            pl.BlockSpec((8, LANES), lambda i: (0, 0)),
        ],
        out_shape=[
            jax.ShapeDtypeStruct((rows, channels + LANES), low),
            jax.ShapeDtypeStruct((8, channels), full),
            jax.ShapeDtypeStruct((8, channels), full),
            jax.ShapeDtypeStruct((8, LANES), full),
        ],
        scratch_shapes=[
            pltpu.VMEM((inner, STATE), full),
            pltpu.VMEM((CHUNK, inner), low),
            pltpu.VMEM((CHUNK, inner), low),
            pltpu.VMEM((CHUNK, inner), low),
            pltpu.VMEM((CHUNK, inner), low),
            pltpu.VMEM((CHUNK, inner), low),
            pltpu.VMEM((CHUNK + RIM, channels), full),
            pltpu.VMEM((CHUNK + 8, channels), full),
        ],
        compiler_params=pltpu.CompilerParams(
            dimension_semantics=("arbitrary",), vmem_limit_bytes=40 * 1024 * 1024
        ),
        cost_estimate=pl.CostEstimate(
            flops=rows * inner * 2 * 16 * STATE,
            bytes_accessed=rows * inner * 16,
            transcendentals=rows * heads * CHUNK * 2,
        ),
        name="ssm_backward",
    )(act, act, dt, cum, cum_t, skip_row, dy, starts, later, feed, feed, rim, taps, raw, bias, rate, pick)


def heads_to_channels(values):
    heads = values.shape[1]
    head = lax.broadcasted_iota(jnp.int32, (heads, heads * HEADDIM), 0)
    channel = lax.broadcasted_iota(jnp.int32, (heads, heads * HEADDIM), 1)
    return dot_nn(values, (channel // HEADDIM == head).astype(full), highest)


def silu_slope(value, sig):
    return sig * (1.0 + value * (1.0 - sig))


def layer_forward(hidden, before, valid, weights, params):
    gain, taps, step_bias, decay_log, skip, out_gain = params
    feed_weight, gate_weight, out_weight = weights
    rows, width = hidden.shape
    heads = step_bias.shape[0]
    inner = heads * HEADDIM
    channels = inner + 2 * STATE
    norm = lax.rsqrt(jnp.mean(hidden * hidden, axis=-1, keepdims=True) + epsilon)
    normed = (hidden * norm * gain).astype(low)
    feed_all = dot_nn(normed, feed_weight)
    feed = feed_all[:, :channels].astype(low)
    raw = feed_all[:, channels:]
    before = before.astype(full)
    before_norm = lax.rsqrt(jnp.mean(before * before, axis=-1, keepdims=True) + epsilon)
    rim = dot_nn((before * before_norm * gain).astype(low), feed_weight[:, :channels]).astype(low)
    gate = dot_nn(normed, gate_weight)
    lanes = ((0, 0), (0, LANES - heads))
    bias = jnp.pad(step_bias[None], lanes)
    rate = jnp.pad(-jnp.exp(decay_log)[None], lanes)
    taps = jnp.pad(taps, ((0, 8 - CONV - 1), (0, 0)))
    act, dt, cum, cum_t, since, local_state = mixer_prep(feed, rim, taps, raw, bias, rate, heads)
    shrink = jnp.repeat(since[rows - 1, :heads], HEADDIM)[:, None]
    entering = chain(local_state, shrink, 1)
    skip_row = jnp.repeat(skip, HEADDIM)[None]
    scan = (act, dt, cum, cum_t, skip_row)
    conv = (feed, rim, taps, raw, bias, rate)
    ssm_out, starts = ssm_forward(*scan, entering)
    gated = ssm_out * (gate * jax.nn.sigmoid(gate))
    squares = jnp.sum(gated * gated, axis=-1)
    scaled = (gated * out_gain).astype(low)
    term = dot_nt(scaled, out_weight).astype(low)
    branch = term.astype(full) + swap_cores(term).astype(full)
    squares = squares + swap_cores(squares)
    out_norm = lax.rsqrt(squares / INNER + epsilon)[:, None]
    result = hidden + valid * out_norm * branch
    kept = (
        hidden, norm, normed, act, gate, since, shrink,
        scan, conv, starts, ssm_out, scaled, branch.astype(low), out_norm,
    )
    return result, kept


def chain(local_state, shrink, steps):
    entering = shifted(local_state.astype(low), "ctx", steps)
    for _ in range(lax.axis_size("ctx") - 2):
        leaving = shrink * entering.astype(full) + local_state
        entering = shifted(leaving.astype(low), "ctx", steps)
    return entering


def layer_backward(incoming, valid, weights, params, kept, pending=None):
    gain, taps, step_bias, decay_log, skip, out_gain = params
    feed_weight, gate_weight, out_weight = weights
    (
        hidden, norm, normed, act, gate, since, shrink,
        scan, conv, starts, ssm_out, scaled, branch, out_norm,
    ) = kept
    rows, width = hidden.shape
    heads = step_bias.shape[0]
    inner = heads * HEADDIM
    channels = inner + 2 * STATE
    back_branch = (valid * incoming).astype(low)
    back_normed = dot_nn(back_branch, out_weight)
    if pending is not None:
        pair, feed = pending
        back_normed, (pair.sums, feed.sums) = tied(back_normed, (pair.sums, feed.sums))
        pair.sums = pair_sum(pair.sums)
        feed.second()
    back_wide = back_branch.astype(full)
    grad_out = dot_tn((back_wide * out_norm).astype(low), scaled).astype(low)
    along = jnp.sum(back_wide * branch.astype(full), axis=-1, keepdims=True)
    sig = jax.nn.sigmoid(gate)
    silu = gate * sig
    gated = ssm_out * silu
    grad_out_gain = jnp.sum(back_normed * gated * out_norm, axis=0)
    back_gated = out_norm * out_gain * back_normed - gated * (out_norm**3 * along / INNER)
    back_ssm = back_gated * silu
    back_gate = (back_gated * ssm_out * silu_slope(gate, sig)).astype(low)
    grad_gate = dot_tn(normed, back_gate).astype(low)
    weighted = (back_ssm * heads_to_channels(since[:, :heads])).astype(low)
    local_adjoint = dot_tn(weighted, act[:, inner + STATE :].astype(low))
    later = chain(local_adjoint, shrink, -1)
    early = whole_reduction(grad_gate, grad_out)
    if pending is not None:
        back_ssm, feed.sums = tied(back_ssm, feed.sums)
        feed.sums = feed_sum(feed.sums, inner)
    early.first()
    back_all, first_rows, sums, head_sums = ssm_backward(*scan, back_ssm, starts, later, *conv)
    following = shifted(first_rows, "ctx", -1)
    taps = conv[2]
    edge = sum(
        jnp.pad(taps[k] * following[: CONV - 1 - k], ((RIM - CONV + 1 + k, 0), (0, LANES))) for k in range(CONV - 1)
    )
    back_all = lax.dynamic_update_slice_in_dim(
        back_all, (back_all[rows - RIM :].astype(full) + edge).astype(low), rows - RIM, 0
    )
    back_all, early.sums = tied(back_all, early.sums)
    if pending is not None:
        back_all, (pair.sums, feed.sums) = tied(back_all, (pair.sums, feed.sums))
    early.second()
    grad_skip = jnp.sum(sums[CONV + 1, :inner].reshape(heads, HEADDIM), axis=1)
    grad_step_bias, grad_decay = head_sums[0, :heads], head_sums[1, :heads]
    grad_taps = sums[: CONV + 1]
    term = (dot_nt(back_all, feed_weight) + dot_nt(back_gate, gate_weight)).astype(low)
    back_in = term.astype(full) + swap_cores(term).astype(full)
    grad_feed = dot_tn(normed, back_all).astype(low)
    grad_gain = jnp.sum(back_in * hidden * norm, axis=0)
    scaled_in = back_in * gain
    along_in = jnp.sum(scaled_in * hidden, axis=-1, keepdims=True)
    delta = norm * scaled_in - hidden * (norm**3 * along_in / width)
    small = jnp.concatenate(
        [
            grad_taps[:, :inner].reshape(-1), grad_taps[:, inner:].reshape(-1),
            grad_out_gain, grad_step_bias, grad_decay, grad_skip, grad_gain,
        ]
    )
    return delta, grad_feed, small, early


class Reduction:
    def __init__(self, half_a, half_b):
        self.half_a, self.half_b = half_a, half_b

    def first(self):
        ndp, nctx = lax.axis_size("dp"), lax.axis_size("ctx")

        def rows_of(half, owners):
            array, low_row, high_row = half
            each = array.shape[0] // (ndp * nctx)
            return jnp.concatenate(
                [
                    lax.dynamic_slice_in_dim(array, owner * each + low_row, high_row - low_row, 0)
                    for owner in owners
                ],
                axis=0,
            )

        self.sums = (
            scatter_sum(
                lambda at: rows_of(self.half_a, [i * nctx + at for i in range(ndp)]), "ctx"
            ).astype(low),
            scatter_sum(
                lambda at: rows_of(self.half_b, [at * nctx + j for j in range(nctx)]), "dp"
            ).astype(low),
        )

    def second(self):
        def own(value, axis):
            each = value.shape[0] // lax.axis_size(axis)
            return scatter_sum(
                lambda at: lax.dynamic_slice_in_dim(value, at * each, each, 0), axis
            ).astype(low)

        self.sums = own(self.sums[0], "dp"), own(self.sums[1], "ctx")


def whole_reduction(first, second):
    rows = first.shape[0] // (lax.axis_size("dp") * lax.axis_size("ctx"))
    return Reduction((first, 0, rows), (second, 0, rows))


def split_reduction(array):
    rows = array.shape[0] // (lax.axis_size("dp") * lax.axis_size("ctx"))
    return Reduction((array, 0, rows // 2), (array, rows // 2, rows))


def lanes_of(value, at, inner):
    each = inner // lax.axis_size("tp")
    return lax.dynamic_slice_in_dim(value, at * each, each, 1)


def pair_sum(sums):
    return scatter_sum(lambda at: columns(lanes_of(part, at, part.shape[1]) for part in sums), "tp")


def feed_sum(sums, inner, small=None):
    joined = jnp.concatenate(sums, axis=0)

    def pick(at):
        block = columns([lanes_of(joined, at, inner), joined[:, inner:]])
        if small is not None:
            block = jnp.concatenate([block, as_rows(small, block.shape[1])], axis=0)
        return block

    return scatter_sum(pick, "tp")


def on_device(
    acts,
    cotangent,
    lengths,
    norm_gain,
    proj_gate_x,
    proj_state,
    proj_step,
    conv_inner,
    conv_state,
    step_bias,
    decay_log,
    skip_weight,
    out_gain,
    proj_out,
):
    micro_count, rows, width = (acts.shape[0], acts.shape[2], acts.shape[3])
    tp_count = lax.axis_size("tp")
    core = lax.axis_index("section")
    lane = lax.axis_index("tp")
    first = core == 0
    own_rows = proj_gate_x.shape[1]
    half = proj_gate_x.shape[3] // 2
    step_half = proj_step.shape[2] // 2
    heads = step_half * tp_count
    inner = half * tp_count
    quarter = 2 * STATE // tp_count
    wide = quarter

    state_part = lax.dynamic_slice_in_dim(proj_state[0], lane * quarter, quarter, 1)

    def pack(c):
        step = proj_step[0, :, c * step_half : (c + 1) * step_half]
        tail = jnp.pad(columns([step, norm_gain[0][:, None]]), ((0, 0), (0, wide - step_half - 1)))
        return columns(
            [
                proj_gate_x[0, :, 1, c * half : (c + 1) * half],
                state_part,
                tail,
                proj_gate_x[0, :, 0, c * half : (c + 1) * half],
                proj_out[0, c * half : (c + 1) * half].T,
            ]
        )

    def pack_small(c):
        vector = jnp.concatenate(
            [
                conv_inner[0, :, c * half : (c + 1) * half].reshape(-1),
                out_gain[0, c * half : (c + 1) * half],
                step_bias[0, c * step_half : (c + 1) * step_half],
                decay_log[0, c * step_half : (c + 1) * step_half],
                skip_weight[0, c * step_half : (c + 1) * step_half],
                conv_state[0].reshape(-1),
            ]
        )
        parts = []
        for _ in range(3):
            part = lax.reduce_precision(vector, 8, 7)
            parts.append(part.astype(low))
            vector = vector - part
        return as_rows(jnp.concatenate(parts), cut)

    def both_layers(make):
        zero, one = make(0), make(1)
        keep = jnp.where(first, zero, one)
        came = swap_cores(jnp.where(first, one, zero))
        return jnp.where(first, keep, came), jnp.where(first, came, keep)

    def layer_params(rows_of_small):
        size = (CONV + 1) * half + half + 3 * step_half + (CONV + 1) * 2 * STATE
        three = rows_of_small.reshape(tp_count, -1)[:, : 3 * size].reshape(tp_count, 3, size)
        part = jnp.sum(three.astype(full), axis=1)
        at = (CONV + 1) * half
        taps_inner = jnp.moveaxis(part[:, :at].reshape(tp_count, CONV + 1, half), 0, 1)
        gains = part[:, at : at + half].reshape(-1)
        at += half
        scalars = []
        for _ in range(3):
            scalars.append(part[:, at : at + step_half].reshape(-1))
            at += step_half
        taps_state = part[0, at:].reshape(CONV + 1, 2 * STATE)
        taps = columns([taps_inner.reshape(CONV + 1, inner), taps_state])
        return taps, scalars[0], scalars[1], scalars[2], gains

    cut = half + quarter + wide
    middle = tp_count // 2

    def gather_item(part, sections):
        def side(pieces):
            parts, at = [], 0
            for size in sections:
                parts.append(columns(pieces[..., at : at + size]))
                at += size
            return columns(parts)

        half_a, half_b = gather_rows(side(part[:middle]), side(part[middle:]))
        result, at = [], 0
        for size in sections:
            result.append((half_a[:, at : at + middle * size], half_b[:, at : at + middle * size]))
            at += middle * size
        return result

    def feed_weights(parts):
        tails = [side.reshape(-1, middle, wide)[:, :, :step_half].reshape(-1, heads // 2) for side in parts[2]]
        gain = parts[2][0][:, step_half].astype(full)
        steps = jnp.pad(columns(tails), ((0, 0), (0, LANES - heads)))
        return columns(parts[0] + parts[1] + (steps,)), gain

    own_acts = lax.dynamic_index_in_dim(acts[:, 0], lane, 0, False)
    before = shifted(own_acts[rows - RIM :], "ctx", 1)
    smalls = both_layers(pack_small)
    packs = both_layers(pack)
    feed_sections, pair_sections = (half, quarter, wide), (half, half)
    along_feed = ring_gather(jnp.concatenate([packs[0][:, :cut], smalls[0]], axis=0), "tp")
    pair_pack, along_feed = tied(packs[0][:, cut:], along_feed)
    along_pair = ring_gather(pair_pack, "tp")
    feed_parts = gather_item(along_feed[:, :own_rows], feed_sections)
    last_pack, along_pair = tied(packs[1], along_pair)
    small_pad = jnp.pad(smalls[1], ((0, 0), (0, last_pack.shape[1] - cut)))
    along_last = ring_gather(jnp.concatenate([last_pack, small_pad], axis=0), "tp")
    pair_parts = gather_item(along_pair, pair_sections)
    along_last, pair_parts = tied(along_last, pair_parts)
    last_parts = gather_item(along_last[:, :own_rows, :cut], feed_sections)
    along_last, last_parts = tied(along_last, last_parts)
    last_parts += gather_item(along_last[:, :own_rows, cut:], pair_sections)
    feed_first, gain_first = feed_weights(feed_parts)
    feed_last, gain_last = feed_weights(last_parts[:3])
    weights = [
        (feed_first, columns(pair_parts[0]), columns(pair_parts[1])),
        (feed_last, columns(last_parts[3]), columns(last_parts[4])),
    ]
    params = [
        (gain_first,) + layer_params(along_feed[:, own_rows:]),
        (gain_last,) + layer_params(along_last[:, own_rows:, :cut]),
    ]

    places = lax.axis_index("ctx") * rows + jnp.arange(rows, dtype=jnp.int32)
    length = lax.dynamic_index_in_dim(lengths[:, 0], lane, 0, False)
    valid = (places < length).astype(full)[:, None]
    hidden = own_acts.astype(full)
    out_grad = lax.dynamic_index_in_dim(cotangent[:, 0], lane, 0, False)

    result_first, kept_first = layer_forward(hidden, before, valid, weights[0], params[0])
    low_first = result_first.astype(low)
    before = shifted(low_first[rows - RIM :], "ctx", 1)
    result_last, kept_last = layer_forward(low_first.astype(full), before, valid, weights[1], params[1])
    own_result = jnp.where(first, low_first, result_last.astype(low))
    quarter_rows = rows // tp_count
    section_out = spread_rows(own_result.reshape(tp_count, quarter_rows, width), (0, 1))

    delta_last, feed_last, small_last, pair_last = layer_backward(
        out_grad, valid, weights[1], params[1], kept_last
    )
    last = split_reduction(feed_last)
    last.first()
    spread_last = spread_rows(delta_last.astype(low).reshape(tp_count, quarter_rows, width), (1,))
    incoming = (out_grad + delta_last).astype(low).astype(full)
    delta_first, feed_first, small_first, pair_first = layer_backward(
        incoming, valid, weights[0], params[0], kept_first, (pair_last, last)
    )
    grad_first = (incoming + delta_first).astype(low)
    feed_first, (grad_first, pair_first.sums) = tied(feed_first, (grad_first, pair_first.sums))
    feed = split_reduction(feed_first)
    feed.first()
    pair_first_sum = pair_sum(pair_first.sums)
    small = jnp.stack([small_first, small_last])
    spread_first = spread_rows(grad_first.reshape(tp_count, quarter_rows, width), (0,))
    small = all_sum(all_sum(small, "ctx"), "dp")
    feed.second()
    feed_sums = feed_sum(feed.sums, inner, small.astype(low).reshape(-1))
    own_cotangent = lax.dynamic_slice_in_dim(
        cotangent[:, 0], lane * quarter_rows, quarter_rows, 1
    )
    input_grad = jnp.where(
        first, spread_first.astype(full), own_cotangent + spread_last.astype(full)
    )

    pair_keep = jnp.where(first, pair_first_sum, pair_last.sums)
    pair_came = swap_cores(jnp.where(first, pair_last.sums, pair_first_sum))
    size = small_first.shape[0]
    small_sums = feed_sums[own_rows:].reshape(-1)[: 2 * size].reshape(2, size)
    sums_last = last.sums
    total_width = sums_last.shape[1]
    joined = [
        jnp.concatenate([sums, as_rows(vector, total_width)])
        for sums, vector in zip((feed_sums[:own_rows], sums_last), small_sums)
    ]
    keep = jnp.where(first, joined[0], joined[1])
    came = swap_cores(jnp.where(first, joined[1], joined[0]))
    small_keep = keep[own_rows:].reshape(-1)[:size]
    small_came = came[own_rows:].reshape(-1)[:size]
    keep, came = keep[:own_rows], came[:own_rows]

    def halves(kept_part, came_part, axis):
        zero = jnp.where(first, kept_part, came_part)
        one = jnp.where(first, came_part, kept_part)
        return jnp.concatenate([zero, one], axis=axis)

    def own_lane(value, shape, axis):
        return lax.dynamic_index_in_dim(value.reshape(shape), lane, axis, False)

    grad_gate = halves(pair_keep[:, :half], pair_came[:, :half], 1)
    grad_out = halves(pair_keep[:, half:].T, pair_came[:, half:].T, 0)
    at = 0
    grad_x = halves(keep[:, at : at + half], came[:, at : at + half], 1)
    at += half
    grad_state = keep[:, at : at + 2 * STATE] + came[:, at : at + 2 * STATE]
    at += 2 * STATE + lane * step_half
    grad_step = halves(
        lax.dynamic_slice_in_dim(keep, at, step_half, 1), lax.dynamic_slice_in_dim(came, at, step_half, 1), 1
    )
    grad_gate_x = jnp.stack([grad_gate, grad_x], axis=1)

    at = (CONV + 1) * inner
    taps_shape = (CONV + 1, tp_count, half)
    grad_conv_inner = halves(
        own_lane(small_keep[:at], taps_shape, 1), own_lane(small_came[:at], taps_shape, 1), 1
    )
    end = at + (CONV + 1) * 2 * STATE
    grad_conv_state = (small_keep[at:end] + small_came[at:end]).reshape(CONV + 1, 2 * STATE)
    at = end
    vectors = []
    for size in (inner, heads, heads, heads):
        shape = (tp_count, size // tp_count)
        vectors.append(
            halves(
                own_lane(small_keep[at : at + size], shape, 0),
                own_lane(small_came[at : at + size], shape, 0),
                0,
            )
        )
        at += size
    owner = lax.axis_index("dp") * lax.axis_size("ctx") + lax.axis_index("ctx")
    grad_norm_gain = lax.dynamic_slice_in_dim(small_keep[at:], owner * own_rows, own_rows, 0)
    return (
        section_out[None, :, None],
        input_grad[None, :, None],
        grad_norm_gain[None],
        grad_gate_x[None],
        grad_state[None],
        grad_step[None],
        grad_conv_inner[None],
        grad_conv_state[None],
        vectors[1][None],
        vectors[2][None],
        vectors[3][None],
        vectors[0][None],
        grad_out[None],
    )


def solution(mesh):
    placed = (
        P(None, "dp", "ctx", None),
        P(None, "dp", "ctx", None),
        P(None, "dp"),
        P("section", ("dp", "ctx")),
        P("section", ("dp", "ctx"), None, "tp"),
        P("section", ("dp", "ctx"), None),
        P("section", ("dp", "ctx"), "tp"),
        P("section", None, "tp"),
        P("section", None, None),
        P("section", "tp"),
        P("section", "tp"),
        P("section", "tp"),
        P("section", "tp"),
        P("section", "tp", ("dp", "ctx")),
    )
    return jax.shard_map(
        on_device,
        mesh=mesh,
        in_specs=placed,
        out_specs=(
            P("section", None, "dp", ("ctx", "tp"), None),
            P("section", None, "dp", ("ctx", "tp"), None),
            P("section", ("dp", "ctx")),
            P("section", ("dp", "ctx"), None, "tp"),
            P("section", ("dp", "ctx"), None),
            P("section", ("dp", "ctx"), "tp"),
            P("section", None, "tp"),
            P("section", None, None),
            P("section", "tp"),
            P("section", "tp"),
            P("section", "tp"),
            P("section", "tp"),
            P("section", "tp", ("dp", "ctx")),
        ),
        check_vma=False,
    )
```

```python
import functools

import jax
import jax.numpy as jnp
from jax import lax
from jax.experimental import pallas as pl
from jax.experimental.pallas import tpu as pltpu
from jax.sharding import PartitionSpec as P

HEADDIM = 64
STATE = 128
INNER = 2048
CONV = 4
CHUNK = 128
LANES = 128
RIM = 16

highest = lax.Precision.HIGHEST
epsilon = 1e-05
low = jnp.bfloat16
full = jnp.float32


def dot_nn(a, b, precision=None):
    return lax.dot_general(
        a, b, (((1,), (0,)), ((), ())), precision=precision, preferred_element_type=full
    )


def dot_nt(a, b, precision=None):
    return lax.dot_general(
        a, b, (((1,), (1,)), ((), ())), precision=precision, preferred_element_type=full
    )


def dot_tn(a, b, precision=None):
    return lax.dot_general(
        a, b, (((0,), (0,)), ((), ())), precision=precision, preferred_element_type=full
    )


def shifted(value, axis, steps):
    count = lax.axis_size(axis)
    first, last = (max(0, -steps), min(count, count - steps))
    return lax.ppermute(value, axis, [(source, source + steps) for source in range(first, last)])


def rotated(value, axis, steps):
    count = lax.axis_size(axis)
    return lax.ppermute(value, axis, [(i, (i + steps) % count) for i in range(count)])


def line_gather(value, axis, dim=0):
    count = lax.axis_size(axis)
    place = lax.axis_index(axis)
    if count == 1:
        return jnp.expand_dims(value, dim)
    if count == 2:
        other = rotated(value, axis, 1)
        first = place == 0
        return jnp.stack([jnp.where(first, value, other), jnp.where(first, other, value)], axis=dim)
    up = down = value
    before, after = [], []
    for _ in range(1, count):
        up = shifted(up, axis, 1)
        down = shifted(down, axis, -1)
        before.insert(0, up)
        after.append(down)
    line = jnp.stack(before + [value] + after, axis=dim)
    return lax.dynamic_slice_in_dim(line, count - 1 - place, count, dim)


def tp_gather(value):
    copies = jnp.broadcast_to(value, (lax.axis_size("tp"),) + value.shape)
    return lax.all_to_all(copies, "tp", 0, 0)


def tp_sum(blocks):
    return jnp.sum(lax.all_to_all(blocks, "tp", 0, 0).astype(full), axis=0)


def scatter_sum(pick, axis):
    count = lax.axis_size(axis)
    place = lax.axis_index(axis)
    total = pick(place).astype(full)
    for steps in range(1, count):
        total = total + rotated(pick((place + steps) % count), axis, steps).astype(full)
    return total


def all_sum(value, axis):
    total = value
    for steps in range(1, lax.axis_size(axis)):
        total = total + rotated(value, axis, steps)
    return total


def swap_cores(value):
    return lax.ppermute(value, "section", [(0, 1), (1, 0)])


def spread_rows(value):
    count = lax.axis_size("tp")
    return lax.all_to_all(value.reshape(count, value.shape[0] // count, value.shape[1]), "tp", 0, 0)


def gather_rows(early, late):
    width = early.shape[-1]
    half_a = line_gather(line_gather(early, "ctx"), "dp").reshape(-1, width)
    half_b = line_gather(line_gather(late, "dp"), "ctx", 1).reshape(-1, width)
    return half_a, half_b


def columns(pieces):
    return jnp.concatenate(list(pieces), axis=-1)


def as_rows(vector, width):
    rows = -(-vector.shape[0] // (16 * width)) * 16
    return jnp.pad(vector, (0, rows * width - vector.shape[0])).reshape(rows, width)


def tied(value, other):
    return lax.optimization_barrier((value, other))


def conv_taps_sum(taps_ref, rows_of):
    total = taps_ref[CONV : CONV + 1, :]
    for k in range(CONV):
        total = total + taps_ref[k : k + 1, :] * rows_of(k)
    return total


def prep_kernel(
    feed_ref, rim_ref, taps_ref, raw_ref, bias_ref, rate_ref,
    act_ref, dt_ref, cum_ref, cumt_ref, since_ref, local_ref,
    window, run,
):
    inner = local_ref.shape[0]

    @pl.when(pl.program_id(0) == 0)
    def _():
        window[:RIM, :] = rim_ref[...].astype(full)
        run[...] = jnp.zeros_like(run)
        local_ref[...] = jnp.zeros_like(local_ref)

    window[RIM:, :] = feed_ref[...].astype(full)
    pre = conv_taps_sum(taps_ref, lambda k: window[RIM - CONV + 1 + k : RIM - CONV + 1 + k + CHUNK, :])
    act = pre * jax.nn.sigmoid(pre)
    act_ref[...] = act
    window[:RIM, :] = window[CHUNK:, :]
    raw = raw_ref[...] + bias_ref[...]
    dt = jnp.maximum(raw, 0.0) + jnp.log1p(jnp.exp(-jnp.abs(raw)))
    row = lax.broadcasted_iota(jnp.int32, (CHUNK, CHUNK), 0)
    col = lax.broadcasted_iota(jnp.int32, (CHUNK, CHUNK), 1)
    cum = dot_nn((row >= col).astype(full), rate_ref[...] * dt, highest)
    dt_ref[...] = dt
    cum_ref[...] = cum
    cumt_ref[...] = cum.T[: cumt_ref.shape[0]]
    since_ref[...] = jnp.exp(run[0:1, :] + cum)
    end = cum[CHUNK - 1 : CHUNK, :]
    run[...] = run[...] + end
    weight = jnp.exp(end - cum) * dt
    shrink = jnp.exp(end)
    left = col < HEADDIM
    upper = row < HEADDIM
    b_low = act[:, inner : inner + STATE].astype(low)
    for pair in range(inner // LANES):
        h0, h1 = 2 * pair, 2 * pair + 1
        span = slice(pair * LANES, (pair + 1) * LANES)
        each = jnp.where(left, weight[:, h0 : h0 + 1], weight[:, h1 : h1 + 1])
        fresh = dot_tn((act[:, span] * each).astype(low), b_low)
        keep = jnp.where(upper, shrink[:, h0 : h0 + 1], shrink[:, h1 : h1 + 1])
        local_ref[span, :] = keep * local_ref[span, :] + fresh


def mixer_prep(feed, rim, taps, raw, bias, rate, heads):
    rows, channels = feed.shape
    inner = heads * HEADDIM
    lanes = pl.BlockSpec((CHUNK, LANES), lambda i: (i, 0))
    lane_row = pl.BlockSpec((1, LANES), lambda i: (0, 0))
    by_lane = jax.ShapeDtypeStruct((rows, LANES), full)
    return pl.pallas_call(
        prep_kernel,
        grid=(rows // CHUNK,),
        in_specs=[
            pl.BlockSpec((CHUNK, channels), lambda i: (i, 0)),
            pl.BlockSpec((RIM, channels), lambda i: (0, 0)),
            pl.BlockSpec((8, channels), lambda i: (0, 0)),
            lanes,
            lane_row,
            lane_row,
        ],
        out_specs=[
            pl.BlockSpec((CHUNK, channels), lambda i: (i, 0)),
            lanes,
            lanes,
            pl.BlockSpec((heads, CHUNK), lambda i: (0, i)),
            lanes,
            pl.BlockSpec((inner, STATE), lambda i: (0, 0)),
        ],
        out_shape=[
            jax.ShapeDtypeStruct((rows, channels), full),
            by_lane,
            by_lane,
            jax.ShapeDtypeStruct((heads, rows), full),
            by_lane,
            jax.ShapeDtypeStruct((inner, STATE), full),
        ],
        scratch_shapes=[pltpu.VMEM((CHUNK + RIM, channels), full), pltpu.VMEM((8, LANES), full)],
        compiler_params=pltpu.CompilerParams(
            dimension_semantics=("arbitrary",), vmem_limit_bytes=40 * 1024 * 1024
        ),
        cost_estimate=pl.CostEstimate(
            flops=rows * inner * 2 * STATE, bytes_accessed=rows * channels * 6, transcendentals=rows * channels
        ),
        name="mixer_prep",
    )(feed, rim, taps, raw, bias, rate)


def fwd_kernel(x_ref, bc_ref, dt_ref, cum_ref, cumt_ref, skip_ref, enter_ref, y_ref, start_ref, state):
    @pl.when(pl.program_id(0) == 0)
    def _():
        state[...] = enter_ref[...].astype(full)

    heads = cumt_ref.shape[0]
    start_ref[0] = state[...].astype(low)
    b_low = bc_ref[:, :STATE].astype(low)
    c_low = bc_ref[:, STATE:].astype(low)
    row = lax.broadcasted_iota(jnp.int32, (CHUNK, CHUNK), 0)
    col = lax.broadcasted_iota(jnp.int32, (CHUNK, CHUNK), 1)
    left = col < HEADDIM
    upper = row < HEADDIM
    masked = jnp.where(row >= col, dot_nt(c_low, b_low), 0.0)
    for pair in range(heads // 2):
        h0, h1 = 2 * pair, 2 * pair + 1
        span = slice(pair * LANES, (pair + 1) * LANES)
        cum0 = jnp.broadcast_to(cum_ref[:, h0 : h0 + 1], (CHUNK, CHUNK))
        cum1 = jnp.broadcast_to(cum_ref[:, h1 : h1 + 1], (CHUNK, CHUNK))
        w0 = jnp.exp(jnp.minimum(cum0 - cumt_ref[h0 : h0 + 1, :], 0.0)) * masked
        w1 = jnp.exp(jnp.minimum(cum1 - cumt_ref[h1 : h1 + 1, :], 0.0)) * masked
        weights = jnp.concatenate([w0.astype(low), w1.astype(low)], axis=1)
        x_pair = x_ref[:, span]
        u = x_pair * jnp.where(left, dt_ref[:, h0 : h0 + 1], dt_ref[:, h1 : h1 + 1])
        u_low = u.astype(low)
        zero = jnp.zeros_like(u_low)
        u_both = jnp.concatenate([jnp.where(left, u_low, zero), jnp.where(left, zero, u_low)], axis=0)
        cum_pair = jnp.where(left, cum0, cum1)
        s_pair = state[span, :]
        carried = jnp.exp(cum_pair) * dot_nt(c_low, s_pair.astype(low))
        y_ref[:, span] = dot_nn(weights, u_both) + carried + skip_ref[:, span] * x_pair
        end0 = cum_ref[CHUNK - 1 : CHUNK, h0 : h0 + 1]
        end1 = cum_ref[CHUNK - 1 : CHUNK, h1 : h1 + 1]
        ahead = jnp.exp(jnp.where(left, end0, end1) - cum_pair)
        fresh = dot_tn((u * ahead).astype(low), b_low)
        state[span, :] = jnp.exp(jnp.where(upper, end0, end1)) * s_pair + fresh


def bwd_kernel(
    x_ref, bc_ref, dt_ref, cum_ref, cumt_ref, skip_ref, dy_ref, start_ref, later_ref,
    feed_ref, before_ref, rim_ref, taps_ref, raw_ref, bias_ref, rate_ref, pick_ref,
    back_ref, first_ref, sums_ref, head_sums_ref,
    adjoint, dye, uw, xdu, dyi, udu, window, back,
):
    channels = feed_ref.shape[1]

    @pl.when(pl.program_id(0) == 0)
    def _():
        adjoint[...] = later_ref[...].astype(full)
        back[CHUNK:, :] = jnp.zeros((8, channels), full)
        sums_ref[...] = jnp.zeros_like(sums_ref)
        head_sums_ref[...] = jnp.zeros_like(head_sums_ref)

    at_start = pl.program_id(0) == pl.num_programs(0) - 1
    window[:RIM, :] = jnp.where(at_start, rim_ref[...].astype(full), before_ref[...].astype(full))
    window[RIM:, :] = feed_ref[...].astype(full)

    heads = cumt_ref.shape[0]
    inner = heads * HEADDIM
    b_low = bc_ref[:, :STATE].astype(low)
    c_low = bc_ref[:, STATE:].astype(low)
    row = lax.broadcasted_iota(jnp.int32, (CHUNK, CHUNK), 0)
    col = lax.broadcasted_iota(jnp.int32, (CHUNK, CHUNK), 1)
    left = col < HEADDIM
    causal = row >= col
    onward = (row <= col).astype(low)
    masked = jnp.where(causal, dot_nt(c_low, b_low), 0.0)
    d_affinity = jnp.zeros((CHUNK, CHUNK), full)
    dlog = jnp.zeros((CHUNK, LANES), full)
    for pair in range(heads // 2):
        h0, h1 = 2 * pair, 2 * pair + 1
        span = slice(pair * LANES, (pair + 1) * LANES)
        cum0 = jnp.broadcast_to(cum_ref[:, h0 : h0 + 1], (CHUNK, CHUNK))
        cum1 = jnp.broadcast_to(cum_ref[:, h1 : h1 + 1], (CHUNK, CHUNK))
        m0 = jnp.exp(jnp.minimum(cum0 - cumt_ref[h0 : h0 + 1, :], 0.0))
        m1 = jnp.exp(jnp.minimum(cum1 - cumt_ref[h1 : h1 + 1, :], 0.0))
        w0 = m0 * masked
        w1 = m1 * masked
        dt_pair = jnp.where(left, dt_ref[:, h0 : h0 + 1], dt_ref[:, h1 : h1 + 1])
        x_pair = x_ref[:, span]
        u = x_pair * dt_pair
        u_low = u.astype(low)
        dy_pair = dy_ref[:, span]
        dy_low = dy_pair.astype(low)
        zero = jnp.zeros_like(dy_low)
        dy_both = jnp.concatenate([jnp.where(left, dy_low, zero), jnp.where(left, zero, dy_low)], axis=0)
        dw = dot_nt(dy_both, u_low)
        dw0, dw1 = dw[:CHUNK], dw[CHUNK:]
        d_affinity = d_affinity + dw0 * m0 + dw1 * m1
        z_both = jnp.concatenate([(dw0 * w0).astype(low), (dw1 * w1).astype(low)], axis=1)
        reach = dot_nn(onward, z_both)
        k0 = jnp.sum(jnp.where(row > col, reach[:, :CHUNK], 0.0), axis=1, keepdims=True)
        k1 = jnp.sum(jnp.where(row > col, reach[:, CHUNK:], 0.0), axis=1, keepdims=True)
        dlog = jnp.where(col == h0, k0, jnp.where(col == h1, k1, dlog))
        w_both = jnp.concatenate([w0.astype(low), w1.astype(low)], axis=0)
        cum_pair = jnp.where(left, cum0, cum1)
        end0 = cum_ref[CHUNK - 1 : CHUNK, h0 : h0 + 1]
        end1 = cum_ref[CHUNK - 1 : CHUNK, h1 : h1 + 1]
        ahead = jnp.exp(jnp.where(left, end0, end1) - cum_pair)
        since = jnp.exp(cum_pair)
        du_state = ahead * dot_nt(b_low, adjoint[span, :].astype(low))
        du = dot_tn(w_both, dy_both) + du_state
        back[:CHUNK, span] = dt_pair * du + skip_ref[:, span] * dy_pair
        sums_ref[CONV + 1 : CONV + 2, span] += jnp.sum(x_pair * dy_pair, axis=0, keepdims=True)
        y_state = since * dot_nt(c_low, start_ref[0, span, :])
        xdu[:, span] = (x_pair * du).astype(low)
        dyi[:, span] = (dy_pair * y_state).astype(low)
        udu[:, span] = (u * du_state).astype(low)
        dye[:, span] = (dy_pair * since).astype(low)
        uw[:, span] = (u * ahead).astype(low)
    pick = pick_ref[...]
    ddt = dot_nn(xdu[...], pick)
    by_state = dot_nn(dyi[...], pick)
    by_later = dot_nn(udu[...], pick)
    adjoint_now = adjoint[...]
    start_now = start_ref[0]
    both = adjoint_now * start_now.astype(full)
    by_head = jnp.sum(both.reshape(heads, HEADDIM, STATE), axis=1)
    by_head = jnp.concatenate([by_head, jnp.zeros((LANES - heads, STATE), full)], axis=0)
    over = dot_nt(jnp.ones((8, STATE), full), by_head, highest)
    ends = jnp.exp(cum_ref[CHUNK - 1 : CHUNK, :])
    dlog = dlog + over[0:1] * ends
    dlog = dlog + dot_nn((row <= col).astype(full), by_state, highest)
    dlog = dlog + dot_nn((row > col).astype(full), by_later, highest)
    rate = rate_ref[...]
    step = (ddt + rate * dlog) * jax.nn.sigmoid(raw_ref[...] + bias_ref[...])
    back_ref[:, channels:] = step.astype(low)
    head_sums_ref[0:1, :] += jnp.sum(step, axis=0, keepdims=True)
    head_sums_ref[1:2, :] += jnp.sum(dlog * rate * dt_ref[...], axis=0, keepdims=True)
    d_aff = jnp.where(causal, d_affinity, 0.0).astype(low)
    back[:CHUNK, inner : inner + STATE] = dot_tn(d_aff, c_low) + dot_nn(uw[...], adjoint_now.astype(low))
    back[:CHUNK, inner + STATE :] = dot_nn(d_aff, b_low) + dot_nn(dye[...], start_now)
    fresh = dot_tn(dye[...], c_low)
    for pair in range(heads // 2):
        h0, h1 = 2 * pair, 2 * pair + 1
        span = slice(pair * LANES, (pair + 1) * LANES)
        shrink = jnp.where(row < HEADDIM, ends[:, h0 : h0 + 1], ends[:, h1 : h1 + 1])
        adjoint[span, :] = shrink * adjoint_now[span, :] + fresh[span, :]
    for group in range(channels // LANES):
        span = slice(group * LANES, (group + 1) * LANES)
        taken = [
            window[RIM - CONV + 1 + k : RIM - CONV + 1 + k + CHUNK, span] for k in range(CONV)
        ]
        pre = taps_ref[CONV : CONV + 1, span]
        for k in range(CONV):
            pre = pre + taps_ref[k : k + 1, span] * taken[k]
        sig = jax.nn.sigmoid(pre)
        back_pre = back[:CHUNK, span] * (sig * (1.0 + pre * (1.0 - sig)))
        back[:CHUNK, span] = back_pre
        for k in range(CONV):
            sums_ref[k : k + 1, span] += jnp.sum(back_pre * taken[k], axis=0, keepdims=True)
        sums_ref[CONV : CONV + 1, span] += jnp.sum(back_pre, axis=0, keepdims=True)
        total = taps_ref[CONV - 1 : CONV, span] * back_pre
        for k in range(CONV - 1):
            total = total + taps_ref[k : k + 1, span] * back[CONV - 1 - k : CONV - 1 - k + CHUNK, span]
        back_ref[:, span] = total.astype(low)
    back[CHUNK:, :] = back[:8, :]

    @pl.when(at_start)
    def _():
        first_ref[...] = back[:8, :]


def ssm_forward(act, dt, cum, cum_t, skip_row, entering):
    rows = act.shape[0]
    heads = cum_t.shape[0]
    inner = heads * HEADDIM
    blocks = rows // CHUNK
    return pl.pallas_call(
        fwd_kernel,
        grid=(blocks,),
        in_specs=[
            pl.BlockSpec((CHUNK, inner), lambda i: (i, 0)),
            pl.BlockSpec((CHUNK, 2 * STATE), lambda i: (i, inner // (2 * STATE))),
            pl.BlockSpec((CHUNK, LANES), lambda i: (i, 0)),
            pl.BlockSpec((CHUNK, LANES), lambda i: (i, 0)),
            pl.BlockSpec((heads, CHUNK), lambda i: (0, i)),
            pl.BlockSpec((1, inner), lambda i: (0, 0)),
            pl.BlockSpec((inner, STATE), lambda i: (0, 0)),
        ],
        out_specs=[
            pl.BlockSpec((CHUNK, inner), lambda i: (i, 0)),
            pl.BlockSpec((1, inner, STATE), lambda i: (i, 0, 0)),
        ],
        out_shape=[
            jax.ShapeDtypeStruct((rows, inner), full),
            jax.ShapeDtypeStruct((blocks, inner, STATE), low),
        ],
        scratch_shapes=[pltpu.VMEM((inner, STATE), full)],
        compiler_params=pltpu.CompilerParams(
            dimension_semantics=("arbitrary",), vmem_limit_bytes=40 * 1024 * 1024
        ),
        cost_estimate=pl.CostEstimate(
            flops=rows * inner * 2 * 4 * STATE,
            bytes_accessed=rows * inner * 10,
            transcendentals=rows * heads * CHUNK * 2,
        ),
        name="ssm_forward",
    )(act, act, dt, cum, cum_t, skip_row, entering)


def ssm_backward(act, dt, cum, cum_t, skip_row, dy, starts, later, feed, rim, taps, raw, bias, rate):
    rows, channels = feed.shape
    lane_row = pl.BlockSpec((1, LANES), lambda i: (0, 0))
    per_block = CHUNK // RIM
    channel = lax.broadcasted_iota(jnp.int32, (cum_t.shape[0] * HEADDIM, LANES), 0)
    pick = (channel // HEADDIM == lax.broadcasted_iota(jnp.int32, channel.shape, 1)).astype(low)
    heads = cum_t.shape[0]
    inner = heads * HEADDIM
    blocks = rows // CHUNK
    last = blocks - 1
    return pl.pallas_call(
        bwd_kernel,
        grid=(blocks,),
        in_specs=[
            pl.BlockSpec((CHUNK, inner), lambda i: (last - i, 0)),
            pl.BlockSpec((CHUNK, 2 * STATE), lambda i: (last - i, inner // (2 * STATE))),
            pl.BlockSpec((CHUNK, LANES), lambda i: (last - i, 0)),
            pl.BlockSpec((CHUNK, LANES), lambda i: (last - i, 0)),
            pl.BlockSpec((heads, CHUNK), lambda i: (0, last - i)),
            pl.BlockSpec((1, inner), lambda i: (0, 0)),
            pl.BlockSpec((CHUNK, inner), lambda i: (last - i, 0)),
            pl.BlockSpec((1, inner, STATE), lambda i: (last - i, 0, 0)),
            pl.BlockSpec((inner, STATE), lambda i: (0, 0)),
            pl.BlockSpec((CHUNK, channels), lambda i: (last - i, 0)),
            pl.BlockSpec((RIM, channels), lambda i: (jnp.maximum((last - i) * per_block - 1, 0), 0)),
            pl.BlockSpec((RIM, channels), lambda i: (0, 0)),
            pl.BlockSpec((8, channels), lambda i: (0, 0)),
            pl.BlockSpec((CHUNK, LANES), lambda i: (last - i, 0)),
            lane_row,
            lane_row,
            pl.BlockSpec((inner, LANES), lambda i: (0, 0)),
        ],
        out_specs=[
            pl.BlockSpec((CHUNK, channels + LANES), lambda i: (last - i, 0)),
            pl.BlockSpec((8, channels), lambda i: (0, 0)),
            pl.BlockSpec((8, channels), lambda i: (0, 0)),
            pl.BlockSpec((8, LANES), lambda i: (0, 0)),
        ],
        out_shape=[
            jax.ShapeDtypeStruct((rows, channels + LANES), low),
            jax.ShapeDtypeStruct((8, channels), full),
            jax.ShapeDtypeStruct((8, channels), full),
            jax.ShapeDtypeStruct((8, LANES), full),
        ],
        scratch_shapes=[
            pltpu.VMEM((inner, STATE), full),
            pltpu.VMEM((CHUNK, inner), low),
            pltpu.VMEM((CHUNK, inner), low),
            pltpu.VMEM((CHUNK, inner), low),
            pltpu.VMEM((CHUNK, inner), low),
            pltpu.VMEM((CHUNK, inner), low),
            pltpu.VMEM((CHUNK + RIM, channels), full),
            pltpu.VMEM((CHUNK + 8, channels), full),
        ],
        compiler_params=pltpu.CompilerParams(
            dimension_semantics=("arbitrary",), vmem_limit_bytes=40 * 1024 * 1024
        ),
        cost_estimate=pl.CostEstimate(
            flops=rows * inner * 2 * 16 * STATE,
            bytes_accessed=rows * inner * 16,
            transcendentals=rows * heads * CHUNK * 2,
        ),
        name="ssm_backward",
    )(act, act, dt, cum, cum_t, skip_row, dy, starts, later, feed, feed, rim, taps, raw, bias, rate, pick)


def heads_to_channels(values):
    heads = values.shape[1]
    head = lax.broadcasted_iota(jnp.int32, (heads, heads * HEADDIM), 0)
    channel = lax.broadcasted_iota(jnp.int32, (heads, heads * HEADDIM), 1)
    return dot_nn(values, (channel // HEADDIM == head).astype(full), highest)


def silu_slope(value, sig):
    return sig * (1.0 + value * (1.0 - sig))


def layer_forward(hidden, before, valid, weights, params):
    gain, taps, step_bias, decay_log, skip, out_gain = params
    feed_weight, gate_weight, out_weight = weights
    rows, width = hidden.shape
    heads = step_bias.shape[0]
    inner = heads * HEADDIM
    channels = inner + 2 * STATE
    norm = lax.rsqrt(jnp.mean(hidden * hidden, axis=-1, keepdims=True) + epsilon)
    normed = (hidden * norm * gain).astype(low)
    feed_all = dot_nn(normed, feed_weight)
    feed = feed_all[:, :channels].astype(low)
    raw = feed_all[:, channels:]
    before = before.astype(full)
    before_norm = lax.rsqrt(jnp.mean(before * before, axis=-1, keepdims=True) + epsilon)
    rim = dot_nn((before * before_norm * gain).astype(low), feed_weight[:, :channels]).astype(low)
    gate = dot_nn(normed, gate_weight)
    lanes = ((0, 0), (0, LANES - heads))
    bias = jnp.pad(step_bias[None], lanes)
    rate = jnp.pad(-jnp.exp(decay_log)[None], lanes)
    taps = jnp.pad(taps, ((0, 8 - CONV - 1), (0, 0)))
    act, dt, cum, cum_t, since, local_state = mixer_prep(feed, rim, taps, raw, bias, rate, heads)
    shrink = jnp.repeat(since[rows - 1, :heads], HEADDIM)[:, None]
    entering = chain(local_state, shrink, 1)
    skip_row = jnp.repeat(skip, HEADDIM)[None]
    scan = (act, dt, cum, cum_t, skip_row)
    conv = (feed, rim, taps, raw, bias, rate)
    ssm_out, starts = ssm_forward(*scan, entering)
    gated = ssm_out * (gate * jax.nn.sigmoid(gate))
    squares = jnp.sum(gated * gated, axis=-1)
    scaled = (gated * out_gain).astype(low)
    term = dot_nt(scaled, out_weight).astype(low)
    branch = term.astype(full) + swap_cores(term).astype(full)
    squares = squares + swap_cores(squares)
    out_norm = lax.rsqrt(squares / INNER + epsilon)[:, None]
    result = hidden + valid * out_norm * branch
    kept = (
        hidden, norm, normed, act, gate, since, shrink,
        scan, conv, starts, ssm_out, scaled, branch.astype(low), out_norm,
    )
    return result, kept


def chain(local_state, shrink, steps):
    entering = shifted(local_state.astype(low), "ctx", steps)
    for _ in range(lax.axis_size("ctx") - 2):
        leaving = shrink * entering.astype(full) + local_state
        entering = shifted(leaving.astype(low), "ctx", steps)
    return entering


def layer_backward(incoming, valid, weights, params, kept, pending=None):
    gain, taps, step_bias, decay_log, skip, out_gain = params
    feed_weight, gate_weight, out_weight = weights
    (
        hidden, norm, normed, act, gate, since, shrink,
        scan, conv, starts, ssm_out, scaled, branch, out_norm,
    ) = kept
    rows, width = hidden.shape
    heads = step_bias.shape[0]
    inner = heads * HEADDIM
    channels = inner + 2 * STATE
    back_branch = (valid * incoming).astype(low)
    back_normed = dot_nn(back_branch, out_weight)
    if pending is not None:
        pair, feed = pending
        back_normed, pair.sums = tied(back_normed, pair.sums)
        pair.sums = pair_sum(pair.sums)
    back_wide = back_branch.astype(full)
    grad_out = dot_tn((back_wide * out_norm).astype(low), scaled).astype(low)
    along = jnp.sum(back_wide * branch.astype(full), axis=-1, keepdims=True)
    sig = jax.nn.sigmoid(gate)
    silu = gate * sig
    gated = ssm_out * silu
    grad_out_gain = jnp.sum(back_normed * gated * out_norm, axis=0)
    back_gated = out_norm * out_gain * back_normed - gated * (out_norm**3 * along / INNER)
    back_ssm = back_gated * silu
    back_gate = (back_gated * ssm_out * silu_slope(gate, sig)).astype(low)
    grad_gate = dot_tn(normed, back_gate).astype(low)
    weighted = (back_ssm * heads_to_channels(since[:, :heads])).astype(low)
    local_adjoint = dot_tn(weighted, act[:, inner + STATE :].astype(low))
    later = chain(local_adjoint, shrink, -1)
    early = whole_reduction(grad_gate, grad_out)
    if pending is not None:
        back_ssm, feed.sums = tied(back_ssm, feed.sums)
        feed.second()
    early.first()
    back_all, first_rows, sums, head_sums = ssm_backward(*scan, back_ssm, starts, later, *conv)
    following = shifted(first_rows, "ctx", -1)
    taps = conv[2]
    edge = sum(
        jnp.pad(taps[k] * following[: CONV - 1 - k], ((RIM - CONV + 1 + k, 0), (0, LANES))) for k in range(CONV - 1)
    )
    back_all = lax.dynamic_update_slice_in_dim(
        back_all, (back_all[rows - RIM :].astype(full) + edge).astype(low), rows - RIM, 0
    )
    back_all, early.sums = tied(back_all, early.sums)
    if pending is not None:
        back_all, (pair.sums, feed.sums) = tied(back_all, (pair.sums, feed.sums))
        feed.sums = feed_sum(feed.sums, inner)
    early.second()
    grad_skip = jnp.sum(sums[CONV + 1, :inner].reshape(heads, HEADDIM), axis=1)
    grad_step_bias, grad_decay = head_sums[0, :heads], head_sums[1, :heads]
    grad_taps = sums[: CONV + 1]
    term = (dot_nt(back_all, feed_weight) + dot_nt(back_gate, gate_weight)).astype(low)
    back_in = term.astype(full) + swap_cores(term).astype(full)
    grad_feed = dot_tn(normed, back_all).astype(low)
    grad_gain = jnp.sum(back_in * hidden * norm, axis=0)
    scaled_in = back_in * gain
    along_in = jnp.sum(scaled_in * hidden, axis=-1, keepdims=True)
    delta = norm * scaled_in - hidden * (norm**3 * along_in / width)
    small = jnp.concatenate(
        [
            grad_taps[:, :inner].reshape(-1), grad_taps[:, inner:].reshape(-1),
            grad_out_gain, grad_step_bias, grad_decay, grad_skip, grad_gain,
        ]
    )
    return delta, grad_feed, small, early


class Reduction:
    def __init__(self, half_a, half_b):
        self.half_a, self.half_b = half_a, half_b

    def first(self):
        ndp, nctx = lax.axis_size("dp"), lax.axis_size("ctx")

        def rows_of(half, owners):
            array, low_row, high_row = half
            each = array.shape[0] // (ndp * nctx)
            return jnp.concatenate(
                [
                    lax.dynamic_slice_in_dim(array, owner * each + low_row, high_row - low_row, 0)
                    for owner in owners
                ],
                axis=0,
            )

        self.sums = (
            scatter_sum(
                lambda at: rows_of(self.half_a, [i * nctx + at for i in range(ndp)]), "ctx"
            ).astype(low),
            scatter_sum(
                lambda at: rows_of(self.half_b, [at * nctx + j for j in range(nctx)]), "dp"
            ).astype(low),
        )

    def second(self):
        def own(value, axis):
            each = value.shape[0] // lax.axis_size(axis)
            return scatter_sum(
                lambda at: lax.dynamic_slice_in_dim(value, at * each, each, 0), axis
            ).astype(low)

        self.sums = own(self.sums[0], "dp"), own(self.sums[1], "ctx")


def whole_reduction(first, second):
    rows = first.shape[0] // (lax.axis_size("dp") * lax.axis_size("ctx"))
    return Reduction((first, 0, rows), (second, 0, rows))


def split_reduction(array):
    rows = array.shape[0] // (lax.axis_size("dp") * lax.axis_size("ctx"))
    return Reduction((array, 0, rows // 2), (array, rows // 2, rows))


def lane_blocks(value, inner):
    each = inner // lax.axis_size("tp")
    return jnp.stack([value[:, at : at + each] for at in range(0, inner, each)])


def pair_sum(sums):
    return tp_sum(columns(lane_blocks(part, part.shape[1]) for part in sums))


def feed_sum(sums, inner, small=None):
    joined = jnp.concatenate(sums, axis=0)
    rest = joined[:, inner:]
    count = lax.axis_size("tp")
    blocks = columns([lane_blocks(joined, inner), jnp.broadcast_to(rest, (count,) + rest.shape)])
    if small is not None:
        extra = as_rows(small, blocks.shape[2])
        blocks = jnp.concatenate([blocks, jnp.broadcast_to(extra, (count,) + extra.shape)], axis=1)
    return tp_sum(blocks)


def on_device(
    acts,
    cotangent,
    lengths,
    norm_gain,
    proj_gate_x,
    proj_state,
    proj_step,
    conv_inner,
    conv_state,
    step_bias,
    decay_log,
    skip_weight,
    out_gain,
    proj_out,
):
    micro_count, rows, width = (acts.shape[0], acts.shape[2], acts.shape[3])
    tp_count = lax.axis_size("tp")
    core = lax.axis_index("section")
    lane = lax.axis_index("tp")
    first = core == 0
    own_rows = proj_gate_x.shape[1]
    half = proj_gate_x.shape[3] // 2
    step_half = proj_step.shape[2] // 2
    heads = step_half * tp_count
    inner = half * tp_count
    quarter = 2 * STATE // tp_count
    wide = quarter

    state_part = lax.dynamic_slice_in_dim(proj_state[0], lane * quarter, quarter, 1)

    def pack(c):
        step = proj_step[0, :, c * step_half : (c + 1) * step_half]
        tail = jnp.pad(columns([step, norm_gain[0][:, None]]), ((0, 0), (0, wide - step_half - 1)))
        return columns(
            [
                proj_gate_x[0, :, 1, c * half : (c + 1) * half],
                state_part,
                tail,
                proj_gate_x[0, :, 0, c * half : (c + 1) * half],
                proj_out[0, c * half : (c + 1) * half].T,
            ]
        )

    def pack_small(c):
        vector = jnp.concatenate(
            [
                conv_inner[0, :, c * half : (c + 1) * half].reshape(-1),
                out_gain[0, c * half : (c + 1) * half],
                step_bias[0, c * step_half : (c + 1) * step_half],
                decay_log[0, c * step_half : (c + 1) * step_half],
                skip_weight[0, c * step_half : (c + 1) * step_half],
                conv_state[0].reshape(-1),
            ]
        )
        parts = []
        for _ in range(3):
            part = lax.reduce_precision(vector, 8, 7)
            parts.append(part.astype(low))
            vector = vector - part
        return as_rows(jnp.concatenate(parts), cut)

    def both_layers(make):
        zero, one = make(0), make(1)
        keep = jnp.where(first, zero, one)
        came = swap_cores(jnp.where(first, one, zero))
        return jnp.where(first, keep, came), jnp.where(first, came, keep)

    def layer_params(rows_of_small):
        size = (CONV + 1) * half + half + 3 * step_half + (CONV + 1) * 2 * STATE
        three = rows_of_small.reshape(tp_count, -1)[:, : 3 * size].reshape(tp_count, 3, size)
        part = jnp.sum(three.astype(full), axis=1)
        at = (CONV + 1) * half
        taps_inner = jnp.moveaxis(part[:, :at].reshape(tp_count, CONV + 1, half), 0, 1)
        gains = part[:, at : at + half].reshape(-1)
        at += half
        scalars = []
        for _ in range(3):
            scalars.append(part[:, at : at + step_half].reshape(-1))
            at += step_half
        taps_state = part[0, at:].reshape(CONV + 1, 2 * STATE)
        taps = columns([taps_inner.reshape(CONV + 1, inner), taps_state])
        return taps, scalars[0], scalars[1], scalars[2], gains

    cut = half + quarter + wide
    middle = tp_count // 2

    def gather_item(part, sections):
        def side(pieces):
            parts, at = [], 0
            for size in sections:
                parts.append(columns(pieces[..., at : at + size]))
                at += size
            return columns(parts)

        half_a, half_b = gather_rows(side(part[:middle]), side(part[middle:]))
        result, at = [], 0
        for size in sections:
            result.append((half_a[:, at : at + middle * size], half_b[:, at : at + middle * size]))
            at += middle * size
        return result

    def feed_weights(parts):
        tails = [side.reshape(-1, middle, wide)[:, :, :step_half].reshape(-1, heads // 2) for side in parts[2]]
        gain = parts[2][0][:, step_half].astype(full)
        steps = jnp.pad(columns(tails), ((0, 0), (0, LANES - heads)))
        return columns(parts[0] + parts[1] + (steps,)), gain

    own_acts = lax.dynamic_index_in_dim(acts[:, 0], lane, 0, False)
    before = shifted(own_acts[rows - RIM :], "ctx", 1)
    smalls = both_layers(pack_small)
    packs = both_layers(pack)
    feed_sections, pair_sections = (half, quarter, wide), (half, half)
    along_feed = tp_gather(jnp.concatenate([packs[0][:, :cut], smalls[0]], axis=0))
    pair_pack, along_feed = tied(packs[0][:, cut:], along_feed)
    along_pair = tp_gather(pair_pack)
    feed_parts = gather_item(along_feed[:, :own_rows], feed_sections)
    last_pack, along_feed = tied(packs[1], along_feed)
    along_pair, feed_parts = tied(along_pair, feed_parts)
    small_pad = jnp.pad(smalls[1], ((0, 0), (0, last_pack.shape[1] - cut)))
    along_last = tp_gather(jnp.concatenate([last_pack, small_pad], axis=0))
    pair_parts = gather_item(along_pair, pair_sections)
    along_last, pair_parts = tied(along_last, pair_parts)
    last_parts = gather_item(along_last[:, :own_rows, :cut], feed_sections)
    along_last, last_parts = tied(along_last, last_parts)
    last_parts += gather_item(along_last[:, :own_rows, cut:], pair_sections)
    feed_first, gain_first = feed_weights(feed_parts)
    feed_last, gain_last = feed_weights(last_parts[:3])
    weights = [
        (feed_first, columns(pair_parts[0]), columns(pair_parts[1])),
        (feed_last, columns(last_parts[3]), columns(last_parts[4])),
    ]
    params = [
        (gain_first,) + layer_params(along_feed[:, own_rows:]),
        (gain_last,) + layer_params(along_last[:, own_rows:, :cut]),
    ]

    places = lax.axis_index("ctx") * rows + jnp.arange(rows, dtype=jnp.int32)
    length = lax.dynamic_index_in_dim(lengths[:, 0], lane, 0, False)
    valid = (places < length).astype(full)[:, None]
    hidden = own_acts.astype(full)
    out_grad = lax.dynamic_index_in_dim(cotangent[:, 0], lane, 0, False)

    result_first, kept_first = layer_forward(hidden, before, valid, weights[0], params[0])
    low_first = result_first.astype(low)
    before = shifted(low_first[rows - RIM :], "ctx", 1)
    result_last, kept_last = layer_forward(low_first.astype(full), before, valid, weights[1], params[1])
    own_result = jnp.where(first, low_first, result_last.astype(low))
    quarter_rows = rows // tp_count
    section_out = spread_rows(own_result)

    column = core * (width // 2)

    def half_columns(value):
        return lax.dynamic_slice_in_dim(value.astype(low), column, width // 2, 1)

    delta_last, feed_last, small_last, pair_last = layer_backward(
        out_grad, valid, weights[1], params[1], kept_last
    )
    last = split_reduction(feed_last)
    last.first()
    spread_last = spread_rows(half_columns(delta_last))
    incoming = (out_grad + delta_last).astype(low).astype(full)
    delta_first, feed_first, small_first, pair_first = layer_backward(
        incoming, valid, weights[0], params[0], kept_first, (pair_last, last)
    )
    grad_first = (incoming + delta_first).astype(low)
    feed_first, (grad_first, pair_first.sums) = tied(feed_first, (grad_first, pair_first.sums))
    feed = split_reduction(feed_first)
    feed.first()
    pair_first_sum = pair_sum(pair_first.sums)
    small = jnp.stack([small_first, small_last])
    spread_first = spread_rows(half_columns(grad_first))
    small = all_sum(all_sum(small, "ctx"), "dp")
    feed.second()
    feed_sums = feed_sum(feed.sums, inner, small.astype(low).reshape(-1))
    own_cotangent = lax.dynamic_slice_in_dim(
        cotangent[:, 0], lane * quarter_rows, quarter_rows, 1
    )
    spread_keep = jnp.where(first, spread_first, spread_last)
    spread_came = swap_cores(jnp.where(first, spread_last, spread_first))
    spread = columns(
        [jnp.where(first, spread_keep, spread_came), jnp.where(first, spread_came, spread_keep)]
    ).astype(full)
    input_grad = jnp.where(first, spread, own_cotangent + spread)

    pair_keep = jnp.where(first, pair_first_sum, pair_last.sums)
    pair_came = swap_cores(jnp.where(first, pair_last.sums, pair_first_sum))
    size = small_first.shape[0]
    small_sums = feed_sums[own_rows:].reshape(-1)[: 2 * size].reshape(2, size)
    sums_last = last.sums
    total_width = sums_last.shape[1]
    joined = [
        jnp.concatenate([sums, as_rows(vector, total_width)])
        for sums, vector in zip((feed_sums[:own_rows], sums_last), small_sums)
    ]
    keep = jnp.where(first, joined[0], joined[1])
    came = swap_cores(jnp.where(first, joined[1], joined[0]))
    small_keep = keep[own_rows:].reshape(-1)[:size]
    small_came = came[own_rows:].reshape(-1)[:size]
    keep, came = keep[:own_rows], came[:own_rows]

    def halves(kept_part, came_part, axis):
        zero = jnp.where(first, kept_part, came_part)
        one = jnp.where(first, came_part, kept_part)
        return jnp.concatenate([zero, one], axis=axis)

    def own_lane(value, shape, axis):
        return lax.dynamic_index_in_dim(value.reshape(shape), lane, axis, False)

    grad_gate = halves(pair_keep[:, :half], pair_came[:, :half], 1)
    grad_out = halves(pair_keep[:, half:].T, pair_came[:, half:].T, 0)
    at = 0
    grad_x = halves(keep[:, at : at + half], came[:, at : at + half], 1)
    at += half
    grad_state = keep[:, at : at + 2 * STATE] + came[:, at : at + 2 * STATE]
    at += 2 * STATE + lane * step_half
    grad_step = halves(
        lax.dynamic_slice_in_dim(keep, at, step_half, 1), lax.dynamic_slice_in_dim(came, at, step_half, 1), 1
    )
    grad_gate_x = jnp.stack([grad_gate, grad_x], axis=1)

    at = (CONV + 1) * inner
    taps_shape = (CONV + 1, tp_count, half)
    grad_conv_inner = halves(
        own_lane(small_keep[:at], taps_shape, 1), own_lane(small_came[:at], taps_shape, 1), 1
    )
    end = at + (CONV + 1) * 2 * STATE
    grad_conv_state = (small_keep[at:end] + small_came[at:end]).reshape(CONV + 1, 2 * STATE)
    at = end
    vectors = []
    for size in (inner, heads, heads, heads):
        shape = (tp_count, size // tp_count)
        vectors.append(
            halves(
                own_lane(small_keep[at : at + size], shape, 0),
                own_lane(small_came[at : at + size], shape, 0),
                0,
            )
        )
        at += size
    owner = lax.axis_index("dp") * lax.axis_size("ctx") + lax.axis_index("ctx")
    grad_norm_gain = lax.dynamic_slice_in_dim(small_keep[at:], owner * own_rows, own_rows, 0)
    return (
        section_out[None, :, None],
        input_grad[None, :, None],
        grad_norm_gain[None],
        grad_gate_x[None],
        grad_state[None],
        grad_step[None],
        grad_conv_inner[None],
        grad_conv_state[None],
        vectors[1][None],
        vectors[2][None],
        vectors[3][None],
        vectors[0][None],
        grad_out[None],
    )


def solution(mesh):
    placed = (
        P(None, "dp", "ctx", None),
        P(None, "dp", "ctx", None),
        P(None, "dp"),
        P("section", ("dp", "ctx")),
        P("section", ("dp", "ctx"), None, "tp"),
        P("section", ("dp", "ctx"), None),
        P("section", ("dp", "ctx"), "tp"),
        P("section", None, "tp"),
        P("section", None, None),
        P("section", "tp"),
        P("section", "tp"),
        P("section", "tp"),
        P("section", "tp"),
        P("section", "tp", ("dp", "ctx")),
    )
    return jax.shard_map(
        on_device,
        mesh=mesh,
        in_specs=placed,
        out_specs=(
            P("section", None, "dp", ("ctx", "tp"), None),
            P("section", None, "dp", ("ctx", "tp"), None),
            P("section", ("dp", "ctx")),
            P("section", ("dp", "ctx"), None, "tp"),
            P("section", ("dp", "ctx"), None),
            P("section", ("dp", "ctx"), "tp"),
            P("section", None, "tp"),
            P("section", None, None),
            P("section", "tp"),
            P("section", "tp"),
            P("section", "tp"),
            P("section", "tp"),
            P("section", "tp", ("dp", "ctx")),
        ),
        check_vma=False,
    )
```

```python
import functools

import jax
import jax.numpy as jnp
from jax import lax
from jax.experimental import pallas as pl
from jax.experimental.pallas import tpu as pltpu
from jax.sharding import PartitionSpec as P

HEADDIM = 64
STATE = 128
INNER = 2048
CONV = 4
CHUNK = 128
LANES = 128
RIM = 16

highest = lax.Precision.HIGHEST
epsilon = 1e-05
low = jnp.bfloat16
full = jnp.float32


def dot_nn(a, b, precision=None):
    return lax.dot_general(
        a, b, (((1,), (0,)), ((), ())), precision=precision, preferred_element_type=full
    )


def dot_nt(a, b, precision=None):
    return lax.dot_general(
        a, b, (((1,), (1,)), ((), ())), precision=precision, preferred_element_type=full
    )


def dot_tn(a, b, precision=None):
    return lax.dot_general(
        a, b, (((0,), (0,)), ((), ())), precision=precision, preferred_element_type=full
    )


def shifted(value, axis, steps):
    count = lax.axis_size(axis)
    first, last = (max(0, -steps), min(count, count - steps))
    return lax.ppermute(value, axis, [(source, source + steps) for source in range(first, last)])


def rotated(value, axis, steps):
    count = lax.axis_size(axis)
    return lax.ppermute(value, axis, [(i, (i + steps) % count) for i in range(count)])


def line_gather(value, axis, dim=0, after=None):
    count = lax.axis_size(axis)
    place = lax.axis_index(axis)
    if count == 1:
        return jnp.expand_dims(value, dim)
    if count == 2:
        other = rotated(value, axis, 1)
        if after is not None:
            other, _ = tied(other, after)
        first = place == 0
        return jnp.stack([jnp.where(first, value, other), jnp.where(first, other, value)], axis=dim)
    up = down = value
    before, after = [], []
    for _ in range(1, count):
        up = shifted(up, axis, 1)
        down = shifted(down, axis, -1)
        before.insert(0, up)
        after.append(down)
    line = jnp.stack(before + [value] + after, axis=dim)
    return lax.dynamic_slice_in_dim(line, count - 1 - place, count, dim)


def tp_gather(value):
    copies = jnp.broadcast_to(value, (lax.axis_size("tp"),) + value.shape)
    return lax.all_to_all(copies, "tp", 0, 0)


def tp_sum(blocks):
    return jnp.sum(lax.all_to_all(blocks, "tp", 0, 0).astype(full), axis=0)


def scatter_sum(pick, axis, after=None):
    count = lax.axis_size(axis)
    place = lax.axis_index(axis)
    total = pick(place).astype(full)
    for steps in range(1, count):
        arrived = rotated(pick((place + steps) % count), axis, steps)
        if after is not None:
            arrived, _ = tied(arrived, after)
        total = total + arrived.astype(full)
    return total


def all_sum(value, axis):
    total = value
    for steps in range(1, lax.axis_size(axis)):
        total = total + rotated(value, axis, steps)
    return total


def swap_cores(value):
    return lax.ppermute(value, "section", [(0, 1), (1, 0)])


def spread_rows(value):
    count = lax.axis_size("tp")
    return lax.all_to_all(value.reshape(count, value.shape[0] // count, value.shape[1]), "tp", 0, 0)


def gather_rows(early, late, after):
    width = early.shape[-1]
    half_a = line_gather(line_gather(early, "ctx"), "dp", 0, after).reshape(-1, width)
    half_b = line_gather(line_gather(late, "dp"), "ctx", 1, after).reshape(-1, width)
    return half_a, half_b


def columns(pieces):
    return jnp.concatenate(list(pieces), axis=-1)


def as_rows(vector, width):
    rows = -(-vector.shape[0] // (16 * width)) * 16
    return jnp.pad(vector, (0, rows * width - vector.shape[0])).reshape(rows, width)


def tied(value, other):
    return lax.optimization_barrier((value, other))


def conv_taps_sum(taps_ref, rows_of):
    total = taps_ref[CONV : CONV + 1, :]
    for k in range(CONV):
        total = total + taps_ref[k : k + 1, :] * rows_of(k)
    return total


def prep_kernel(
    feed_ref, rim_ref, taps_ref, raw_ref, bias_ref, rate_ref,
    act_ref, dt_ref, cum_ref, cumt_ref, since_ref, local_ref,
    window, run,
):
    inner = local_ref.shape[0]

    @pl.when(pl.program_id(0) == 0)
    def _():
        window[:RIM, :] = rim_ref[...].astype(full)
        run[...] = jnp.zeros_like(run)
        local_ref[...] = jnp.zeros_like(local_ref)

    window[RIM:, :] = feed_ref[...].astype(full)
    pre = conv_taps_sum(taps_ref, lambda k: window[RIM - CONV + 1 + k : RIM - CONV + 1 + k + CHUNK, :])
    act = pre * jax.nn.sigmoid(pre)
    act_ref[...] = act
    window[:RIM, :] = window[CHUNK:, :]
    raw = raw_ref[...] + bias_ref[...]
    dt = jnp.maximum(raw, 0.0) + jnp.log1p(jnp.exp(-jnp.abs(raw)))
    row = lax.broadcasted_iota(jnp.int32, (CHUNK, CHUNK), 0)
    col = lax.broadcasted_iota(jnp.int32, (CHUNK, CHUNK), 1)
    cum = dot_nn((row >= col).astype(full), rate_ref[...] * dt, highest)
    dt_ref[...] = dt
    cum_ref[...] = cum
    cumt_ref[...] = cum.T[: cumt_ref.shape[0]]
    since_ref[...] = jnp.exp(run[0:1, :] + cum)
    end = cum[CHUNK - 1 : CHUNK, :]
    run[...] = run[...] + end
    weight = jnp.exp(end - cum) * dt
    shrink = jnp.exp(end)
    left = col < HEADDIM
    upper = row < HEADDIM
    b_low = act[:, inner : inner + STATE].astype(low)
    for pair in range(inner // LANES):
        h0, h1 = 2 * pair, 2 * pair + 1
        span = slice(pair * LANES, (pair + 1) * LANES)
        each = jnp.where(left, weight[:, h0 : h0 + 1], weight[:, h1 : h1 + 1])
        fresh = dot_tn((act[:, span] * each).astype(low), b_low)
        keep = jnp.where(upper, shrink[:, h0 : h0 + 1], shrink[:, h1 : h1 + 1])
        local_ref[span, :] = keep * local_ref[span, :] + fresh


def mixer_prep(feed, rim, taps, raw, bias, rate, heads):
    rows, channels = feed.shape
    inner = heads * HEADDIM
    lanes = pl.BlockSpec((CHUNK, LANES), lambda i: (i, 0))
    lane_row = pl.BlockSpec((1, LANES), lambda i: (0, 0))
    by_lane = jax.ShapeDtypeStruct((rows, LANES), full)
    return pl.pallas_call(
        prep_kernel,
        grid=(rows // CHUNK,),
        in_specs=[
            pl.BlockSpec((CHUNK, channels), lambda i: (i, 0)),
            pl.BlockSpec((RIM, channels), lambda i: (0, 0)),
            pl.BlockSpec((8, channels), lambda i: (0, 0)),
            lanes,
            lane_row,
            lane_row,
        ],
        out_specs=[
            pl.BlockSpec((CHUNK, channels), lambda i: (i, 0)),
            lanes,
            lanes,
            pl.BlockSpec((heads, CHUNK), lambda i: (0, i)),
            lanes,
            pl.BlockSpec((inner, STATE), lambda i: (0, 0)),
        ],
        out_shape=[
            jax.ShapeDtypeStruct((rows, channels), full),
            by_lane,
            by_lane,
            jax.ShapeDtypeStruct((heads, rows), full),
            by_lane,
            jax.ShapeDtypeStruct((inner, STATE), full),
        ],
        scratch_shapes=[pltpu.VMEM((CHUNK + RIM, channels), full), pltpu.VMEM((8, LANES), full)],
        compiler_params=pltpu.CompilerParams(
            dimension_semantics=("arbitrary",), vmem_limit_bytes=40 * 1024 * 1024
        ),
        cost_estimate=pl.CostEstimate(
            flops=rows * inner * 2 * STATE, bytes_accessed=rows * channels * 6, transcendentals=rows * channels
        ),
        name="mixer_prep",
    )(feed, rim, taps, raw, bias, rate)


def fwd_kernel(x_ref, bc_ref, dt_ref, cum_ref, cumt_ref, skip_ref, enter_ref, y_ref, start_ref, state):
    @pl.when(pl.program_id(0) == 0)
    def _():
        state[...] = enter_ref[...].astype(full)

    heads = cumt_ref.shape[0]
    start_ref[0] = state[...].astype(low)
    b_low = bc_ref[:, :STATE].astype(low)
    c_low = bc_ref[:, STATE:].astype(low)
    row = lax.broadcasted_iota(jnp.int32, (CHUNK, CHUNK), 0)
    col = lax.broadcasted_iota(jnp.int32, (CHUNK, CHUNK), 1)
    left = col < HEADDIM
    upper = row < HEADDIM
    masked = jnp.where(row >= col, dot_nt(c_low, b_low), 0.0)
    for pair in range(heads // 2):
        h0, h1 = 2 * pair, 2 * pair + 1
        span = slice(pair * LANES, (pair + 1) * LANES)
        cum0 = jnp.broadcast_to(cum_ref[:, h0 : h0 + 1], (CHUNK, CHUNK))
        cum1 = jnp.broadcast_to(cum_ref[:, h1 : h1 + 1], (CHUNK, CHUNK))
        w0 = jnp.exp(jnp.minimum(cum0 - cumt_ref[h0 : h0 + 1, :], 0.0)) * masked
        w1 = jnp.exp(jnp.minimum(cum1 - cumt_ref[h1 : h1 + 1, :], 0.0)) * masked
        weights = jnp.concatenate([w0.astype(low), w1.astype(low)], axis=1)
        x_pair = x_ref[:, span]
        u = x_pair * jnp.where(left, dt_ref[:, h0 : h0 + 1], dt_ref[:, h1 : h1 + 1])
        u_low = u.astype(low)
        zero = jnp.zeros_like(u_low)
        u_both = jnp.concatenate([jnp.where(left, u_low, zero), jnp.where(left, zero, u_low)], axis=0)
        cum_pair = jnp.where(left, cum0, cum1)
        s_pair = state[span, :]
        carried = jnp.exp(cum_pair) * dot_nt(c_low, s_pair.astype(low))
        y_ref[:, span] = dot_nn(weights, u_both) + carried + skip_ref[:, span] * x_pair
        end0 = cum_ref[CHUNK - 1 : CHUNK, h0 : h0 + 1]
        end1 = cum_ref[CHUNK - 1 : CHUNK, h1 : h1 + 1]
        ahead = jnp.exp(jnp.where(left, end0, end1) - cum_pair)
        fresh = dot_tn((u * ahead).astype(low), b_low)
        state[span, :] = jnp.exp(jnp.where(upper, end0, end1)) * s_pair + fresh


def bwd_kernel(
    x_ref, bc_ref, dt_ref, cum_ref, cumt_ref, skip_ref, dy_ref, start_ref, later_ref,
    feed_ref, before_ref, rim_ref, taps_ref, raw_ref, bias_ref, rate_ref, pick_ref,
    back_ref, first_ref, sums_ref, head_sums_ref,
    adjoint, dye, uw, xdu, dyi, udu, window, back,
):
    channels = feed_ref.shape[1]

    @pl.when(pl.program_id(0) == 0)
    def _():
        adjoint[...] = later_ref[...].astype(full)
        back[CHUNK:, :] = jnp.zeros((8, channels), full)
        sums_ref[...] = jnp.zeros_like(sums_ref)
        head_sums_ref[...] = jnp.zeros_like(head_sums_ref)

    at_start = pl.program_id(0) == pl.num_programs(0) - 1
    window[:RIM, :] = jnp.where(at_start, rim_ref[...].astype(full), before_ref[...].astype(full))
    window[RIM:, :] = feed_ref[...].astype(full)

    heads = cumt_ref.shape[0]
    inner = heads * HEADDIM
    b_low = bc_ref[:, :STATE].astype(low)
    c_low = bc_ref[:, STATE:].astype(low)
    row = lax.broadcasted_iota(jnp.int32, (CHUNK, CHUNK), 0)
    col = lax.broadcasted_iota(jnp.int32, (CHUNK, CHUNK), 1)
    left = col < HEADDIM
    causal = row >= col
    onward = (row <= col).astype(low)
    masked = jnp.where(causal, dot_nt(c_low, b_low), 0.0)
    d_affinity = jnp.zeros((CHUNK, CHUNK), full)
    dlog = jnp.zeros((CHUNK, LANES), full)
    for pair in range(heads // 2):
        h0, h1 = 2 * pair, 2 * pair + 1
        span = slice(pair * LANES, (pair + 1) * LANES)
        cum0 = jnp.broadcast_to(cum_ref[:, h0 : h0 + 1], (CHUNK, CHUNK))
        cum1 = jnp.broadcast_to(cum_ref[:, h1 : h1 + 1], (CHUNK, CHUNK))
        m0 = jnp.exp(jnp.minimum(cum0 - cumt_ref[h0 : h0 + 1, :], 0.0))
        m1 = jnp.exp(jnp.minimum(cum1 - cumt_ref[h1 : h1 + 1, :], 0.0))
        w0 = m0 * masked
        w1 = m1 * masked
        dt_pair = jnp.where(left, dt_ref[:, h0 : h0 + 1], dt_ref[:, h1 : h1 + 1])
        x_pair = x_ref[:, span]
        u = x_pair * dt_pair
        u_low = u.astype(low)
        dy_pair = dy_ref[:, span]
        dy_low = dy_pair.astype(low)
        zero = jnp.zeros_like(dy_low)
        dy_both = jnp.concatenate([jnp.where(left, dy_low, zero), jnp.where(left, zero, dy_low)], axis=0)
        dw = dot_nt(dy_both, u_low)
        dw0, dw1 = dw[:CHUNK], dw[CHUNK:]
        d_affinity = d_affinity + dw0 * m0 + dw1 * m1
        z_both = jnp.concatenate([(dw0 * w0).astype(low), (dw1 * w1).astype(low)], axis=1)
        reach = dot_nn(onward, z_both)
        k0 = jnp.sum(jnp.where(row > col, reach[:, :CHUNK], 0.0), axis=1, keepdims=True)
        k1 = jnp.sum(jnp.where(row > col, reach[:, CHUNK:], 0.0), axis=1, keepdims=True)
        dlog = jnp.where(col == h0, k0, jnp.where(col == h1, k1, dlog))
        w_both = jnp.concatenate([w0.astype(low), w1.astype(low)], axis=0)
        cum_pair = jnp.where(left, cum0, cum1)
        end0 = cum_ref[CHUNK - 1 : CHUNK, h0 : h0 + 1]
        end1 = cum_ref[CHUNK - 1 : CHUNK, h1 : h1 + 1]
        ahead = jnp.exp(jnp.where(left, end0, end1) - cum_pair)
        since = jnp.exp(cum_pair)
        du_state = ahead * dot_nt(b_low, adjoint[span, :].astype(low))
        du = dot_tn(w_both, dy_both) + du_state
        back[:CHUNK, span] = dt_pair * du + skip_ref[:, span] * dy_pair
        sums_ref[CONV + 1 : CONV + 2, span] += jnp.sum(x_pair * dy_pair, axis=0, keepdims=True)
        y_state = since * dot_nt(c_low, start_ref[0, span, :])
        xdu[:, span] = (x_pair * du).astype(low)
        dyi[:, span] = (dy_pair * y_state).astype(low)
        udu[:, span] = (u * du_state).astype(low)
        dye[:, span] = (dy_pair * since).astype(low)
        uw[:, span] = (u * ahead).astype(low)
    pick = pick_ref[...]
    ddt = dot_nn(xdu[...], pick)
    by_state = dot_nn(dyi[...], pick)
    by_later = dot_nn(udu[...], pick)
    adjoint_now = adjoint[...]
    start_now = start_ref[0]
    both = adjoint_now * start_now.astype(full)
    by_head = jnp.sum(both.reshape(heads, HEADDIM, STATE), axis=1)
    by_head = jnp.concatenate([by_head, jnp.zeros((LANES - heads, STATE), full)], axis=0)
    over = dot_nt(jnp.ones((8, STATE), full), by_head, highest)
    ends = jnp.exp(cum_ref[CHUNK - 1 : CHUNK, :])
    dlog = dlog + over[0:1] * ends
    dlog = dlog + dot_nn((row <= col).astype(full), by_state, highest)
    dlog = dlog + dot_nn((row > col).astype(full), by_later, highest)
    rate = rate_ref[...]
    step = (ddt + rate * dlog) * jax.nn.sigmoid(raw_ref[...] + bias_ref[...])
    back_ref[:, channels:] = step.astype(low)
    head_sums_ref[0:1, :] += jnp.sum(step, axis=0, keepdims=True)
    head_sums_ref[1:2, :] += jnp.sum(dlog * rate * dt_ref[...], axis=0, keepdims=True)
    d_aff = jnp.where(causal, d_affinity, 0.0).astype(low)
    back[:CHUNK, inner : inner + STATE] = dot_tn(d_aff, c_low) + dot_nn(uw[...], adjoint_now.astype(low))
    back[:CHUNK, inner + STATE :] = dot_nn(d_aff, b_low) + dot_nn(dye[...], start_now)
    fresh = dot_tn(dye[...], c_low)
    for pair in range(heads // 2):
        h0, h1 = 2 * pair, 2 * pair + 1
        span = slice(pair * LANES, (pair + 1) * LANES)
        shrink = jnp.where(row < HEADDIM, ends[:, h0 : h0 + 1], ends[:, h1 : h1 + 1])
        adjoint[span, :] = shrink * adjoint_now[span, :] + fresh[span, :]
    for group in range(channels // LANES):
        span = slice(group * LANES, (group + 1) * LANES)
        taken = [
            window[RIM - CONV + 1 + k : RIM - CONV + 1 + k + CHUNK, span] for k in range(CONV)
        ]
        pre = taps_ref[CONV : CONV + 1, span]
        for k in range(CONV):
            pre = pre + taps_ref[k : k + 1, span] * taken[k]
        sig = jax.nn.sigmoid(pre)
        back_pre = back[:CHUNK, span] * (sig * (1.0 + pre * (1.0 - sig)))
        back[:CHUNK, span] = back_pre
        for k in range(CONV):
            sums_ref[k : k + 1, span] += jnp.sum(back_pre * taken[k], axis=0, keepdims=True)
        sums_ref[CONV : CONV + 1, span] += jnp.sum(back_pre, axis=0, keepdims=True)
        total = taps_ref[CONV - 1 : CONV, span] * back_pre
        for k in range(CONV - 1):
            total = total + taps_ref[k : k + 1, span] * back[CONV - 1 - k : CONV - 1 - k + CHUNK, span]
        back_ref[:, span] = total.astype(low)
    back[CHUNK:, :] = back[:8, :]

    @pl.when(at_start)
    def _():
        first_ref[...] = back[:8, :]


def ssm_forward(act, dt, cum, cum_t, skip_row, entering):
    rows = act.shape[0]
    heads = cum_t.shape[0]
    inner = heads * HEADDIM
    blocks = rows // CHUNK
    return pl.pallas_call(
        fwd_kernel,
        grid=(blocks,),
        in_specs=[
            pl.BlockSpec((CHUNK, inner), lambda i: (i, 0)),
            pl.BlockSpec((CHUNK, 2 * STATE), lambda i: (i, inner // (2 * STATE))),
            pl.BlockSpec((CHUNK, LANES), lambda i: (i, 0)),
            pl.BlockSpec((CHUNK, LANES), lambda i: (i, 0)),
            pl.BlockSpec((heads, CHUNK), lambda i: (0, i)),
            pl.BlockSpec((1, inner), lambda i: (0, 0)),
            pl.BlockSpec((inner, STATE), lambda i: (0, 0)),
        ],
        out_specs=[
            pl.BlockSpec((CHUNK, inner), lambda i: (i, 0)),
            pl.BlockSpec((1, inner, STATE), lambda i: (i, 0, 0)),
        ],
        out_shape=[
            jax.ShapeDtypeStruct((rows, inner), full),
            jax.ShapeDtypeStruct((blocks, inner, STATE), low),
        ],
        scratch_shapes=[pltpu.VMEM((inner, STATE), full)],
        compiler_params=pltpu.CompilerParams(
            dimension_semantics=("arbitrary",), vmem_limit_bytes=40 * 1024 * 1024
        ),
        cost_estimate=pl.CostEstimate(
            flops=rows * inner * 2 * 4 * STATE,
            bytes_accessed=rows * inner * 10,
            transcendentals=rows * heads * CHUNK * 2,
        ),
        name="ssm_forward",
    )(act, act, dt, cum, cum_t, skip_row, entering)


def ssm_backward(act, dt, cum, cum_t, skip_row, dy, starts, later, feed, rim, taps, raw, bias, rate):
    rows, channels = feed.shape
    lane_row = pl.BlockSpec((1, LANES), lambda i: (0, 0))
    per_block = CHUNK // RIM
    channel = lax.broadcasted_iota(jnp.int32, (cum_t.shape[0] * HEADDIM, LANES), 0)
    pick = (channel // HEADDIM == lax.broadcasted_iota(jnp.int32, channel.shape, 1)).astype(low)
    heads = cum_t.shape[0]
    inner = heads * HEADDIM
    blocks = rows // CHUNK
    last = blocks - 1
    return pl.pallas_call(
        bwd_kernel,
        grid=(blocks,),
        in_specs=[
            pl.BlockSpec((CHUNK, inner), lambda i: (last - i, 0)),
            pl.BlockSpec((CHUNK, 2 * STATE), lambda i: (last - i, inner // (2 * STATE))),
            pl.BlockSpec((CHUNK, LANES), lambda i: (last - i, 0)),
            pl.BlockSpec((CHUNK, LANES), lambda i: (last - i, 0)),
            pl.BlockSpec((heads, CHUNK), lambda i: (0, last - i)),
            pl.BlockSpec((1, inner), lambda i: (0, 0)),
            pl.BlockSpec((CHUNK, inner), lambda i: (last - i, 0)),
            pl.BlockSpec((1, inner, STATE), lambda i: (last - i, 0, 0)),
            pl.BlockSpec((inner, STATE), lambda i: (0, 0)),
            pl.BlockSpec((CHUNK, channels), lambda i: (last - i, 0)),
            pl.BlockSpec((RIM, channels), lambda i: (jnp.maximum((last - i) * per_block - 1, 0), 0)),
            pl.BlockSpec((RIM, channels), lambda i: (0, 0)),
            pl.BlockSpec((8, channels), lambda i: (0, 0)),
            pl.BlockSpec((CHUNK, LANES), lambda i: (last - i, 0)),
            lane_row,
            lane_row,
            pl.BlockSpec((inner, LANES), lambda i: (0, 0)),
        ],
        out_specs=[
            pl.BlockSpec((CHUNK, channels + LANES), lambda i: (last - i, 0)),
            pl.BlockSpec((8, channels), lambda i: (0, 0)),
            pl.BlockSpec((8, channels), lambda i: (0, 0)),
            pl.BlockSpec((8, LANES), lambda i: (0, 0)),
        ],
        out_shape=[
            jax.ShapeDtypeStruct((rows, channels + LANES), low),
            jax.ShapeDtypeStruct((8, channels), full),
            jax.ShapeDtypeStruct((8, channels), full),
            jax.ShapeDtypeStruct((8, LANES), full),
        ],
        scratch_shapes=[
            pltpu.VMEM((inner, STATE), full),
            pltpu.VMEM((CHUNK, inner), low),
            pltpu.VMEM((CHUNK, inner), low),
            pltpu.VMEM((CHUNK, inner), low),
            pltpu.VMEM((CHUNK, inner), low),
            pltpu.VMEM((CHUNK, inner), low),
            pltpu.VMEM((CHUNK + RIM, channels), full),
            pltpu.VMEM((CHUNK + 8, channels), full),
        ],
        compiler_params=pltpu.CompilerParams(
            dimension_semantics=("arbitrary",), vmem_limit_bytes=40 * 1024 * 1024
        ),
        cost_estimate=pl.CostEstimate(
            flops=rows * inner * 2 * 16 * STATE,
            bytes_accessed=rows * inner * 16,
            transcendentals=rows * heads * CHUNK * 2,
        ),
        name="ssm_backward",
    )(act, act, dt, cum, cum_t, skip_row, dy, starts, later, feed, feed, rim, taps, raw, bias, rate, pick)


def heads_to_channels(values):
    heads = values.shape[1]
    head = lax.broadcasted_iota(jnp.int32, (heads, heads * HEADDIM), 0)
    channel = lax.broadcasted_iota(jnp.int32, (heads, heads * HEADDIM), 1)
    return dot_nn(values, (channel // HEADDIM == head).astype(full), highest)


def silu_slope(value, sig):
    return sig * (1.0 + value * (1.0 - sig))


def layer_forward(hidden, before, valid, weights, params):
    gain, taps, step_bias, decay_log, skip, out_gain = params
    feed_weight, gate_weight, out_weight = weights
    rows, width = hidden.shape
    heads = step_bias.shape[0]
    inner = heads * HEADDIM
    channels = inner + 2 * STATE
    norm = lax.rsqrt(jnp.mean(hidden * hidden, axis=-1, keepdims=True) + epsilon)
    normed = (hidden * norm * gain).astype(low)
    feed_all = dot_nn(normed, feed_weight)
    feed = feed_all[:, :channels].astype(low)
    raw = feed_all[:, channels:]
    before = before.astype(full)
    before_norm = lax.rsqrt(jnp.mean(before * before, axis=-1, keepdims=True) + epsilon)
    rim = dot_nn((before * before_norm * gain).astype(low), feed_weight[:, :channels]).astype(low)
    gate = dot_nn(normed, gate_weight)
    lanes = ((0, 0), (0, LANES - heads))
    bias = jnp.pad(step_bias[None], lanes)
    rate = jnp.pad(-jnp.exp(decay_log)[None], lanes)
    taps = jnp.pad(taps, ((0, 8 - CONV - 1), (0, 0)))
    act, dt, cum, cum_t, since, local_state = mixer_prep(feed, rim, taps, raw, bias, rate, heads)
    shrink = jnp.repeat(since[rows - 1, :heads], HEADDIM)[:, None]
    entering = chain(local_state, shrink, 1)
    skip_row = jnp.repeat(skip, HEADDIM)[None]
    scan = (act, dt, cum, cum_t, skip_row)
    conv = (feed, rim, taps, raw, bias, rate)
    ssm_out, starts = ssm_forward(*scan, entering)
    gated = ssm_out * (gate * jax.nn.sigmoid(gate))
    squares = jnp.sum(gated * gated, axis=-1)
    scaled = (gated * out_gain).astype(low)
    term = dot_nt(scaled, out_weight).astype(low)
    branch = term.astype(full) + swap_cores(term).astype(full)
    squares = squares + swap_cores(squares)
    out_norm = lax.rsqrt(squares / INNER + epsilon)[:, None]
    result = hidden + valid * out_norm * branch
    kept = (
        hidden, norm, normed, act, gate, since, shrink,
        scan, conv, starts, ssm_out, scaled, branch.astype(low), out_norm,
    )
    return result, kept


def chain(local_state, shrink, steps):
    entering = shifted(local_state.astype(low), "ctx", steps)
    for _ in range(lax.axis_size("ctx") - 2):
        leaving = shrink * entering.astype(full) + local_state
        entering = shifted(leaving.astype(low), "ctx", steps)
    return entering


def layer_backward(incoming, valid, weights, params, kept, beside, pending=None):
    gain, taps, step_bias, decay_log, skip, out_gain = params
    feed_weight, gate_weight, out_weight = weights
    (
        hidden, norm, normed, act, gate, since, shrink,
        scan, conv, starts, ssm_out, scaled, branch, out_norm,
    ) = kept
    rows, width = hidden.shape
    heads = step_bias.shape[0]
    inner = heads * HEADDIM
    channels = inner + 2 * STATE
    back_branch = (valid * incoming).astype(low)
    back_normed = dot_nn(back_branch, out_weight)
    if pending is not None:
        pair, feed = pending
        back_normed, pair.sums = tied(back_normed, pair.sums)
        pair.sums = pair_sum(pair.sums)
    back_wide = back_branch.astype(full)
    grad_out = dot_tn((back_wide * out_norm).astype(low), scaled).astype(low)
    along = jnp.sum(back_wide * branch.astype(full), axis=-1, keepdims=True)
    sig = jax.nn.sigmoid(gate)
    silu = gate * sig
    gated = ssm_out * silu
    grad_out_gain = jnp.sum(back_normed * gated * out_norm, axis=0)
    back_gated = out_norm * out_gain * back_normed - gated * (out_norm**3 * along / INNER)
    back_ssm = back_gated * silu
    back_gate = (back_gated * ssm_out * silu_slope(gate, sig)).astype(low)
    grad_gate = dot_tn(normed, back_gate).astype(low)
    weighted = (back_ssm * heads_to_channels(since[:, :heads])).astype(low)
    local_adjoint = dot_tn(weighted, act[:, inner + STATE :].astype(low))
    later = chain(local_adjoint, shrink, -1)
    early = whole_reduction(grad_gate, grad_out)
    if pending is not None:
        back_ssm, (feed.sums, beside) = tied(back_ssm, (feed.sums, beside))
        feed.second()
    early.first()
    back_all, first_rows, sums, head_sums = ssm_backward(*scan, back_ssm, starts, later, *conv)
    following = shifted(first_rows, "ctx", -1)
    taps = conv[2]
    edge = sum(
        jnp.pad(taps[k] * following[: CONV - 1 - k], ((RIM - CONV + 1 + k, 0), (0, LANES))) for k in range(CONV - 1)
    )
    back_all = lax.dynamic_update_slice_in_dim(
        back_all, (back_all[rows - RIM :].astype(full) + edge).astype(low), rows - RIM, 0
    )
    back_all, early.sums = tied(back_all, early.sums)
    if pending is not None:
        back_all, (pair.sums, feed.sums) = tied(back_all, (pair.sums, feed.sums))
        feed.sums = feed_sum(feed.sums, inner)
    else:
        back_all, beside = tied(back_all, beside)
    grad_skip = jnp.sum(sums[CONV + 1, :inner].reshape(heads, HEADDIM), axis=1)
    grad_step_bias, grad_decay = head_sums[0, :heads], head_sums[1, :heads]
    grad_taps = sums[: CONV + 1]
    term = (dot_nt(back_all, feed_weight) + dot_nt(back_gate, gate_weight)).astype(low)
    back_in = term.astype(full) + swap_cores(term).astype(full)
    grad_feed = dot_tn(normed, back_all).astype(low)
    grad_gain = jnp.sum(back_in * hidden * norm, axis=0)
    scaled_in = back_in * gain
    along_in = jnp.sum(scaled_in * hidden, axis=-1, keepdims=True)
    delta = norm * scaled_in - hidden * (norm**3 * along_in / width)
    small = jnp.concatenate(
        [
            grad_taps[:, :inner].reshape(-1), grad_taps[:, inner:].reshape(-1),
            grad_out_gain, grad_step_bias, grad_decay, grad_skip, grad_gain,
        ]
    )
    return delta, grad_feed, small, early, beside


class Reduction:
    def __init__(self, half_a, half_b):
        self.half_a, self.half_b = half_a, half_b

    def first(self, after=None):
        ndp, nctx = lax.axis_size("dp"), lax.axis_size("ctx")

        def rows_of(half, owners):
            array, low_row, high_row = half
            each = array.shape[0] // (ndp * nctx)
            return jnp.concatenate(
                [
                    lax.dynamic_slice_in_dim(array, owner * each + low_row, high_row - low_row, 0)
                    for owner in owners
                ],
                axis=0,
            )

        self.sums = (
            scatter_sum(
                lambda at: rows_of(self.half_a, [i * nctx + at for i in range(ndp)]), "ctx", after
            ).astype(low),
            scatter_sum(
                lambda at: rows_of(self.half_b, [at * nctx + j for j in range(nctx)]), "dp", after
            ).astype(low),
        )

    def second(self, after=None):
        def own(value, axis):
            each = value.shape[0] // lax.axis_size(axis)
            return scatter_sum(
                lambda at: lax.dynamic_slice_in_dim(value, at * each, each, 0), axis, after
            ).astype(low)

        self.sums = own(self.sums[0], "dp"), own(self.sums[1], "ctx")


def whole_reduction(first, second):
    rows = first.shape[0] // (lax.axis_size("dp") * lax.axis_size("ctx"))
    return Reduction((first, 0, rows), (second, 0, rows))


def split_reduction(array):
    rows = array.shape[0] // (lax.axis_size("dp") * lax.axis_size("ctx"))
    return Reduction((array, 0, rows // 2), (array, rows // 2, rows))


def lane_blocks(value, inner):
    each = inner // lax.axis_size("tp")
    return jnp.stack([value[:, at : at + each] for at in range(0, inner, each)])


def pair_sum(sums):
    return tp_sum(columns(lane_blocks(part, part.shape[1]) for part in sums))


def feed_sum(sums, inner, small=None):
    joined = jnp.concatenate(sums, axis=0)
    rest = joined[:, inner:]
    count = lax.axis_size("tp")
    blocks = columns([lane_blocks(joined, inner), jnp.broadcast_to(rest, (count,) + rest.shape)])
    if small is not None:
        extra = as_rows(small, blocks.shape[2])
        blocks = jnp.concatenate([blocks, jnp.broadcast_to(extra, (count,) + extra.shape)], axis=1)
    return tp_sum(blocks)


def on_device(
    acts,
    cotangent,
    lengths,
    norm_gain,
    proj_gate_x,
    proj_state,
    proj_step,
    conv_inner,
    conv_state,
    step_bias,
    decay_log,
    skip_weight,
    out_gain,
    proj_out,
):
    micro_count, rows, width = (acts.shape[0], acts.shape[2], acts.shape[3])
    tp_count = lax.axis_size("tp")
    core = lax.axis_index("section")
    lane = lax.axis_index("tp")
    first = core == 0
    own_rows = proj_gate_x.shape[1]
    half = proj_gate_x.shape[3] // 2
    step_half = proj_step.shape[2] // 2
    heads = step_half * tp_count
    inner = half * tp_count
    quarter = 2 * STATE // tp_count
    wide = quarter

    state_part = lax.dynamic_slice_in_dim(proj_state[0], lane * quarter, quarter, 1)

    def pack(c):
        step = proj_step[0, :, c * step_half : (c + 1) * step_half]
        tail = jnp.pad(columns([step, norm_gain[0][:, None]]), ((0, 0), (0, wide - step_half - 1)))
        return columns(
            [
                proj_gate_x[0, :, 1, c * half : (c + 1) * half],
                state_part,
                tail,
                proj_gate_x[0, :, 0, c * half : (c + 1) * half],
                proj_out[0, c * half : (c + 1) * half].T,
            ]
        )

    def pack_small(c):
        vector = jnp.concatenate(
            [
                conv_inner[0, :, c * half : (c + 1) * half].reshape(-1),
                out_gain[0, c * half : (c + 1) * half],
                step_bias[0, c * step_half : (c + 1) * step_half],
                decay_log[0, c * step_half : (c + 1) * step_half],
                skip_weight[0, c * step_half : (c + 1) * step_half],
                conv_state[0].reshape(-1),
            ]
        )
        parts = []
        for _ in range(3):
            part = lax.reduce_precision(vector, 8, 7)
            parts.append(part.astype(low))
            vector = vector - part
        return as_rows(jnp.concatenate(parts), cut)

    def both_layers(make):
        zero, one = make(0), make(1)
        keep = jnp.where(first, zero, one)
        came = swap_cores(jnp.where(first, one, zero))
        return jnp.where(first, keep, came), jnp.where(first, came, keep)

    def layer_params(rows_of_small):
        size = (CONV + 1) * half + half + 3 * step_half + (CONV + 1) * 2 * STATE
        three = rows_of_small.reshape(tp_count, -1)[:, : 3 * size].reshape(tp_count, 3, size)
        part = jnp.sum(three.astype(full), axis=1)
        at = (CONV + 1) * half
        taps_inner = jnp.moveaxis(part[:, :at].reshape(tp_count, CONV + 1, half), 0, 1)
        gains = part[:, at : at + half].reshape(-1)
        at += half
        scalars = []
        for _ in range(3):
            scalars.append(part[:, at : at + step_half].reshape(-1))
            at += step_half
        taps_state = part[0, at:].reshape(CONV + 1, 2 * STATE)
        taps = columns([taps_inner.reshape(CONV + 1, inner), taps_state])
        return taps, scalars[0], scalars[1], scalars[2], gains

    cut = half + quarter + wide
    middle = tp_count // 2

    def gather_item(part, sections, after=None):
        def side(pieces):
            parts, at = [], 0
            for size in sections:
                parts.append(columns(pieces[..., at : at + size]))
                at += size
            return columns(parts)

        half_a, half_b = gather_rows(side(part[:middle]), side(part[middle:]), after)
        result, at = [], 0
        for size in sections:
            result.append((half_a[:, at : at + middle * size], half_b[:, at : at + middle * size]))
            at += middle * size
        return result

    def feed_weights(parts):
        tails = [side.reshape(-1, middle, wide)[:, :, :step_half].reshape(-1, heads // 2) for side in parts[2]]
        gain = parts[2][0][:, step_half].astype(full)
        steps = jnp.pad(columns(tails), ((0, 0), (0, LANES - heads)))
        return columns(parts[0] + parts[1] + (steps,)), gain

    own_acts = lax.dynamic_index_in_dim(acts[:, 0], lane, 0, False)
    before = shifted(own_acts[rows - RIM :], "ctx", 1)
    smalls = both_layers(pack_small)
    packs = both_layers(pack)
    feed_sections, pair_sections = (half, quarter, wide), (half, half)
    along_feed = tp_gather(jnp.concatenate([packs[0][:, :cut], smalls[0]], axis=0))
    pair_pack, along_feed = tied(packs[0][:, cut:], along_feed)
    along_pair = tp_gather(pair_pack)
    feed_parts = gather_item(along_feed[:, :own_rows], feed_sections)
    last_pack, along_feed = tied(packs[1], along_feed)
    along_pair, feed_parts = tied(along_pair, feed_parts)
    small_pad = jnp.pad(smalls[1], ((0, 0), (0, last_pack.shape[1] - cut)))
    along_last = tp_gather(jnp.concatenate([last_pack, small_pad], axis=0))
    pair_parts = gather_item(along_pair, pair_sections)
    feed_first, gain_first = feed_weights(feed_parts)
    weights = [(feed_first, columns(pair_parts[0]), columns(pair_parts[1]))]
    params = [(gain_first,) + layer_params(along_feed[:, own_rows:])]

    places = lax.axis_index("ctx") * rows + jnp.arange(rows, dtype=jnp.int32)
    length = lax.dynamic_index_in_dim(lengths[:, 0], lane, 0, False)
    valid = (places < length).astype(full)[:, None]
    hidden = own_acts.astype(full)
    out_grad = lax.dynamic_index_in_dim(cotangent[:, 0], lane, 0, False)

    result_first, kept_first = layer_forward(hidden, before, valid, weights[0], params[0])
    low_first = result_first.astype(low)
    before = shifted(low_first[rows - RIM :], "ctx", 1)
    last_parts = gather_item(along_last[:, :own_rows, :cut], feed_sections, low_first)
    along_last, last_parts = tied(along_last, last_parts)
    last_parts += gather_item(along_last[:, :own_rows, cut:], pair_sections)
    feed_last, gain_last = feed_weights(last_parts[:3])
    weights.append((feed_last, columns(last_parts[3]), columns(last_parts[4])))
    params.append((gain_last,) + layer_params(along_last[:, own_rows:, :cut]))
    result_last, kept_last = layer_forward(low_first.astype(full), before, valid, weights[1], params[1])
    own_result = jnp.where(first, low_first, result_last.astype(low))
    quarter_rows = rows // tp_count
    section_out = spread_rows(own_result)

    column = core * (width // 2)

    def half_columns(value):
        return lax.dynamic_slice_in_dim(value.astype(low), column, width // 2, 1)

    delta_last, feed_last, small_last, pair_last, section_out = layer_backward(
        out_grad, valid, weights[1], params[1], kept_last, section_out
    )
    spread_last = spread_rows(half_columns(delta_last))
    incoming = (out_grad + delta_last).astype(low).astype(full)
    pair_last.second(incoming)
    last = split_reduction(feed_last)
    last.first(incoming)
    delta_first, feed_first, small_first, pair_first, spread_last = layer_backward(
        incoming, valid, weights[0], params[0], kept_first, spread_last, (pair_last, last)
    )
    grad_first = (incoming + delta_first).astype(low)
    pair_first.second(grad_first)
    feed_first, grad_first = tied(feed_first, grad_first)
    feed = split_reduction(feed_first)
    feed.first()
    pair_first_sum = pair_sum(pair_first.sums)
    small = jnp.stack([small_first, small_last])
    spread_first = spread_rows(half_columns(grad_first))
    small = all_sum(all_sum(small, "ctx"), "dp")
    feed.second()
    feed_sums = feed_sum(feed.sums, inner, small.astype(low).reshape(-1))
    own_cotangent = lax.dynamic_slice_in_dim(
        cotangent[:, 0], lane * quarter_rows, quarter_rows, 1
    )
    spread_keep = jnp.where(first, spread_first, spread_last)
    spread_came = swap_cores(jnp.where(first, spread_last, spread_first))
    spread = columns(
        [jnp.where(first, spread_keep, spread_came), jnp.where(first, spread_came, spread_keep)]
    ).astype(full)
    input_grad = jnp.where(first, spread, own_cotangent + spread)

    pair_keep = jnp.where(first, pair_first_sum, pair_last.sums)
    pair_came = swap_cores(jnp.where(first, pair_last.sums, pair_first_sum))
    size = small_first.shape[0]
    small_sums = feed_sums[own_rows:].reshape(-1)[: 2 * size].reshape(2, size)
    sums_last = last.sums
    total_width = sums_last.shape[1]
    joined = [
        jnp.concatenate([sums, as_rows(vector, total_width)])
        for sums, vector in zip((feed_sums[:own_rows], sums_last), small_sums)
    ]
    keep = jnp.where(first, joined[0], joined[1])
    came = swap_cores(jnp.where(first, joined[1], joined[0]))
    small_keep = keep[own_rows:].reshape(-1)[:size]
    small_came = came[own_rows:].reshape(-1)[:size]
    keep, came = keep[:own_rows], came[:own_rows]

    def halves(kept_part, came_part, axis):
        zero = jnp.where(first, kept_part, came_part)
        one = jnp.where(first, came_part, kept_part)
        return jnp.concatenate([zero, one], axis=axis)

    def own_lane(value, shape, axis):
        return lax.dynamic_index_in_dim(value.reshape(shape), lane, axis, False)

    grad_gate = halves(pair_keep[:, :half], pair_came[:, :half], 1)
    grad_out = halves(pair_keep[:, half:].T, pair_came[:, half:].T, 0)
    at = 0
    grad_x = halves(keep[:, at : at + half], came[:, at : at + half], 1)
    at += half
    grad_state = keep[:, at : at + 2 * STATE] + came[:, at : at + 2 * STATE]
    at += 2 * STATE + lane * step_half
    grad_step = halves(
        lax.dynamic_slice_in_dim(keep, at, step_half, 1), lax.dynamic_slice_in_dim(came, at, step_half, 1), 1
    )
    grad_gate_x = jnp.stack([grad_gate, grad_x], axis=1)

    at = (CONV + 1) * inner
    taps_shape = (CONV + 1, tp_count, half)
    grad_conv_inner = halves(
        own_lane(small_keep[:at], taps_shape, 1), own_lane(small_came[:at], taps_shape, 1), 1
    )
    end = at + (CONV + 1) * 2 * STATE
    grad_conv_state = (small_keep[at:end] + small_came[at:end]).reshape(CONV + 1, 2 * STATE)
    at = end
    vectors = []
    for size in (inner, heads, heads, heads):
        shape = (tp_count, size // tp_count)
        vectors.append(
            halves(
                own_lane(small_keep[at : at + size], shape, 0),
                own_lane(small_came[at : at + size], shape, 0),
                0,
            )
        )
        at += size
    owner = lax.axis_index("dp") * lax.axis_size("ctx") + lax.axis_index("ctx")
    grad_norm_gain = lax.dynamic_slice_in_dim(small_keep[at:], owner * own_rows, own_rows, 0)
    return (
        section_out[None, :, None],
        input_grad[None, :, None],
        grad_norm_gain[None],
        grad_gate_x[None],
        grad_state[None],
        grad_step[None],
        grad_conv_inner[None],
        grad_conv_state[None],
        vectors[1][None],
        vectors[2][None],
        vectors[3][None],
        vectors[0][None],
        grad_out[None],
    )


def solution(mesh):
    placed = (
        P(None, "dp", "ctx", None),
        P(None, "dp", "ctx", None),
        P(None, "dp"),
        P("section", ("dp", "ctx")),
        P("section", ("dp", "ctx"), None, "tp"),
        P("section", ("dp", "ctx"), None),
        P("section", ("dp", "ctx"), "tp"),
        P("section", None, "tp"),
        P("section", None, None),
        P("section", "tp"),
        P("section", "tp"),
        P("section", "tp"),
        P("section", "tp"),
        P("section", "tp", ("dp", "ctx")),
    )
    return jax.shard_map(
        on_device,
        mesh=mesh,
        in_specs=placed,
        out_specs=(
            P("section", None, "dp", ("ctx", "tp"), None),
            P("section", None, "dp", ("ctx", "tp"), None),
            P("section", ("dp", "ctx")),
            P("section", ("dp", "ctx"), None, "tp"),
            P("section", ("dp", "ctx"), None),
            P("section", ("dp", "ctx"), "tp"),
            P("section", None, "tp"),
            P("section", None, None),
            P("section", "tp"),
            P("section", "tp"),
            P("section", "tp"),
            P("section", "tp"),
            P("section", "tp", ("dp", "ctx")),
        ),
        check_vma=False,
    )
```
